32 devices in a mesh: req: 4 (over y, x), seq: 8 (over z, core).
Axes of the slice: x: 2, y: 2, z: 4, core: 2. Of those that a mesh axis runs over, the one named last changes fastest.
Arguments:
- hidden_in: bfloat16 [4, 1024, 1600], P('req', 'seq'), may hold values from -6 to 6
- mamba_in: bfloat16 [4, 1024, 3200], P('req', 'seq'), may hold values from -6 to 6
- conv_weight: float32 [4, 3200], replicated, may hold values from -3 to 3
- conv_bias: float32 [3200], replicated, may hold values from -3 to 3
- x_proj: bfloat16 [3200, 132], replicated, may hold values from -0.109375 to 0.109375
- dt_proj: bfloat16 [100, 3200], replicated, may hold values from -0.625 to 0.625
- dt_bias: float32 [3200], replicated, may hold values from -2 to 0.5
- decay_rate: float32 [3200], replicated, may hold values from 9.765625e-05 to 0.05
- skip_gain: float32 [3200], replicated, may hold values from 0.5 to 1.5
- out_proj: bfloat16 [3200, 1600], replicated, may hold values from -0.109375 to 0.109375
- norm_gain: float32 [1600], replicated, may hold values from 0.3 to 1.7
- mlp_gate: bfloat16 [1600, 5504], P(None, 'req'), may hold values from -0.15625 to 0.15625
- mlp_up: bfloat16 [1600, 5504], P(None, 'req'), may hold values from -0.15625 to 0.15625
- mlp_down: bfloat16 [5504, 1600], P('req'), may hold values from -0.078125 to 0.078125
- cache_state: float32 [4, 8, 16, 3200], P('req', 'seq'), may hold values from -6 to 6
- cache_edge: bfloat16 [4, 8, 3, 3200], P('req', 'seq'), may hold values from -6 to 6
- req_lengths: int32 [4, 4], P('req'), may hold values from 1 to 768, 1024 in all within a row
- cont_flag: int32 [4, 4], P('req'), may hold values from 0 to 1, as said below
- cache_source: int32 [4, 4], P('req'), may hold values from 0 to 7, as said below
- owner_slot: int32 [4, 4], P('req'), may hold values from 0 to 7, as said below
Outputs:
- block_out: bfloat16 [4, 1024, 1600], P('req', 'seq')
- new_state: float32 [4, 8, 16, 3200], P('req', 'seq')
- new_edge: bfloat16 [4, 8, 3, 3200], P('req', 'seq')
The draws below stay inside these ranges and needn't reach their ends.
Inputs may be any that keep to these rules, and one draw needn't show every extreme that they name: `req_lengths`: each row sums to 1024; its largest entry is exactly 768. `owner_slot`: the 4 entries of a row are distinct; slots 0 and 7 each own a request of every group. `cont_flag`: request 0 of every group continues; request 1 of group 0 does not; the others continue with probability one half. `cache_source`: request 0 reads slot 4 in groups 0, 4, 8 ..., slot 7 in groups 1, 5 ..., slot 0 in groups 2, 6 ..., slot 1 in groups 3, 7 ...; other requests read any slot.
All inputs are finite; a program needn't handle non-finite values.
Results may differ from the reference program's by a relative error of at most 0.007.
Values may be sent and summed in bfloat16 or wider, within the bound.
No kernel may reach another device: no remote copies, remote signals or barrier semaphores. Data moves between devices by JAX's collectives and lax.ppermute only.
A program may use at most 256 MiB of HBM per device.

```python
import math
import jax
import jax.numpy as jnp
import numpy as np
from jax import lax

D = 1600
INNER = 3200
STATE = 16
CONV = 4
DT_RANK = 100
FF = 5504
TOK_DEV = 128
REQS = 4
GROUP_TOK = 1024
EDGE = 3
N_REQ = 4
N_SEQ = 8


def draw_owner_slot(key, part):
    slot_count = GROUP_TOK // TOK_DEV
    row_keys = jax.random.split(key, N_REQ)

    def one_row(row_key):
        first_key, second_key = jax.random.split(row_key)
        middle = (jax.random.permutation(first_key, slot_count - 2) + 1).astype(jnp.int32)
        chosen = jnp.concatenate([jnp.array([0, slot_count - 1], dtype=jnp.int32), middle[:REQS - 2]])
        return jax.random.permutation(second_key, chosen).astype(jnp.int32)
    return jax.vmap(one_row)(row_keys).astype(jnp.int32)


def draw_cont_flag(key, part):
    flags = jax.random.randint(jax.random.fold_in(key, 11), (N_REQ, REQS), 0, 2).astype(jnp.int32)
    flags = flags.at[:, 0].set(1)
    flags = flags.at[0, 1].set(0)
    return flags.astype(jnp.int32)


def draw_cache_source(key, part):
    slot_count = GROUP_TOK // TOK_DEV
    sources = jax.random.randint(jax.random.fold_in(key, 23), (N_REQ, REQS), 0, slot_count).astype(jnp.int32)
    group_ids = jnp.arange(N_REQ, dtype=jnp.int32) % 4
    fixed = jnp.where(group_ids == 0, slot_count // 2, jnp.where(group_ids == 1, slot_count - 1, jnp.where(group_ids == 2, 0, 1))).astype(jnp.int32)
    return sources.at[:, 0].set(fixed).astype(jnp.int32)


def shard_levels(stream_key, dims, cuts, low, largest):
    factor_of = 1.0
    for dim, blocks in cuts:
        heights = jax.random.uniform(jax.random.fold_in(jax.random.fold_in(stream_key, 6), dim), (blocks,), jnp.float32, low / len(cuts), largest / len(cuts))
        factor_of = factor_of * jnp.repeat(jnp.exp(heights), dims[dim] // blocks).reshape((-1,) + (1,) * (len(dims) - 1 - dim))
    return factor_of


def split_up(number_of, total, most, skew):
    loads = [(1 << 20) // math.isqrt(standing ** skew) + 1 for standing in range(2, number_of + 1)]
    rest, given = total - most - (number_of - 1), [1] * (number_of - 1)
    while rest > 0:
        movable = [i for i in range(number_of - 1) if given[i] < most]
        mass, left = sum([loads[i] for i in movable]), rest
        for i in movable:
            addition = min(most - given[i], max(1, left * loads[i] // mass), rest)
            given[i] = given[i] + addition
            rest = rest - addition
    return np.array([most] + given)


def uneven_parts(stream_key, amount, total, reach, slope):
    if amount == 2:
        one = jax.random.randint(stream_key, (), max(1, total - reach), min(reach, total - 1) + 1)
        return jnp.stack([one, total - one])
    sizes = jnp.asarray(split_up(amount, total, reach, slope), jnp.int32)
    twos = (amount - 1) // 2
    source_of, receiver = sizes[1:1 + 2 * twos:2], sizes[2:2 + 2 * twos:2]
    margin = jnp.minimum(source_of - 1, reach - receiver)
    moved = jax.random.randint(jax.random.fold_in(stream_key, 1), (twos,), 0, 1 << 20) % (margin + 1)
    sizes = sizes.at[1:1 + 2 * twos:2].set(source_of - moved).at[2:2 + 2 * twos:2].set(receiver + moved)
    return sizes[jax.random.permutation(jax.random.fold_in(stream_key, 2), amount)]


def gaussian(rng, extent, spread, bound, cuts=(), kind=jnp.bfloat16):
    values = jax.random.normal(rng, extent, jnp.float32) * spread
    if len(cuts) > 0:
        values = shard_levels(rng, extent, cuts, -0.22, 0.18) * values
    return jnp.clip(values, min=-bound, max=bound).astype(kind)


def setup_inputs(seed: int = 0) -> dict:
    key_list = jax.random.split(jax.random.key(seed), 21)
    return {
        "hidden_in": gaussian(key_list[0], (N_REQ, GROUP_TOK, D), 1.0, 6.0, ((0, 4), (1, 8))),
        "mamba_in": gaussian(key_list[1], (N_REQ, GROUP_TOK, INNER), 1.0, 6.0, ((0, 4), (1, 8))),
        "conv_weight": gaussian(key_list[2], (CONV, INNER), 0.5, 3.0, (), jnp.float32),
        "conv_bias": gaussian(key_list[3], (INNER,), 0.5, 3.0, (), jnp.float32),
        "x_proj": gaussian(key_list[4], (INNER, DT_RANK + 2 * STATE), INNER ** -0.5, 0.109375),
        "dt_proj": gaussian(key_list[5], (DT_RANK, INNER), DT_RANK ** -0.5, 0.625),
        "dt_bias": jnp.clip(jax.random.uniform(key_list[6], (INNER,), jnp.float32, -2.0, 0.5), -2.0, 0.5),
        "decay_rate": jnp.clip(jnp.exp(jax.random.uniform(key_list[7], (INNER,), jnp.float32, math.log(9.765625145519152e-05), math.log(0.05))), 9.765625145519152e-05, 0.05),
        "skip_gain": jnp.clip(jax.random.uniform(key_list[8], (INNER,), jnp.float32, 0.5, 1.5), 0.5, 1.5),
        "out_proj": gaussian(key_list[9], (INNER, D), INNER ** -0.5, 0.109375),
        "norm_gain": jnp.clip(jax.random.uniform(key_list[10], (D,), jnp.float32, 0.3, 1.7), 0.3, 1.7),
        "mlp_gate": gaussian(key_list[11], (D, FF), D ** -0.5, 0.15625, ((1, 4),)),
        "mlp_up": gaussian(key_list[12], (D, FF), D ** -0.5, 0.15625, ((1, 4),)),
        "mlp_down": gaussian(key_list[13], (FF, D), FF ** -0.5, 0.078125, ((0, 4),)),
        "cache_state": gaussian(key_list[14], (N_REQ, N_SEQ, STATE, INNER), 1.0, 6.0, ((0, 4), (1, 8)), jnp.float32),
        "cache_edge": gaussian(key_list[15], (N_REQ, N_SEQ, EDGE, INNER), 1.0, 6.0, ((0, 4), (1, 8))),
        "req_lengths": jax.vmap(lambda own: uneven_parts(own, REQS, TOK_DEV * N_SEQ, TOK_DEV * N_SEQ * 3 // 4, 2))(jax.random.split(key_list[16], N_REQ)).reshape((N_REQ, REQS)).astype(jnp.int32),
        "cont_flag": draw_cont_flag(jax.random.fold_in(key_list[20], 71), 0),
        "cache_source": draw_cache_source(jax.random.fold_in(key_list[20], 71), 0),
        "owner_slot": draw_owner_slot(jax.random.fold_in(key_list[20], 71), 0),
    }


HIGHEST_PREC = lax.Precision.HIGHEST
NORM_EPS = 1e-06

def request_layout(length_row, first_pos, row_count):
    length_row = length_row.astype(jnp.int32)
    end_marks = jnp.cumsum(length_row).astype(jnp.int32)
    start_marks = (end_marks - length_row).astype(jnp.int32)
    position = (first_pos + jnp.arange(row_count, dtype=jnp.int32)).astype(jnp.int32)
    request_id = lax.optimization_barrier(jnp.sum((position[:, None] >= end_marks[None, :]).astype(jnp.int32), axis=1)).astype(jnp.int32)
    member = jnp.arange(length_row.shape[0], dtype=jnp.int32)[None, :] == request_id[:, None]
    begin = lax.optimization_barrier(jnp.sum(jnp.where(member, start_marks[None, :], 0), axis=1)).astype(jnp.int32)
    finish = lax.optimization_barrier(jnp.sum(jnp.where(member, end_marks[None, :], 0), axis=1)).astype(jnp.int32)
    offset = (position - begin).astype(jnp.int32)
    is_last = position + 1 == finish
    return (member, offset, is_last)

def conv_window(extended, member, offset, edges, continuing):
    row_count = member.shape[0]
    request_count = member.shape[1]
    edge_rows = edges.shape[1]
    active = member.astype(jnp.float32) * continuing.astype(jnp.float32)[None, :]
    flat_edges = edges.reshape(request_count * edge_rows, edges.shape[2])
    window = []
    for lag_back in range(edge_rows, 0, -1):
        near_rows = extended[edge_rows - lag_back:edge_rows - lag_back + row_count].astype(jnp.float32)
        edge_slot = offset - lag_back + edge_rows
        chooser = active[:, :, None] * (jnp.arange(edge_rows, dtype=jnp.int32)[None, None, :] == edge_slot[:, None, None]).astype(jnp.float32)
        far_rows = jnp.dot(chooser.reshape(row_count, request_count * edge_rows), flat_edges, precision=HIGHEST_PREC)
        window.append(jnp.where((offset >= lag_back)[:, None], near_rows, far_rows))
    window.append(extended[edge_rows:].astype(jnp.float32))
    return window

def conv_apply(window, conv_weight, conv_bias):
    result = conv_bias[None, :] + conv_weight[0][None, :] * window[0]
    for tap_index in range(1, len(window)):
        result = result + conv_weight[tap_index][None, :] * window[tap_index]
    return jax.nn.silu(result).astype(jnp.bfloat16)

def selective_terms(mixed_in, x_proj, dt_proj, dt_bias, state_size):
    projected = jnp.dot(mixed_in, x_proj, preferred_element_type=jnp.float32)
    rank_size = dt_proj.shape[0]
    dt_low = projected[:, :rank_size].astype(jnp.bfloat16)
    b_coef = projected[:, rank_size:rank_size + state_size]
    c_coef = projected[:, rank_size + state_size:rank_size + 2 * state_size]
    step_size = jax.nn.softplus(jnp.dot(dt_low, dt_proj, preferred_element_type=jnp.float32) + dt_bias[None, :])
    return (b_coef, c_coef, step_size)

def norm_input(ssm_out, hidden_rows, out_proj, norm_gain):
    middle = hidden_rows.astype(jnp.float32) + jnp.dot(ssm_out, out_proj, preferred_element_type=jnp.float32)
    inverse_rms = lax.rsqrt(lax.optimization_barrier(jnp.mean(middle * middle, axis=1, keepdims=True)) + NORM_EPS)
    normed = (middle * inverse_rms * norm_gain[None, :]).astype(jnp.bfloat16)
    return (middle, normed)

def reference(hidden_in, mamba_in, conv_weight, conv_bias, x_proj, dt_proj, dt_bias, decay_rate, skip_gain, out_proj, norm_gain, mlp_gate, mlp_up, mlp_down, cache_state, cache_edge, req_lengths, cont_flag, cache_source, owner_slot):
    rate_matrix = (jnp.arange(STATE, dtype=jnp.int32) + 1).astype(jnp.float32)[:, None] * decay_rate[None, :]
    outputs = []
    states_out = []
    edges_out = []
    for group in range(N_REQ):
        token_rows = mamba_in[group]
        row_count = token_rows.shape[0]
        inner_size = token_rows.shape[1]
        edge_rows = cache_edge.shape[2]
        member, offset, is_last = request_layout(req_lengths[group], 0, row_count)
        continuing = cont_flag[group]
        keep_flag = continuing.astype(jnp.float32)
        start_state = keep_flag[:, None, None] * cache_state[group][cache_source[group]]
        start_edge = keep_flag[:, None, None] * cache_edge[group][cache_source[group]].astype(jnp.float32)
        extended = jnp.concatenate([jnp.zeros((edge_rows, inner_size), token_rows.dtype), token_rows], axis=0)
        window = conv_window(extended, member, offset, start_edge, continuing)
        mixed_in = conv_apply(window, conv_weight, conv_bias)
        b_coef, c_coef, step_size = selective_terms(mixed_in, x_proj, dt_proj, dt_bias, STATE)
        mixed_f = mixed_in.astype(jnp.float32)
        request_id = lax.optimization_barrier(jnp.sum(member.astype(jnp.int32) * jnp.arange(REQS, dtype=jnp.int32)[None, :], axis=1)).astype(jnp.int32)
        is_first = offset == 0

        def advance(carry, item):
            held, finals = carry
            step_t, b_t, c_t, input_t, first_t, request_t, last_t = item
            decay = jnp.exp(-step_t[None, :] * rate_matrix)
            before = jnp.where(first_t, start_state[request_t], held)
            held = decay * before + step_t[None, :] * b_t[:, None] * input_t[None, :]
            output_t = lax.optimization_barrier(jnp.sum(c_t[:, None] * held, axis=0))
            finals = finals.at[request_t].add(jnp.where(last_t, held, jnp.zeros_like(held)))
            return ((held, finals), output_t)
        carry_init = (jnp.zeros((STATE, inner_size), jnp.float32), jnp.zeros((REQS, STATE, inner_size), jnp.float32))
        (_, finals), ssm_core = lax.scan(advance, carry_init, (step_size, b_coef, c_coef, mixed_f, is_first, request_id, is_last))
        ssm_out = (ssm_core + skip_gain[None, :] * mixed_f).astype(jnp.bfloat16)
        middle, normed = norm_input(ssm_out, hidden_in[group], out_proj, norm_gain)
        gate_v = jnp.dot(normed, mlp_gate, preferred_element_type=jnp.float32)
        up_v = jnp.dot(normed, mlp_up, preferred_element_type=jnp.float32)
        hidden = (jax.nn.silu(gate_v) * up_v).astype(jnp.bfloat16)
        block_rows = (middle + jnp.dot(hidden, mlp_down, preferred_element_type=jnp.float32)).astype(jnp.bfloat16)
        outputs.append(block_rows)
        end_marks = jnp.cumsum(req_lengths[group].astype(jnp.int32)).astype(jnp.int32)
        window_tail = jnp.stack(window[1:], axis=1)
        final_edge = window_tail[end_marks - 1]
        owners = owner_slot[group]
        slot_state = jnp.zeros((N_SEQ, STATE, inner_size), jnp.float32).at[owners].set(finals)
        slot_edge = jnp.zeros((N_SEQ, edge_rows, inner_size), jnp.float32).at[owners].set(final_edge)
        states_out.append(slot_state)
        edges_out.append(slot_edge.astype(jnp.bfloat16))
    return (jnp.stack(outputs, axis=0), jnp.stack(states_out, axis=0), jnp.stack(edges_out, axis=0))
```

```python
import functools

import jax
import jax.numpy as jnp
from jax import lax
from jax.experimental import pallas as pl
from jax.experimental.pallas import tpu as pltpu
from jax.sharding import PartitionSpec as P

STATE = 16
NORM_EPS = 1e-06
LANE = 128
FAR = 1e30
F32 = jnp.float32
BF16 = jnp.bfloat16
VMEM_BYTES = 48 * 1024 * 1024


def request_marks(lens_ref, first_pos):
    marks = []
    begin = -first_pos
    for r in range(lens_ref.shape[1]):
        end = begin + lens_ref[0, r]
        marks.append((begin, end))
        begin = end
    return marks


def segment_of(index, marks):
    total = jnp.zeros(index.shape, jnp.int32)
    for begin, _ in marks:
        total = total + (index >= begin).astype(jnp.int32)
    return total


def segment_masks(row_count, marks):
    row = lax.broadcasted_iota(jnp.int32, (row_count, row_count), 0)
    col = lax.broadcasted_iota(jnp.int32, (row_count, row_count), 1)
    same = segment_of(row, marks) == segment_of(col, marks)
    return row, col, same


def three_parts(values):
    high = values.astype(BF16)
    rest = values - high.astype(F32)
    middle = rest.astype(BF16)
    low = (rest - middle.astype(F32)).astype(BF16)
    return jnp.concatenate([high, middle, low], axis=0)


def tripled(mask):
    one = mask.astype(F32).astype(BF16)
    return jnp.concatenate([one, one, one], axis=1)


def rate_block(rate_row):
    power = lax.broadcasted_iota(jnp.int32, (STATE, rate_row.shape[1]), 0) + 1
    return power.astype(F32) * rate_row


def softplus(v):
    return jnp.maximum(v, 0.0) + jnp.log1p(jnp.exp(-jnp.abs(v)))


def sum_layout(tiles):
    groups = -(-tiles // STATE)
    return groups, 2 * groups * LANE


def read_sum(ext_ref, tile, inner):
    groups, _ = sum_layout(inner // LANE)
    group, row = divmod(tile, STATE)
    high = inner + group * LANE
    low = high + groups * LANE
    return ext_ref[row : row + 1, high : high + LANE].astype(F32) + ext_ref[
        row : row + 1, low : low + LANE
    ].astype(F32)


def write_sums(ext_ref, sums, inner):
    groups, _ = sum_layout(inner // LANE)
    for group in range(groups):
        part = sums[group * STATE : (group + 1) * STATE, :]
        high = part.astype(BF16)
        low = (part - high.astype(F32)).astype(BF16)
        at = inner + group * LANE
        ext_ref[:, at : at + LANE] = high
        ext_ref[:, at + groups * LANE : at + (groups + 1) * LANE] = low


def terms_kernel(edge_count, *refs):
    lens_ref, cont_ref, source_ref, owner_ref, x_ref, tail_ref = refs[:6]
    edge_refs = refs[6 : 6 + edge_count]
    (taps_ref, vecs_ref, x_proj_ref, dt_proj_ref) = refs[6 + edge_count : 10 + edge_count]
    (mixed_ref, step_ref, proj_ref, ext_ref, slot_edge_ref) = refs[
        10 + edge_count : 15 + edge_count
    ]
    rows_s, conv_s, edge_s, b_s, sums_s = refs[15 + edge_count :]
    row_count, inner = x_ref.shape
    request_count = lens_ref.shape[1]
    lags = tail_ref.shape[0]
    me = lax.axis_index("seq")
    peers = lax.axis_size("seq")
    marks = request_marks(lens_ref, me * row_count)
    row = lax.broadcasted_iota(jnp.int32, (row_count, 1), 0)
    near = []
    for lag in range(1, lags + 1):
        hit = jnp.zeros((row_count, 1), jnp.int32)
        for begin, _ in marks:
            hit = hit + jnp.logical_and(row >= begin, row < begin + lag).astype(jnp.int32)
        near.append((hit == 0).astype(F32))
    width = 5 * LANE
    rows_s[0:8, :] = jnp.zeros((8, inner), F32)
    rows_s[8 - lags : 8, :] = tail_ref[...].astype(F32)
    for at in range(0, inner, width):
        cols = slice(at, at + width)
        here = x_ref[:, cols].astype(F32)
        rows_s[8 : 8 + row_count, cols] = here
        total = vecs_ref[0:1, cols] + taps_ref[lags : lags + 1, cols] * here
        for lag in range(1, lags + 1):
            back = rows_s[8 - lag : 8 - lag + row_count, cols]
            total = total + taps_ref[lags - lag : lags - lag + 1, cols] * (near[lag - 1] * back)
        conv_s[:, cols] = total
    slot_edge_ref[...] = jnp.zeros(slot_edge_ref.shape, F32)
    for r in range(request_count):
        begin, end = marks[r]
        length = lens_ref[0, r]

        @pl.when(jnp.logical_and(begin > -lags, begin < row_count))
        def _(r=r, begin=begin, end=end, length=length):
            keep = cont_ref[0, r].astype(F32)
            for k in range(edge_count):
                slot = lax.rem(me - k + peers, peers)

                @pl.when(slot == source_ref[0, r])
                def _():
                    edge_s[0:lags, :] = keep * edge_refs[k][...].astype(F32)

            for p in range(lags):
                at = begin + p

                @pl.when(jnp.logical_and(jnp.logical_and(at >= 0, at < row_count), p < length))
                def _():
                    extra = jnp.zeros((1, inner), F32)
                    for lag in range(p + 1, lags + 1):
                        extra = extra + taps_ref[lags - lag : lags - lag + 1, :] * edge_s[
                            lags + p - lag : lags + p - lag + 1, :
                        ]
                    conv_s[pl.ds(at, 1), :] = conv_s[pl.ds(at, 1), :] + extra

        @pl.when(jnp.logical_and(end > 0, end <= row_count))
        def _(r=r, end=end, length=length):
            owner = owner_ref[0, r]
            for lag in range(lags):
                @pl.when(length > lag)
                def _():
                    slot_edge_ref[owner, lags - 1 - lag : lags - lag, :] = rows_s[
                        pl.ds(end + 7 - lag, 1), :
                    ]

                @pl.when(length <= lag)
                def _():
                    slot_edge_ref[owner, lags - 1 - lag : lags - lag, :] = edge_s[
                        pl.ds(lags + length - 1 - lag, 1), :
                    ]

    for at in range(0, inner, width):
        cols = slice(at, at + width)
        v = conv_s[:, cols]
        mixed_ref[:, cols] = (v / (1.0 + jnp.exp(-v))).astype(BF16)
    projected = jnp.dot(mixed_ref[...], x_proj_ref[...], preferred_element_type=F32)
    proj_ref[...] = projected
    rank = dt_proj_ref.shape[0]
    dt_low = projected[:, :rank].astype(BF16)
    last_begin = jnp.int32(0)
    for begin, _ in marks:
        last_begin = jnp.where(
            jnp.logical_and(begin >= 0, begin < row_count), jnp.maximum(last_begin, begin), last_begin
        )
    in_last = (row >= last_begin).astype(F32)
    for s in range(STATE):
        b_s[s] = jnp.broadcast_to(
            projected[:, rank + s : rank + s + 1] * in_last, (row_count, LANE)
        )
    m_row, m_col, same = segment_masks(row_count, marks)
    later = tripled(jnp.logical_and(m_col > m_row, same))

    def tile_step(i, carry):
        at = pl.multiple_of(i * LANE, LANE)
        cols = pl.ds(at, LANE)
        step = softplus(
            jnp.dot(dt_low, dt_proj_ref[:, cols], preferred_element_type=F32) + vecs_ref[1:2, cols]
        )
        step_ref[:, cols] = step
        suffix = jnp.dot(later, three_parts(step), preferred_element_type=F32)
        decay = jnp.exp(-vecs_ref[2:3, cols] * suffix)
        weight = step * mixed_ref[:, cols].astype(F32) * decay
        out_rows = []
        for s in range(STATE):
            product = weight * b_s[s]
            total = product[0:8, :]
            for k in range(8, row_count, 8):
                total = total + product[k : k + 8, :]
            out_rows.append(jnp.sum(total, axis=0, keepdims=True))
            if s + 1 < STATE:
                weight = weight * decay
        ext_ref[:, cols] = jnp.concatenate(out_rows, axis=0).astype(BF16)
        sums_s[pl.ds(i, 1), :] = jnp.sum(step * in_last, axis=0, keepdims=True)
        return carry

    sums_s[...] = jnp.zeros(sums_s.shape, F32)
    lax.fori_loop(0, inner // LANE, tile_step, 0)
    write_sums(ext_ref, sums_s[...], inner)


def pair_kernel(tokens, lens_ref, vecs_ref, mine_ref, other_ref, out_ref):
    inner = vecs_ref.shape[1]
    me = lax.axis_index("seq")
    row_count = tokens
    core = lax.rem(me, 2)
    second = me - core + 1
    marks = request_marks(lens_ref, second * row_count)
    whole = jnp.float32(1.0)
    for begin, _ in marks:
        whole = jnp.where(jnp.logical_and(begin >= 0, begin < row_count), 0.0, whole)
    sums = []
    for i in range(inner // LANE):
        cols = slice(i * LANE, (i + 1) * LANE)
        mine, other = mine_ref[:, cols].astype(F32), other_ref[:, cols].astype(F32)
        e0 = jnp.where(core == 0, mine, other)
        e1 = jnp.where(core == 0, other, mine)
        my_sum, other_sum = read_sum(mine_ref, i, inner), read_sum(other_ref, i, inner)
        s0 = jnp.where(core == 0, my_sum, other_sum)
        s1 = jnp.where(core == 0, other_sum, my_sum)
        rate = rate_block(vecs_ref[2:3, cols])
        out_ref[:, cols] = (e1 + whole * jnp.exp(-rate * s1) * e0).astype(BF16)
        sums.append(s1 + whole * s0)
    groups, _ = sum_layout(inner // LANE)
    sums.append(jnp.zeros((groups * STATE - len(sums), LANE), F32))
    write_sums(out_ref, jnp.concatenate(sums, axis=0), inner)


def scan_kernel(lens_ref, vecs_ref, mixed_ref, step_ref, proj_ref, y_ref, q_ref, b_s, c_s):
    row_count, inner = mixed_ref.shape
    me = lax.axis_index("seq")
    marks = request_marks(lens_ref, me * row_count)
    row = lax.broadcasted_iota(jnp.int32, (row_count, 1), 0)
    is_start = jnp.zeros((row_count, 1), jnp.int32)
    for begin, _ in marks:
        is_start = is_start + (row == begin).astype(jnp.int32)
    reset = is_start.astype(F32) * FAR
    m_row, m_col, same = segment_masks(row_count, marks)
    earlier = tripled(jnp.logical_and(m_col <= m_row, same))
    rank = proj_ref.shape[1] - 2 * STATE
    coefs = proj_ref[:, rank : rank + 2 * STATE]
    coefs = jnp.concatenate([coefs, jnp.zeros((row_count, LANE - 2 * STATE), F32)], axis=1)
    flipped = jnp.transpose(coefs)
    for t in range(row_count):
        b_s[t] = jnp.broadcast_to(flipped[0:STATE, t : t + 1], (STATE, LANE))
        c_s[t] = jnp.broadcast_to(flipped[STATE : 2 * STATE, t : t + 1], (STATE, LANE))
    tiles = 5
    width = tiles * LANE

    def chunk_step(i, carry):
        at = pl.multiple_of(i * width, LANE)
        cols = pl.ds(at, width)
        step = step_ref[:, cols]
        prefix = jnp.dot(earlier, three_parts(step), preferred_element_type=F32)
        q_ref[:, cols] = jnp.exp(-vecs_ref[2:3, cols] * prefix)
        rates = [
            -rate_block(vecs_ref[2:3, pl.ds(pl.multiple_of(at + k * LANE, LANE), LANE)])
            for k in range(tiles)
        ]

        def row_step(j, held):
            first = pl.multiple_of(j * 8, 8)
            rows = pl.ds(first, 8)
            held = list(held)
            starts = (lax.broadcasted_iota(jnp.int32, (8, 1), 0) + first)
            jump = jnp.zeros((8, 1), F32)
            for begin, _ in marks:
                jump = jump + (starts == begin).astype(F32) * FAR
            for k in range(tiles):
                lanes = pl.ds(pl.multiple_of(at + k * LANE, LANE), LANE)
                step8 = step_ref[rows, lanes]
                mixed8 = mixed_ref[rows, lanes].astype(F32)
                push8 = step8 * mixed8
                step8 = step8 + jump
                h = held[k]
                outs = []
                for t in range(8):
                    decay = jnp.exp(rates[k] * step8[t : t + 1, :])
                    h = decay * h + b_s[first + t] * push8[t : t + 1, :]
                    product = c_s[first + t] * h
                    outs.append(jnp.sum(product[0:8] + product[8:16], axis=0, keepdims=True))
                held[k] = h
                y_ref[rows, lanes] = jnp.concatenate(outs, axis=0) + vecs_ref[3:4, lanes] * mixed8
            return tuple(held)

        lax.fori_loop(
            0, row_count // 8, row_step, tuple(jnp.zeros((STATE, LANE), F32) for _ in range(tiles))
        )
        return carry

    lax.fori_loop(0, inner // width, chunk_step, 0)


def close_kernel(stage_count, *refs):
    lens_ref, cont_ref, source_ref = refs[:3]
    stage_refs = refs[3 : 3 + stage_count]
    (pair_ref, seeds_ref, vecs_ref, proj_ref, y_ref, q_ref, hidden_ref, gain_ref, weight_hbm) = refs[
        3 + stage_count : 12 + stage_count
    ]
    middle_ref, normed_ref, begins_ref = refs[12 + stage_count : 15 + stage_count]
    c_s, ssm_s, weight_s, sems = refs[15 + stage_count :]
    row_count, inner = y_ref.shape
    parts = 5
    depth = inner // parts
    copies = [
        pltpu.make_async_copy(
            weight_hbm.at[pl.ds(k * depth, depth)], weight_s.at[pl.ds(k * depth, depth)], sems.at[k]
        )
        for k in range(parts)
    ]
    for copy in copies:
        copy.start()
    me = lax.axis_index("seq")
    core = lax.rem(me, 2)
    marks = request_marks(lens_ref, me * row_count)
    rank = proj_ref.shape[1] - 2 * STATE
    for s in range(STATE):
        c_s[s] = jnp.broadcast_to(
            proj_ref[:, rank + STATE + s : rank + STATE + s + 1], (row_count, LANE)
        )
    ssm_s[...] = y_ref[...]
    tiles = 5
    width = tiles * LANE
    block = 16
    for r in range(lens_ref.shape[1]):
        begin, end = marks[r]
        low, high = jnp.maximum(begin, 0), jnp.minimum(end, row_count)

        @pl.when(high > low)
        def _(r=r, begin=begin, low=low, high=high):
            keep = cont_ref[0, r].astype(F32)
            slot = source_ref[0, r]
            for i in range(inner // LANE):
                cols = slice(i * LANE, (i + 1) * LANE)
                begins_ref[r, :, cols] = keep * seeds_ref[slot, :, cols].astype(F32)
            for k in range(stage_count + 1):
                if k < stage_count:
                    chip_first = me - core - 2 * (stage_count - k)
                    ref = stage_refs[stage_count - 1 - k]
                    stage_end = -(core + 2 * (stage_count - 1 - k)) * row_count
                    valid = jnp.logical_and(chip_first >= 0, begin < stage_end)
                else:
                    ref = pair_ref
                    valid = jnp.logical_and(core == 1, begin < 0)

                @pl.when(valid)
                def _(ref=ref):
                    for i in range(inner // LANE):
                        cols = slice(i * LANE, (i + 1) * LANE)
                        decay = jnp.exp(-rate_block(vecs_ref[2:3, cols]) * read_sum(ref, i, inner))
                        begins_ref[r, :, cols] = (
                            ref[:, cols].astype(F32) + decay * begins_ref[r, :, cols]
                        )

            def block_step(j, carry):
                first = pl.multiple_of(j * block, block)
                rows = pl.ds(first, block)
                at_row = lax.broadcasted_iota(jnp.int32, (block, 1), 0) + first
                inside = jnp.logical_and(at_row >= low, at_row < high)

                def lane_step(i, inner_carry):
                    at = pl.multiple_of(i * width, LANE)
                    cols = pl.ds(at, width)
                    q = q_ref[rows, cols]
                    total = jnp.zeros((block, width), F32)
                    for s in range(STATE - 1, -1, -1):
                        c = c_s[s, rows, :]
                        c = jnp.concatenate([c] * tiles, axis=1)
                        total = (total + c * begins_ref[r, s : s + 1, cols]) * q
                    ssm_s[rows, cols] = ssm_s[rows, cols] + jnp.where(inside, total, 0.0)
                    return inner_carry

                lax.fori_loop(0, inner // width, lane_step, 0)
                return carry

            lax.fori_loop(low // block, (high + block - 1) // block, block_step, 0)

    total = hidden_ref[...].astype(F32)
    for k in range(parts):
        copies[k].wait()
        total = total + jnp.dot(
            ssm_s[:, k * depth : (k + 1) * depth].astype(BF16),
            weight_s[k * depth : (k + 1) * depth, :],
            preferred_element_type=F32,
        )
    middle_ref[...] = total
    scale = lax.rsqrt(jnp.mean(total * total, axis=1, keepdims=True) + NORM_EPS)
    normed_ref[...] = (total * scale * gain_ref[...]).astype(BF16)


def final_kernel(
    lens_ref, owner_ref, vecs_ref, mixed_ref, step_ref, proj_ref, q_ref, begins_ref, slot_edge_ref,
    out_ref, b_s, edge_s,
):
    row_count, inner = mixed_ref.shape
    me = lax.axis_index("seq")
    marks = request_marks(lens_ref, me * row_count)
    rank = proj_ref.shape[1] - 2 * STATE
    lags = slot_edge_ref.shape[1]
    m_row, m_col, same = segment_masks(row_count, marks)
    later = tripled(jnp.logical_and(m_col > m_row, same))
    row = lax.broadcasted_iota(jnp.int32, (row_count, 1), 0)
    out_ref[...] = jnp.zeros(out_ref.shape, BF16)
    tiles = inner // LANE
    edge_groups = (out_ref.shape[2] - inner) // LANE
    for r in range(lens_ref.shape[1]):
        begin, end = marks[r]

        @pl.when(jnp.logical_and(end > 0, end <= row_count))
        def _(r=r, begin=begin, end=end):
            owner = owner_ref[0, r]
            inside = jnp.logical_and(row >= begin, row < end).astype(F32)
            for s in range(STATE):
                b_s[s] = jnp.broadcast_to(
                    proj_ref[:, rank + s : rank + s + 1] * inside, (row_count, LANE)
                )

            def tile_step(i, carry):
                at = pl.multiple_of(i * LANE, LANE)
                cols = pl.ds(at, LANE)
                step = step_ref[:, cols]
                suffix = jnp.dot(later, three_parts(step), preferred_element_type=F32)
                decay = jnp.exp(-vecs_ref[2:3, cols] * suffix)
                weight = step * mixed_ref[:, cols].astype(F32) * decay
                out_rows = []
                for s in range(STATE):
                    product = weight * b_s[s]
                    total = product[0:8, :]
                    for k in range(8, row_count, 8):
                        total = total + product[k : k + 8, :]
                    out_rows.append(jnp.sum(total, axis=0, keepdims=True))
                    if s + 1 < STATE:
                        weight = weight * decay
                held = jnp.concatenate(out_rows, axis=0)
                span = jnp.sum(step * inside, axis=0, keepdims=True)
                carried = jnp.exp(-rate_block(vecs_ref[2:3, cols]) * span) * begins_ref[r, :, cols]
                out_ref[owner, :, cols] = (held + carried).astype(BF16)
                return carry

            lax.fori_loop(0, tiles, tile_step, 0)
            edge_s[...] = jnp.zeros(edge_s.shape, F32)
            for lag in range(lags):
                for i in range(tiles):
                    at = lag * tiles + i
                    edge_s[at : at + 1, :] = slot_edge_ref[
                        owner, lag : lag + 1, i * LANE : (i + 1) * LANE
                    ]
            for g in range(edge_groups):
                out_ref[owner, :, inner + g * LANE : inner + (g + 1) * LANE] = edge_s[
                    g * STATE : (g + 1) * STATE, :
                ].astype(BF16)


def unpack_kernel(lags, got_ref, state_ref, edge_ref, edge_s):
    inner = state_ref.shape[1]
    tiles = inner // LANE
    state_ref[...] = got_ref[:, :inner].astype(F32)
    groups = (got_ref.shape[1] - inner) // LANE
    for g in range(groups):
        edge_s[g * STATE : (g + 1) * STATE, :] = got_ref[
            :, inner + g * LANE : inner + (g + 1) * LANE
        ].astype(F32)
    for i in range(tiles):
        edge_ref[:, i * LANE : (i + 1) * LANE] = jnp.concatenate(
            [edge_s[lag * tiles + i : lag * tiles + i + 1, :] for lag in range(lags)], axis=0
        ).astype(BF16)


def call(kernel, outs, scratch, operands, smem, hbm=(), flops=0, bytes_accessed=0):
    in_specs = []
    for k in range(len(operands)):
        if k < smem:
            in_specs.append(pl.BlockSpec(memory_space=pltpu.SMEM))
        elif k in hbm:
            in_specs.append(pl.BlockSpec(memory_space=pl.ANY))
        else:
            in_specs.append(pl.BlockSpec(memory_space=pltpu.VMEM))
    return pl.pallas_call(
        kernel,
        out_shape=tuple(jax.ShapeDtypeStruct(shape, dtype) for shape, dtype in outs),
        in_specs=in_specs,
        out_specs=tuple(pl.BlockSpec(memory_space=pltpu.VMEM) for _ in outs),
        scratch_shapes=scratch,
        compiler_params=pltpu.CompilerParams(vmem_limit_bytes=VMEM_BYTES),
        cost_estimate=pl.CostEstimate(
            flops=flops, bytes_accessed=bytes_accessed, transcendentals=0
        ),
    )(*operands)


def shifted(block, axis, distance):
    size = lax.axis_size(axis)
    return lax.ppermute(block, axis, [(i, (i + distance) % size) for i in range(size)])


def passed_up(block, axis, distance):
    size = lax.axis_size(axis)
    return lax.ppermute(block, axis, [(i, i + distance) for i in range(size - distance)])


def swapped(block, axis, mask):
    return lax.ppermute(block, axis, [(i, i ^ mask) for i in range(lax.axis_size(axis))])


def shards(
    hidden_in,
    mamba_in,
    conv_weight,
    conv_bias,
    x_proj,
    dt_proj,
    dt_bias,
    decay_rate,
    skip_gain,
    out_proj,
    norm_gain,
    mlp_gate,
    mlp_up,
    mlp_down,
    cache_state,
    cache_edge,
    req_lengths,
    cont_flag,
    cache_source,
    owner_slot,
):
    x = mamba_in[0]
    row_count, inner = x.shape
    width = hidden_in.shape[2]
    lags = cache_edge.shape[2]
    peers = lax.axis_size("seq")
    tiles = inner // LANE
    scalars = (req_lengths, cont_flag, cache_source, owner_slot)
    tail = passed_up(x[row_count - lags :], "seq", 1)
    own_edge = cache_edge[0, 0]
    edges = [own_edge] + [shifted(own_edge, "seq", k) for k in range(1, peers)]
    seeds = lax.all_gather(cache_state[0, 0], "seq")
    vecs = jnp.stack([conv_bias, dt_bias, decay_rate, skip_gain], axis=0)
    groups, extra = sum_layout(tiles)
    ext_shape = (STATE, inner + extra)
    mixed, step, proj, ext, slot_edge = call(
        functools.partial(terms_kernel, len(edges)),
        [
            ((row_count, inner), BF16),
            ((row_count, inner), F32),
            ((row_count, x_proj.shape[1]), F32),
            (ext_shape, BF16),
            ((peers, lags, inner), F32),
        ],
        [
            pltpu.VMEM((8 + row_count, inner), F32),
            pltpu.VMEM((row_count, inner), F32),
            pltpu.VMEM((8, inner), F32),
            pltpu.VMEM((STATE, row_count, LANE), F32),
            pltpu.VMEM((groups * STATE, LANE), F32),
        ],
        (*scalars, x, tail, *edges, conv_weight, vecs, x_proj, dt_proj),
        4,
    )
    other = swapped(ext, "seq", 1)
    (chip,) = call(functools.partial(pair_kernel, row_count), [(ext_shape, BF16)], [], (req_lengths, vecs, ext, other), 1)
    stages = [passed_up(chip, "seq", 2 * k) for k in range(1, peers // 2)]
    y, q = call(
        scan_kernel,
        [((row_count, inner), F32), ((row_count, inner), F32)],
        [pltpu.VMEM((row_count, STATE, LANE), F32), pltpu.VMEM((row_count, STATE, LANE), F32)],
        (req_lengths, vecs, mixed, step, proj),
        1,
        flops=6_000_000_000,
        bytes_accessed=16_000_000,
    )
    middle, normed, begins = call(
        functools.partial(close_kernel, len(stages)),
        [
            ((row_count, width), F32),
            ((row_count, width), BF16),
            ((req_lengths.shape[1], STATE, inner), F32),
        ],
        [
            pltpu.VMEM((STATE, row_count, LANE), F32),
            pltpu.VMEM((row_count, inner), F32),
            pltpu.VMEM(out_proj.shape, BF16),
            pltpu.SemaphoreType.DMA((5,)),
        ],
        (
            *scalars[:3], *stages, other, seeds, vecs, proj, y, q, hidden_in[0],
            norm_gain.reshape(1, width), out_proj,
        ),
        3,
        hbm=(3 + len(stages) + 8,),
    )
    edge_groups = -(-lags * tiles // STATE)
    (finals,) = call(
        final_kernel,
        [((peers, STATE, inner + edge_groups * LANE), BF16)],
        [
            pltpu.VMEM((STATE, row_count, LANE), F32),
            pltpu.VMEM((edge_groups * STATE, LANE), F32),
        ],
        (req_lengths, owner_slot, vecs, mixed, step, proj, q, begins, slot_edge),
        2,
    )

    def mlp(tokens):
        gate_v = jnp.dot(tokens, mlp_gate, preferred_element_type=F32)
        up_v = jnp.dot(tokens, mlp_up, preferred_element_type=F32)
        hidden = (jax.nn.silu(gate_v) * up_v).astype(BF16)
        return jnp.dot(hidden, mlp_down, preferred_element_type=F32)

    masks = range(1, lax.axis_size("req"))
    there = [swapped(normed, "req", m) for m in masks]
    total = middle + mlp(normed)
    back = [swapped(mlp(tokens).astype(BF16), "req", m) for tokens, m in zip(there, masks)]
    for part in back:
        total = total + part.astype(F32)
    block_rows = total.astype(BF16)
    own = lax.psum_scatter(finals, "seq", scatter_dimension=0, tiled=True)
    new_state, new_edge = call(
        functools.partial(unpack_kernel, lags),
        [((STATE, inner), F32), ((lags, inner), BF16)],
        [pltpu.VMEM((edge_groups * STATE, LANE), F32)],
        (own[0],),
        0,
    )
    return (block_rows[None], new_state[None, None], new_edge[None, None])


def solution(mesh):
    return jax.shard_map(
        shards,
        mesh=mesh,
        in_specs=(
            P("req", "seq", None),
            P("req", "seq", None),
            P(),
            P(),
            P(),
            P(),
            P(),
            P(),
            P(),
            P(),
            P(),
            P(None, "req"),
            P(None, "req"),
            P("req", None),
            P("req", "seq", None, None),
            P("req", "seq", None, None),
            P("req", None),
            P("req", None),
            P("req", None),
            P("req", None),
        ),
        out_specs=(P("req", "seq", None), P("req", "seq", None, None), P("req", "seq", None, None)),
        check_vma=False,
    )
```

```python
import functools

import jax
import jax.numpy as jnp
from jax import lax
from jax.experimental import pallas as pl
from jax.experimental.pallas import tpu as pltpu
from jax.sharding import PartitionSpec as P

STATE = 16
NORM_EPS = 1e-06
LANE = 128
FAR = 1e30
OFFER = 24
LOG2E = 1.4426950408889634
F32 = jnp.float32
BF16 = jnp.bfloat16


def request_marks(lens_ref, first_pos):
    marks = []
    begin = -first_pos
    for r in range(lens_ref.shape[1]):
        end = begin + lens_ref[0, r]
        marks.append((begin, end))
        begin = end
    return marks


def segment_of(index, marks):
    total = jnp.zeros(index.shape, jnp.int32)
    for begin, _ in marks:
        total = total + (index >= begin).astype(jnp.int32)
    return total


def segment_masks(row_count, marks):
    row = lax.broadcasted_iota(jnp.int32, (row_count, row_count), 0)
    col = lax.broadcasted_iota(jnp.int32, (row_count, row_count), 1)
    same = segment_of(row, marks) == segment_of(col, marks)
    return row, col, same


def three_parts(values):
    high = values.astype(BF16)
    rest = values - high.astype(F32)
    middle = rest.astype(BF16)
    low = (rest - middle.astype(F32)).astype(BF16)
    return jnp.concatenate([high, middle, low], axis=0)


def tripled(mask):
    one = mask.astype(F32).astype(BF16)
    return jnp.concatenate([one, one, one], axis=1)


def rate_block(rate_row):
    power = lax.broadcasted_iota(jnp.int32, (STATE, rate_row.shape[1]), 0) + 1
    return power.astype(F32) * rate_row


def row_of(vec_ref, tile):
    return vec_ref[pl.ds(tile, 1), :]


def wide_row(vec_ref, first, count):
    return jnp.concatenate([vec_ref[first + k : first + k + 1, :] for k in range(count)], axis=1)


def sums_of_eight(parts):
    sub = lax.broadcasted_iota(jnp.int32, parts[0].shape, 0)
    stride = 1
    while len(parts) > 1:
        first = jnp.bitwise_and(sub, stride) == 0
        parts = [
            jnp.where(first, a, b) + pltpu.roll(jnp.where(first, b, a), stride, 0)
            for a, b in zip(parts[0::2], parts[1::2])
        ]
        stride = 2 * stride
    return parts[0]


def softplus(v):
    return jnp.maximum(v, 0.0) + jnp.log1p(jnp.exp(-jnp.abs(v)))


def sum_layout(tiles):
    groups = -(-tiles // STATE)
    return groups, 2 * groups * LANE


def read_sum(ext_ref, tile, inner):
    groups, _ = sum_layout(inner // LANE)
    group, row = divmod(tile, STATE)
    high = inner + group * LANE
    low = high + groups * LANE
    return ext_ref[row : row + 1, high : high + LANE].astype(F32) + ext_ref[
        row : row + 1, low : low + LANE
    ].astype(F32)


def write_sums(ext_ref, sums, inner):
    groups, _ = sum_layout(inner // LANE)
    for group in range(groups):
        part = sums[group * STATE : (group + 1) * STATE, :]
        high = part.astype(BF16)
        low = (part - high.astype(F32)).astype(BF16)
        at = inner + group * LANE
        ext_ref[:, at : at + LANE] = high
        ext_ref[:, at + groups * LANE : at + (groups + 1) * LANE] = low


NT = (((1,), (1,)), ((), ()))
SIDE = 5 * LANE


def start_all(pairs, sems):
    copies = [pltpu.make_async_copy(src, dst, sems.at[k]) for k, (src, dst) in enumerate(pairs)]
    for copy in copies:
        copy.start()
    return copies


def lane_blocks(size, width):
    return [slice(at, min(at + width, size)) for at in range(0, size, width)]


def offer_kernel(state_hbm, edge_hbm, x_hbm, out_ref, state_s, edge_s, tail_s, sems):
    rows = tail_s.shape[0]
    last = x_hbm.at[pl.ds(x_hbm.shape[0] - rows, rows)]
    for copy in start_all([(state_hbm, state_s), (edge_hbm, edge_s), (last, tail_s)], sems):
        copy.wait()
    lags = edge_s.shape[0]
    tail = tail_s[...].astype(F32)[rows - lags :]
    spare = jnp.zeros((OFFER - STATE - 2 * lags, tail.shape[1]), F32)
    whole = jnp.concatenate([state_s[...], edge_s[...].astype(F32), tail, spare], axis=0)
    out_ref[...] = whole.astype(BF16)


def edges_kernel(*refs):
    for k, ref in enumerate(refs[:-1]):
        refs[-1][k] = ref[...].astype(F32)[STATE:].astype(BF16)


def terms_kernel(lags, seed_count, *refs):
    scalar_hbm = refs[:4]
    x_hbm, taps_hbm, x_proj_hbm, dt_proj_hbm, out_proj_hbm = refs[4:9]
    vec_hbm = refs[9:12]
    edge_mine_ref, edge_other_ref = refs[12:14]
    seed_refs = refs[14 : 14 + seed_count]
    refs = refs[14 + seed_count :]
    (
        mixed_ref, step_ref, push_ref, decay_ref, proj_ref, slot_edge_ref, weight_ref, bundle_ref
    ) = refs[:8]
    scalars = refs[8:12]
    ext_ref = bundle_ref.at[0]
    (x_s, taps_ref, x_proj_ref, dt_proj_ref, bias_s, dt_bias_s, rate_s, rows_s, conv_s, edge_s, b_s,
     sums_s, sems) = refs[12:]
    lens_ref, cont_ref, source_ref, owner_ref = scalars
    row_count, inner = x_s.shape
    request_count = lens_ref.shape[1]
    chips = edge_mine_ref.shape[0]
    blocks = lane_blocks(inner, SIDE)
    side = SIDE // LANE
    pairs = list(zip(scalar_hbm, scalars))
    pairs += [(taps_hbm, taps_ref)]
    pairs += list(zip(vec_hbm, (bias_s, dt_bias_s, rate_s)))
    pairs += [(x_hbm.at[:, cols], x_s.at[:, cols]) for cols in blocks]
    pairs += [(x_proj_hbm, x_proj_ref), (dt_proj_hbm, dt_proj_ref), (out_proj_hbm, weight_ref)]
    copies = start_all(pairs, sems)
    for copy in copies[:8]:
        copy.wait()
    me = lax.axis_index("seq")
    core = lax.rem(me, 2)
    marks = request_marks(lens_ref, me * row_count)
    row = lax.broadcasted_iota(jnp.int32, (row_count, 1), 0)
    near = []
    for lag in range(1, lags + 1):
        hit = jnp.zeros((row_count, 1), jnp.int32)
        for begin, _ in marks:
            hit = hit + jnp.logical_and(row >= begin, row < begin + lag).astype(jnp.int32)
        near.append((hit == 0).astype(F32))
    rows_s[0:8, :] = jnp.zeros((8, inner), F32)
    before = edge_other_ref[1 - core].astype(F32)
    rows_s[8 - lags : 8, :] = before[lags : 2 * lags, :]
    for k, ref in enumerate(seed_refs):
        bundle_ref[1 + k, :, 0:inner] = ref[...].astype(F32)[:STATE].astype(BF16)
    for k, cols in enumerate(blocks):
        copies[8 + k].wait()
        here = x_s[:, cols].astype(F32)
        rows_s[8 : 8 + row_count, cols] = here
        total = wide_row(bias_s, k * side, side) + taps_ref[lags : lags + 1, cols] * here
        for lag in range(1, lags + 1):
            back = rows_s[8 - lag : 8 - lag + row_count, cols]
            total = total + taps_ref[lags - lag : lags - lag + 1, cols] * (near[lag - 1] * back)
        conv_s[:, cols] = total
    slot_edge_ref[...] = jnp.zeros(slot_edge_ref.shape, F32)
    for r in range(request_count):
        begin, end = marks[r]
        length = lens_ref[0, r]

        @pl.when(jnp.logical_and(begin > -lags, begin < row_count))
        def _(r=r, begin=begin, end=end, length=length):
            keep = cont_ref[0, r].astype(F32)
            source = source_ref[0, r]
            away = lax.rem(me // 2 - source // 2 + chips, chips)
            for ref, parity in ((edge_mine_ref, core), (edge_other_ref, 1 - core)):
                @pl.when(lax.rem(source, 2) == parity)
                def _(ref=ref):
                    edge_s[0:lags, :] = keep * ref[away].astype(F32)[0:lags, :]

            for p in range(lags):
                at = begin + p

                @pl.when(jnp.logical_and(jnp.logical_and(at >= 0, at < row_count), p < length))
                def _():
                    extra = jnp.zeros((1, inner), F32)
                    for lag in range(p + 1, lags + 1):
                        extra = extra + taps_ref[lags - lag : lags - lag + 1, :] * edge_s[
                            lags + p - lag : lags + p - lag + 1, :
                        ]
                    conv_s[pl.ds(at, 1), :] = conv_s[pl.ds(at, 1), :] + extra

        @pl.when(jnp.logical_and(end > 0, end <= row_count))
        def _(r=r, end=end, length=length):
            owner = owner_ref[0, r]
            for lag in range(lags):
                @pl.when(length > lag)
                def _():
                    slot_edge_ref[owner, lags - 1 - lag : lags - lag, :] = rows_s[
                        pl.ds(end + 7 - lag, 1), :
                    ]

                @pl.when(length <= lag)
                def _():
                    slot_edge_ref[owner, lags - 1 - lag : lags - lag, :] = edge_s[
                        pl.ds(lags + length - 1 - lag, 1), :
                    ]

    for cols in blocks:
        v = conv_s[:, cols]
        mixed_ref[:, cols] = (v / (1.0 + jnp.exp(-v))).astype(BF16)
    copies[-3].wait()
    projected = lax.dot_general(
        mixed_ref[...], x_proj_ref[...], NT, preferred_element_type=F32
    )
    proj_ref[...] = projected
    rank = dt_proj_ref.shape[0]
    dt_low = projected[:, :rank].astype(BF16)
    last_begin = jnp.int32(0)
    for begin, _ in marks:
        last_begin = jnp.where(
            jnp.logical_and(begin >= 0, begin < row_count), jnp.maximum(last_begin, begin), last_begin
        )
    in_last = (row >= last_begin).astype(F32)
    for s in range(STATE):
        b_s[s] = jnp.broadcast_to(
            projected[:, rank + s : rank + s + 1] * in_last, (row_count, LANE)
        )
    m_row, m_col, same = segment_masks(row_count, marks)
    later = tripled(jnp.logical_and(m_col > m_row, same))
    copies[-2].wait()
    for k, cols in enumerate(blocks):
        step_ref[:, cols] = softplus(
            jnp.dot(dt_low, dt_proj_ref[:, cols], preferred_element_type=F32)
            + wide_row(dt_bias_s, k * side, side)
        )
    for k, cols in enumerate(blocks):
        step = step_ref[:, cols]
        suffix = jnp.dot(later, three_parts(step), preferred_element_type=F32)
        decay_ref[:, cols] = jnp.exp(-wide_row(rate_s, k * side, side) * suffix)
        push_ref[:, cols] = step * mixed_ref[:, cols].astype(F32)

    def tile_step(i, carry):
        at = pl.multiple_of(i * LANE, LANE)
        cols = pl.ds(at, LANE)
        ext_ref[:, cols] = weighted_sum(push_ref[:, cols], decay_ref[:, cols], b_s).astype(BF16)
        sums_s[pl.ds(i, 1), :] = jnp.sum(step_ref[:, cols] * in_last, axis=0, keepdims=True)
        return carry

    sums_s[...] = jnp.zeros(sums_s.shape, F32)
    lax.fori_loop(0, inner // LANE, tile_step, 0)
    write_sums(ext_ref, sums_s[...], inner)
    copies[-1].wait()


def weighted_sum(push, decay, b_ref):
    weight = push * decay
    totals = []
    for s in range(STATE):
        product = weight * b_ref[s]
        total = product[0:8, :]
        for k in range(8, push.shape[0], 8):
            total = total + product[k : k + 8, :]
        totals.append(total)
        if s + 1 < STATE:
            weight = weight * decay
    return jnp.concatenate(
        [sums_of_eight(totals[k : k + 8]) for k in range(0, STATE, 8)], axis=0
    )


def pair_kernel(tokens, *refs):
    lens_hbm, rate_hbm, mine_ref, other_ref = refs[:4]
    mine_ref, other_ref = mine_ref.at[0], other_ref.at[0]
    out_ref, lens_ref, rate_s, sems = refs[4:]
    for copy in start_all([(lens_hbm, lens_ref), (rate_hbm, rate_s)], sems):
        copy.wait()
    inner = LANE * rate_s.shape[0]
    me = lax.axis_index("seq")
    core = lax.rem(me, 2)
    second = me - core + 1
    marks = request_marks(lens_ref, second * tokens)
    whole = jnp.float32(1.0)
    for begin, _ in marks:
        whole = jnp.where(jnp.logical_and(begin >= 0, begin < tokens), 0.0, whole)
    sums = []
    for i in range(inner // LANE):
        cols = slice(i * LANE, (i + 1) * LANE)
        mine, other = mine_ref[:, cols].astype(F32), other_ref[:, cols].astype(F32)
        e0 = jnp.where(core == 0, mine, other)
        e1 = jnp.where(core == 0, other, mine)
        my_sum, other_sum = read_sum(mine_ref, i, inner), read_sum(other_ref, i, inner)
        s0 = jnp.where(core == 0, my_sum, other_sum)
        s1 = jnp.where(core == 0, other_sum, my_sum)
        rate = rate_block(rate_s[i : i + 1, :])
        out_ref[:, cols] = (e1 + whole * jnp.exp(-rate * s1) * e0).astype(BF16)
        sums.append(s1 + whole * s0)
    groups, _ = sum_layout(inner // LANE)
    sums.append(jnp.zeros((groups * STATE - len(sums), LANE), F32))
    write_sums(out_ref, jnp.concatenate(sums, axis=0), inner)


def scan_kernel(
    lens_hbm, gate_hbm, up_hbm, down_hbm, rate_hbm, skip_hbm, mixed_ref, step_ref, push_ref, proj_ref,
    y_ref, q_ref, gate_ref, up_ref, down_ref, lens_ref, rate_s, skip_s, jump_s, b_s, c_s, sems,
):
    row_count, inner = mixed_ref.shape
    copies = start_all(
        [
            (lens_hbm, lens_ref), (rate_hbm, rate_s), (skip_hbm, skip_s),
            (gate_hbm, gate_ref), (up_hbm, up_ref), (down_hbm, down_ref),
        ],
        sems,
    )
    rank = proj_ref.shape[1] - 2 * STATE
    coefs = proj_ref[:, rank : rank + 2 * STATE]
    coefs = jnp.concatenate([coefs, jnp.zeros((row_count, LANE - 2 * STATE), F32)], axis=1)
    flipped = jnp.transpose(coefs)
    for t in range(row_count):
        b_s[t] = jnp.broadcast_to(flipped[0:STATE, t : t + 1], (STATE, LANE))
        c_s[t] = jnp.broadcast_to(flipped[STATE : 2 * STATE, t : t + 1], (STATE, LANE))
    for copy in copies[:3]:
        copy.wait()
    me = lax.axis_index("seq")
    marks = request_marks(lens_ref, me * row_count)
    m_row, m_col, same = segment_masks(row_count, marks)
    earlier = tripled(jnp.logical_and(m_col <= m_row, same))
    row = lax.broadcasted_iota(jnp.int32, (row_count, 1), 0)
    jump = jnp.zeros((row_count, 1), F32)
    for begin, _ in marks:
        jump = jump + (row == begin).astype(F32) * FAR
    tiles = 5
    width = tiles * LANE
    for k, cols in enumerate(lane_blocks(inner, width)):
        step = step_ref[:, cols]
        prefix = jnp.dot(earlier, three_parts(step), preferred_element_type=F32)
        q_ref[:, cols] = jnp.exp(-wide_row(rate_s, k * tiles, tiles) * prefix)
        jump_s[:, cols] = step + jump
        y_ref[:, cols] = wide_row(skip_s, k * tiles, tiles) * mixed_ref[:, cols].astype(F32)

    def chunk_step(i, carry):
        at = pl.multiple_of(i * width, LANE)
        rates = [-LOG2E * rate_block(row_of(rate_s, i * tiles + k)) for k in range(tiles)]

        def row_step(j, held):
            first = pl.multiple_of(j * 8, 8)
            rows = pl.ds(first, 8)
            held = list(held)
            for k in range(tiles):
                lanes = pl.ds(pl.multiple_of(at + k * LANE, LANE), LANE)
                jumps, pushes = jump_s.at[rows, lanes], push_ref.at[rows, lanes]
                h = held[k]
                outs = []
                for t in range(8):
                    decay = jnp.exp2(rates[k] * jumps[t : t + 1, :])
                    h = decay * h + b_s[first + t] * pushes[t : t + 1, :]
                    product = c_s[first + t] * h
                    outs.append(product[0:8] + product[8:16])
                held[k] = h
                y_ref[rows, lanes] = y_ref[rows, lanes] + sums_of_eight(outs)
            return tuple(held)

        lax.fori_loop(
            0, row_count // 8, row_step, tuple(jnp.zeros((STATE, LANE), F32) for _ in range(tiles))
        )
        return carry

    lax.fori_loop(0, inner // width, chunk_step, 0)
    for copy in copies[3:]:
        copy.wait()


def close_kernel(stage_count, *refs):
    scalar_hbm = refs[:3]
    rate_hbm, hidden_hbm = refs[3:5]
    stage_refs = refs[5 : 5 + stage_count]
    (mine_ref, other_ref, proj_ref, y_ref, q_ref, gain_ref, weight_ref) = refs[
        5 + stage_count : 12 + stage_count
    ]
    middle_ref, normed_ref, begins_ref = refs[12 + stage_count : 15 + stage_count]
    scalars = refs[15 + stage_count : 18 + stage_count]
    rate_s, hidden_s, c_s, ssm_s, sems = refs[18 + stage_count :]
    pair_ref = other_ref.at[0]
    lens_ref, cont_ref, source_ref = scalars
    row_count, inner = y_ref.shape
    width = middle_ref.shape[1]
    chips = mine_ref.shape[0] - 1
    copies = start_all(
        list(zip(scalar_hbm, scalars)) + [(rate_hbm, rate_s), (hidden_hbm, hidden_s)], sems
    )
    me = lax.axis_index("seq")
    core = lax.rem(me, 2)
    rank = proj_ref.shape[1] - 2 * STATE
    for s in range(STATE):
        c_s[s] = jnp.broadcast_to(
            proj_ref[:, rank + STATE + s : rank + STATE + s + 1], (row_count, LANE)
        )
    ssm_s[...] = y_ref[...]
    for copy in copies:
        copy.wait()
    marks = request_marks(lens_ref, me * row_count)
    tiles = 5
    side = tiles * LANE
    block = 16
    for r in range(lens_ref.shape[1]):
        begin, end = marks[r]
        low, high = jnp.maximum(begin, 0), jnp.minimum(end, row_count)

        @pl.when(high > low)
        def _(r=r, begin=begin, low=low, high=high):
            keep = cont_ref[0, r].astype(F32)
            source = source_ref[0, r]
            away = lax.rem(me // 2 - source // 2 + chips, chips)
            for ref, parity in ((mine_ref, core), (other_ref, 1 - core)):
                @pl.when(lax.rem(source, 2) == parity)
                def _(ref=ref):
                    begins_ref[r] = keep * ref[1 + away, :, 0:inner].astype(F32)

            for k in range(stage_count + 1):
                if k < stage_count:
                    chip_first = me - core - 2 * (stage_count - k)
                    ref = stage_refs[stage_count - 1 - k]
                    stage_end = -(core + 2 * (stage_count - 1 - k)) * row_count
                    valid = jnp.logical_and(chip_first >= 0, begin < stage_end)
                else:
                    ref = pair_ref
                    valid = jnp.logical_and(core == 1, begin < 0)

                @pl.when(valid)
                def _(ref=ref):
                    for i in range(inner // LANE):
                        cols = slice(i * LANE, (i + 1) * LANE)
                        decay = jnp.exp(-rate_block(rate_s[i : i + 1, :]) * read_sum(ref, i, inner))
                        begins_ref[r, :, cols] = (
                            ref[:, cols].astype(F32) + decay * begins_ref[r, :, cols]
                        )

            def block_step(j, carry):
                first = pl.multiple_of(j * block, block)
                rows = pl.ds(first, block)
                at_row = lax.broadcasted_iota(jnp.int32, (block, 1), 0) + first
                inside = jnp.logical_and(at_row >= low, at_row < high)

                def lane_step(i, inner_carry):
                    at = pl.multiple_of(i * side, LANE)
                    cols = pl.ds(at, side)
                    q = q_ref[rows, cols]
                    total = jnp.zeros((block, side), F32)
                    for s in range(STATE - 1, -1, -1):
                        c = c_s[s, rows, :]
                        c = jnp.concatenate([c] * tiles, axis=1)
                        total = (total + c * begins_ref[r, s : s + 1, cols]) * q
                    ssm_s[rows, cols] = ssm_s[rows, cols] + jnp.where(inside, total, 0.0)
                    return inner_carry

                lax.fori_loop(0, inner // side, lane_step, 0, unroll=True)
                return carry

            lax.fori_loop(low // block, (high + block - 1) // block, block_step, 0)

    total = lax.dot_general(
        ssm_s[...].astype(BF16), weight_ref[...], NT, preferred_element_type=F32
    )
    residual = [
        jnp.transpose(hidden_s[cols, :].astype(F32)) for cols in lane_blocks(width, LANE)
    ]
    total = total + jnp.concatenate(residual, axis=1)
    middle_ref[...] = total
    scale = lax.rsqrt(jnp.mean(total * total, axis=1, keepdims=True) + NORM_EPS)
    normed_ref[...] = (total * scale * gain_ref[...]).astype(BF16)


def final_kernel(
    lens_hbm, owner_hbm, rate_hbm, step_ref, push_ref, decay_ref, proj_ref, begins_ref,
    slot_edge_ref, keep_ref, send_ref, lens_ref, owner_ref, rate_s, b_s, held_s, edge_s, sems,
):
    pairs = [(lens_hbm, lens_ref), (owner_hbm, owner_ref), (rate_hbm, rate_s)]
    for copy in start_all(pairs, sems):
        copy.wait()
    row_count, inner = step_ref.shape
    block = 32
    me = lax.axis_index("seq")
    core = lax.rem(me, 2)
    chips = keep_ref.shape[0]
    marks = request_marks(lens_ref, me * row_count)
    rank = proj_ref.shape[1] - 2 * STATE
    lags = slot_edge_ref.shape[1]
    row = lax.broadcasted_iota(jnp.int32, (row_count, 1), 0)
    keep_ref[...] = jnp.zeros(keep_ref.shape, BF16)
    send_ref[...] = jnp.zeros(send_ref.shape, BF16)
    tiles = inner // LANE
    edge_groups = (keep_ref.shape[2] - inner) // LANE
    for r in range(lens_ref.shape[1]):
        begin, end = marks[r]

        @pl.when(jnp.logical_and(end > 0, end <= row_count))
        def _(r=r, begin=begin, end=end):
            owner = owner_ref[0, r]
            there = lax.rem(owner // 2 - me // 2 + chips, chips)
            mine = lax.rem(owner, 2) == core
            inside = jnp.logical_and(row >= begin, row < end).astype(F32)
            for s in range(STATE):
                b_s[s] = jnp.broadcast_to(
                    proj_ref[:, rank + s : rank + s + 1] * inside, (row_count, LANE)
                )

            def put(cols, block):
                @pl.when(mine)
                def _():
                    keep_ref[there, :, cols] = block

                @pl.when(jnp.logical_not(mine))
                def _():
                    send_ref[there, :, cols] = block

            held_s[...] = jnp.zeros(held_s.shape, F32)

            def block_step(j, carry):
                rows = pl.ds(pl.multiple_of(j * block, block), block)

                def add_tile(i, inner_carry):
                    cols = pl.ds(pl.multiple_of(i * LANE, LANE), LANE)
                    held_s[:, cols] = held_s[:, cols] + weighted_sum(
                        push_ref[rows, cols], decay_ref[rows, cols], b_s.at[:, rows, :]
                    )
                    return inner_carry

                lax.fori_loop(0, tiles, add_tile, 0, unroll=5)
                return carry

            lax.fori_loop(
                jnp.maximum(begin, 0) // block, (end + block - 1) // block, block_step, 0
            )

            def tile_step(i, carry):
                cols = pl.ds(pl.multiple_of(i * LANE, LANE), LANE)
                span = jnp.sum(step_ref[:, cols] * inside, axis=0, keepdims=True)
                carried = jnp.exp(-rate_block(row_of(rate_s, i)) * span) * begins_ref[r, :, cols]
                put(cols, (held_s[:, cols] + carried).astype(BF16))
                return carry

            lax.fori_loop(0, tiles, tile_step, 0)
            edge_s[...] = jnp.zeros(edge_s.shape, F32)
            for lag in range(lags):
                for i in range(tiles):
                    at = lag * tiles + i
                    edge_s[at : at + 1, :] = slot_edge_ref[
                        owner, lag : lag + 1, i * LANE : (i + 1) * LANE
                    ]
            for g in range(edge_groups):
                put(
                    slice(inner + g * LANE, inner + (g + 1) * LANE),
                    edge_s[g * STATE : (g + 1) * STATE, :].astype(BF16),
                )


def unpack_kernel(lags, *refs):
    got_refs, (state_ref, edge_ref, edge_s) = refs[:-3], refs[-3:]
    inner = state_ref.shape[1]
    tiles = inner // LANE

    def whole(cols):
        total = got_refs[0][:, cols].astype(F32)
        for ref in got_refs[1:]:
            total = total + ref[:, cols].astype(F32)
        return total

    state_ref[...] = whole(slice(0, inner))
    groups = (got_refs[0].shape[1] - inner) // LANE
    for g in range(groups):
        edge_s[g * STATE : (g + 1) * STATE, :] = whole(
            slice(inner + g * LANE, inner + (g + 1) * LANE)
        )
    for i in range(tiles):
        edge_ref[:, i * LANE : (i + 1) * LANE] = jnp.concatenate(
            [edge_s[lag * tiles + i : lag * tiles + i + 1, :] for lag in range(lags)], axis=0
        ).astype(BF16)


def feed_forward(tokens, gate_ref, up_ref, down_ref):
    gate = jnp.dot(tokens, gate_ref[...], preferred_element_type=F32)
    up = jnp.dot(tokens, up_ref[...], preferred_element_type=F32)
    hidden = (gate / (1.0 + jnp.exp(-gate)) * up).astype(BF16)
    return lax.dot_general(hidden, down_ref[...], NT, preferred_element_type=F32)


def own_kernel(token_ref, middle_ref, gate_ref, up_ref, down_ref, out_ref):
    out_ref[...] = middle_ref[...] + feed_forward(token_ref[...], gate_ref, up_ref, down_ref)


def peer_kernel(*refs):
    count = (len(refs) - 3) // 2
    tokens = jnp.concatenate([ref[...] for ref in refs[:count]], axis=0)
    out = feed_forward(tokens, *refs[count : count + 3]).astype(BF16)
    part = out.shape[0] // count
    for k, ref in enumerate(refs[count + 3 :]):
        ref[...] = out[k * part : (k + 1) * part]


def far_kernel(low_ref, high_ref, gate_ref, up_ref, down_ref, out_ref):
    tokens = jnp.concatenate([low_ref[...], high_ref[...]], axis=0)
    out_ref[...] = feed_forward(tokens, gate_ref, up_ref, down_ref).astype(BF16)


def join_kernel(own_ref, *refs):
    whole = own_ref[...]
    for ref in refs[:-1]:
        whole = whole + ref[...].astype(F32)
    for cols in lane_blocks(whole.shape[1], LANE):
        refs[-1][cols, :] = jnp.transpose(whole[:, cols]).astype(BF16)


def call(kernel, outs, scratch, operands, hbm=0, limit=16, micros=1.0, last=False):
    spaces = [pltpu.HBM if k < hbm else pltpu.VMEM for k in range(len(operands))]
    operands = [pltpu.with_memory_space_constraint(a, space) for a, space in zip(operands, spaces)]
    out_kind = jax.ShapeDtypeStruct if last else pltpu.VMEM
    return pl.pallas_call(
        kernel,
        out_shape=tuple(out_kind(shape, dtype) for shape, dtype in outs),
        in_specs=[pl.BlockSpec(memory_space=space) for space in spaces],
        out_specs=tuple(pl.BlockSpec(memory_space=pltpu.VMEM) for _ in outs),
        scratch_shapes=scratch,
        compiler_params=pltpu.CompilerParams(vmem_limit_bytes=limit * 1024 * 1024),
        cost_estimate=pl.CostEstimate(
            flops=int(micros * 1.15e9), bytes_accessed=int(micros * 3.6e6), transcendentals=0
        ),
    )(*operands)


def shifted(block, axis, distance):
    size = lax.axis_size(axis)
    return lax.ppermute(block, axis, [(i, (i + distance) % size) for i in range(size)])


def passed_up(block, axis, distance):
    size = lax.axis_size(axis)
    return lax.ppermute(block, axis, [(i, i + distance) for i in range(size - distance)])


def swapped(block, axis, mask):
    return lax.ppermute(block, axis, [(i, i ^ mask) for i in range(lax.axis_size(axis))])


def shards(
    hidden_in,
    mamba_in,
    conv_weight,
    conv_bias,
    x_proj,
    dt_proj,
    dt_bias,
    decay_rate,
    skip_gain,
    out_proj,
    norm_gain,
    mlp_gate,
    mlp_up,
    mlp_down,
    cache_state,
    cache_edge,
    req_lengths,
    cont_flag,
    cache_source,
    owner_slot,
):
    x = mamba_in[0]
    row_count, inner = x.shape
    width = hidden_in.shape[2]
    lags = cache_edge.shape[2]
    peers = lax.axis_size("seq")
    tiles = inner // LANE
    scalars = (req_lengths, cont_flag, cache_source, owner_slot)
    request_count = req_lengths.shape[1]
    chips = peers // 2
    dma = pltpu.SemaphoreType.DMA
    (offer,) = call(
        offer_kernel,
        [((OFFER, inner), BF16)],
        [
            pltpu.VMEM((STATE, inner), F32),
            pltpu.VMEM((lags, inner), BF16),
            pltpu.VMEM((STATE, inner), BF16),
            dma((3,)),
        ],
        (cache_state[0, 0], cache_edge[0, 0], x),
        hbm=3,
        limit=4,
    )
    offers = [offer] + [shifted(offer, "seq", 2 * k) for k in range(1, chips)]
    (edge_mine,) = call(
        edges_kernel, [((chips, OFFER - STATE, inner), BF16)], [], tuple(offers), limit=4
    )
    edge_other = swapped(edge_mine, "seq", 1)
    bias, dt_bias, rate, skip = [
        v.reshape(tiles, LANE) for v in (conv_bias, dt_bias, decay_rate, skip_gain)
    ]
    groups, extra = sum_layout(tiles)
    ext_shape = (STATE, inner + extra)
    scalar_s = pltpu.SMEM((1, request_count), jnp.int32)
    vec_s = pltpu.VMEM((tiles, LANE), F32)
    rank = x_proj.shape[1]
    full = ((row_count, inner), F32)
    bundle_shape = ((chips + 1, *ext_shape), BF16)
    mixed, step, push, decay, proj, slot_edge, weight, bundle = call(
        functools.partial(terms_kernel, lags, chips),
        [
            ((row_count, inner), BF16),
            full,
            full,
            full,
            ((row_count, rank), F32),
            ((peers, lags, inner), F32),
            ((width, inner), BF16),
            bundle_shape,
        ],
        [
            scalar_s, scalar_s, scalar_s, scalar_s,
            pltpu.VMEM((row_count, inner), BF16),
            pltpu.VMEM(conv_weight.shape, F32),
            pltpu.VMEM((rank, inner), BF16),
            pltpu.VMEM(dt_proj.shape, BF16),
            vec_s, vec_s, vec_s,
            pltpu.VMEM((8 + row_count, inner), F32),
            pltpu.VMEM((row_count, inner), F32),
            pltpu.VMEM((8, inner), F32),
            pltpu.VMEM((STATE, row_count, LANE), F32),
            pltpu.VMEM((groups * STATE, LANE), F32),
            dma((11 + len(lane_blocks(inner, SIDE)),)),
        ],
        (
            *scalars, x, conv_weight, x_proj.T, dt_proj, out_proj.T, bias, dt_bias, rate,
            edge_mine, edge_other, *offers,
        ),
        hbm=12,
        micros=10,
    )
    other = swapped(bundle, "seq", 1)
    (chip,) = call(
        functools.partial(pair_kernel, row_count),
        [(ext_shape, BF16)],
        [scalar_s, vec_s, dma((2,))],
        (req_lengths, rate, bundle, other),
        hbm=2,
        limit=4,
    )
    stages = [passed_up(chip, "seq", 2 * k) for k in range(1, chips)]
    y, q, gate, up, down = call(
        scan_kernel,
        [full, full, (mlp_gate.shape, BF16), (mlp_up.shape, BF16), (mlp_down.shape[::-1], BF16)],
        [
            scalar_s, vec_s, vec_s,
            pltpu.VMEM((row_count, inner), F32),
            pltpu.VMEM((row_count, STATE, LANE), F32),
            pltpu.VMEM((row_count, STATE, LANE), F32),
            dma((6,)),
        ],
        (req_lengths, mlp_gate, mlp_up, mlp_down.T, rate, skip, mixed, step, push, proj),
        hbm=6,
        limit=8,
        micros=8,
    )
    middle, normed, begins = call(
        functools.partial(close_kernel, len(stages)),
        [
            ((row_count, width), F32),
            ((row_count, width), BF16),
            ((request_count, STATE, inner), F32),
        ],
        [
            scalar_s, scalar_s, scalar_s,
            vec_s,
            pltpu.VMEM((width, row_count), BF16),
            pltpu.VMEM((STATE, row_count, LANE), F32),
            pltpu.VMEM((row_count, inner), F32),
            dma((5,)),
        ],
        (
            *scalars[:3], rate, hidden_in[0].T, *stages, bundle, other, proj, y, q,
            norm_gain.reshape(1, width), weight,
        ),
        hbm=5,
        limit=12,
        micros=6,
    )
    weights = (gate, up, down)
    tokens_out = ((row_count, width), BF16)
    from_x, from_y = swapped(normed, "req", 1), swapped(normed, "req", 2)
    (own,) = call(
        own_kernel, [((row_count, width), F32)], [], (normed, middle, *weights), limit=4, micros=3
    )
    edge_groups = -(-lags * tiles // STATE)
    packed = ((chips, STATE, inner + edge_groups * LANE), BF16)
    keep, send = call(
        final_kernel,
        [packed, packed],
        [
            scalar_s, scalar_s, vec_s,
            pltpu.VMEM((STATE, row_count, LANE), F32),
            pltpu.VMEM((STATE, inner), F32),
            pltpu.VMEM((edge_groups * STATE, LANE), F32),
            dma((3,)),
        ],
        (req_lengths, owner_slot, rate, step, push, decay, proj, begins, slot_edge),
        hbm=3,
        limit=4,
        micros=4,
    )
    from_x, from_y, send = lax.optimization_barrier((from_x, from_y, send))
    got = swapped(send, "seq", 1)
    half = row_count // 2
    far_high = swapped(from_x[half:], "req", 2)
    far_low = swapped(from_y[:half], "req", 1)
    at_x, at_y = call(
        peer_kernel, [tokens_out] * 2, [], (from_x, from_y, *weights), limit=6, micros=4.5
    )
    got = lax.optimization_barrier((got, at_x))[0]
    parts = [keep[k] + got[k] for k in range(chips)]
    far_low, far_high, parts = lax.optimization_barrier((far_low, far_high, parts))
    back_x, back_y = swapped(at_x, "req", 1), swapped(at_y, "req", 2)
    (at_far,) = call(far_kernel, [tokens_out], [], (far_low, far_high, *weights), limit=4, micros=3)
    back_far = swapped(at_far, "req", 3)
    parts = [parts[0]] + [shifted(parts[k], "seq", 2 * k) for k in range(1, chips)]
    new_state, new_edge = call(
        functools.partial(unpack_kernel, lags),
        [((STATE, inner), F32), ((lags, inner), BF16)],
        [pltpu.VMEM((edge_groups * STATE, LANE), F32)],
        tuple(parts),
        limit=4,
        last=True,
    )
    (block_rows,) = call(
        join_kernel, [((width, row_count), BF16)], [], (own, back_x, back_y, back_far), limit=4,
        last=True,
    )
    return (block_rows.T[None], new_state[None, None], new_edge[None, None])


def solution(mesh):
    return jax.shard_map(
        shards,
        mesh=mesh,
        in_specs=(
            P("req", "seq", None),
            P("req", "seq", None),
            P(),
            P(),
            P(),
            P(),
            P(),
            P(),
            P(),
            P(),
            P(),
            P(None, "req"),
            P(None, "req"),
            P("req", None),
            P("req", "seq", None, None),
            P("req", "seq", None, None),
            P("req", None),
            P("req", None),
            P("req", None),
            P("req", None),
        ),
        out_specs=(P("req", "seq", None), P("req", "seq", None, None), P("req", "seq", None, None)),
        check_vma=False,
    )
```

```python
import functools

import jax
import jax.numpy as jnp
from jax import lax
from jax.experimental import pallas as pl
from jax.experimental.pallas import tpu as pltpu
from jax.sharding import PartitionSpec as P

STATE = 16
NORM_EPS = 1e-06
LANE = 128
FAR = 1e30
OFFER = 24
LOG2E = 1.4426950408889634
F32 = jnp.float32
BF16 = jnp.bfloat16


def request_marks(lens_ref, first_pos):
    marks = []
    begin = -first_pos
    for r in range(lens_ref.shape[1]):
        end = begin + lens_ref[0, r]
        marks.append((begin, end))
        begin = end
    return marks


def segment_of(index, marks):
    total = jnp.zeros(index.shape, jnp.int32)
    for begin, _ in marks:
        total = total + (index >= begin).astype(jnp.int32)
    return total


def segment_masks(row_count, marks):
    row = lax.broadcasted_iota(jnp.int32, (row_count, row_count), 0)
    col = lax.broadcasted_iota(jnp.int32, (row_count, row_count), 1)
    same = segment_of(row, marks) == segment_of(col, marks)
    return row, col, same


def three_parts(values):
    high = values.astype(BF16)
    rest = values - high.astype(F32)
    middle = rest.astype(BF16)
    low = (rest - middle.astype(F32)).astype(BF16)
    return jnp.concatenate([high, middle, low], axis=0)


def tripled(mask):
    one = mask.astype(F32).astype(BF16)
    return jnp.concatenate([one, one, one], axis=1)


def rate_block(rate_row):
    power = lax.broadcasted_iota(jnp.int32, (STATE, rate_row.shape[1]), 0) + 1
    return power.astype(F32) * rate_row


def row_of(vec_ref, tile):
    return vec_ref[pl.ds(tile, 1), :]


def wide_row(vec_ref, first, count):
    return jnp.concatenate([vec_ref[first + k : first + k + 1, :] for k in range(count)], axis=1)


def sums_of_eight(parts):
    sub = lax.broadcasted_iota(jnp.int32, parts[0].shape, 0)
    stride = 1
    while len(parts) > 1:
        first = jnp.bitwise_and(sub, stride) == 0
        parts = [
            jnp.where(first, a, b) + pltpu.roll(jnp.where(first, b, a), stride, 0)
            for a, b in zip(parts[0::2], parts[1::2])
        ]
        stride = 2 * stride
    return parts[0]


def softplus(v):
    return jnp.maximum(v, 0.0) + jnp.log1p(jnp.exp(-jnp.abs(v)))


def sum_layout(tiles):
    groups = -(-tiles // STATE)
    return groups, 2 * groups * LANE


def read_sum(ext_ref, tile, inner):
    groups, _ = sum_layout(inner // LANE)
    group, row = divmod(tile, STATE)
    high = inner + group * LANE
    low = high + groups * LANE
    return ext_ref[row : row + 1, high : high + LANE].astype(F32) + ext_ref[
        row : row + 1, low : low + LANE
    ].astype(F32)


def write_sums(ext_ref, sums, inner):
    groups, _ = sum_layout(inner // LANE)
    for group in range(groups):
        part = sums[group * STATE : (group + 1) * STATE, :]
        high = part.astype(BF16)
        low = (part - high.astype(F32)).astype(BF16)
        at = inner + group * LANE
        ext_ref[:, at : at + LANE] = high
        ext_ref[:, at + groups * LANE : at + (groups + 1) * LANE] = low


NT = (((1,), (1,)), ((), ()))
SIDE = 5 * LANE


def start_all(pairs, sems):
    copies = [pltpu.make_async_copy(src, dst, sems.at[k]) for k, (src, dst) in enumerate(pairs)]
    for copy in copies:
        copy.start()
    return copies


def lane_blocks(size, width):
    return [slice(at, min(at + width, size)) for at in range(0, size, width)]


def offer_kernel(state_hbm, edge_hbm, x_hbm, out_ref, state_s, edge_s, tail_s, sems):
    rows = tail_s.shape[0]
    last = x_hbm.at[pl.ds(x_hbm.shape[0] - rows, rows)]
    for copy in start_all([(state_hbm, state_s), (edge_hbm, edge_s), (last, tail_s)], sems):
        copy.wait()
    lags = edge_s.shape[0]
    tail = tail_s[...].astype(F32)[rows - lags :]
    spare = jnp.zeros((OFFER - STATE - 2 * lags, tail.shape[1]), F32)
    whole = jnp.concatenate([state_s[...], edge_s[...].astype(F32), tail, spare], axis=0)
    out_ref[...] = whole.astype(BF16)


def edges_kernel(*refs):
    for k, ref in enumerate(refs[:-1]):
        refs[-1][k] = ref[...].astype(F32)[STATE:].astype(BF16)


def conv_kernel(
    lens_hbm, x_hbm, taps_hbm, bias_hbm, dt_bias_hbm, rate_hbm, skip_hbm, x_proj_hbm, dt_proj_hbm,
    out_proj_hbm, conv_ref, rows_ref, taps_ref, dt_bias_ref, rate_ref, skip_ref, x_proj_ref,
    dt_proj_ref, weight_ref, lens_ref, x_s, bias_s, sems,
):
    row_count, inner = x_s.shape
    lags = taps_ref.shape[0] - 1
    blocks = lane_blocks(inner, SIDE)
    pairs = [(lens_hbm, lens_ref), (taps_hbm, taps_ref), (bias_hbm, bias_s)]
    pairs += [(x_hbm.at[:, cols], x_s.at[:, cols]) for cols in blocks]
    pairs += [
        (dt_bias_hbm, dt_bias_ref), (rate_hbm, rate_ref), (skip_hbm, skip_ref),
        (x_proj_hbm, x_proj_ref), (dt_proj_hbm, dt_proj_ref), (out_proj_hbm, weight_ref),
    ]
    copies = start_all(pairs, sems)
    for copy in copies[:3]:
        copy.wait()
    marks = request_marks(lens_ref, lax.axis_index("seq") * row_count)
    row = lax.broadcasted_iota(jnp.int32, (row_count, 1), 0)
    near = []
    for lag in range(1, lags + 1):
        hit = jnp.zeros((row_count, 1), jnp.int32)
        for begin, _ in marks:
            hit = hit + jnp.logical_and(row >= begin, row < begin + lag).astype(jnp.int32)
        near.append((hit == 0).astype(F32))
    rows_ref[0:8, :] = jnp.zeros((8, inner), F32)
    for k, cols in enumerate(blocks):
        copies[3 + k].wait()
        here = x_s[:, cols].astype(F32)
        rows_ref[8 : 8 + row_count, cols] = here
        total = wide_row(bias_s, k * (SIDE // LANE), SIDE // LANE) + taps_ref[
            lags : lags + 1, cols
        ] * here
        for lag in range(1, lags + 1):
            back = rows_ref[8 - lag : 8 - lag + row_count, cols]
            total = total + taps_ref[lags - lag : lags - lag + 1, cols] * (near[lag - 1] * back)
        conv_ref[:, cols] = total
    for copy in copies[3 + len(blocks) :]:
        copy.wait()


def terms_kernel(lags, seed_count, *refs):
    scalar_hbm = refs[:4]
    (conv_ref, rows_ref, taps_ref, dt_bias_s, rate_s, skip_s, x_proj_ref, dt_proj_ref,
     edge_mine_ref, edge_other_ref) = refs[4:14]
    seed_refs = refs[14 : 14 + seed_count]
    refs = refs[14 + seed_count :]
    (step_ref, jump_ref, push_ref, base_ref, decay_ref, b_s, c_s, coef_ref, slot_edge_ref,
     bundle_ref) = refs[:10]
    scalars = refs[10:14]
    mixed_s, conv_s, edge_s, tail_s, sums_s, sems = refs[14:]
    ext_ref = bundle_ref.at[0]
    lens_ref, cont_ref, source_ref, owner_ref = scalars
    row_count, inner = conv_s.shape
    request_count = lens_ref.shape[1]
    chips = edge_mine_ref.shape[0]
    blocks = lane_blocks(inner, SIDE)
    side = SIDE // LANE
    copies = start_all(list(zip(scalar_hbm, scalars)), sems)
    me = lax.axis_index("seq")
    core = lax.rem(me, 2)
    row = lax.broadcasted_iota(jnp.int32, (row_count, 1), 0)
    for cols in blocks:
        conv_s[:, cols] = conv_ref[:, cols]
    for k, ref in enumerate(seed_refs):
        bundle_ref[1 + k, :, 0:inner] = ref[...].astype(F32)[:STATE].astype(BF16)
    tail_s[0:lags, :] = edge_other_ref[1 - core].astype(F32)[lags : 2 * lags, :]
    slot_edge_ref[...] = jnp.zeros(slot_edge_ref.shape, F32)
    for copy in copies:
        copy.wait()
    marks = request_marks(lens_ref, me * row_count)
    for p in range(lags):
        extra = jnp.zeros((1, inner), F32)
        for lag in range(p + 1, lags + 1):
            near = jnp.float32(1.0)
            for begin, _ in marks:
                near = jnp.where(jnp.logical_and(begin <= p, begin > p - lag), 0.0, near)
            extra = extra + taps_ref[lags - lag : lags - lag + 1, :] * (
                near * tail_s[lags + p - lag : lags + p - lag + 1, :]
            )
        conv_s[p : p + 1, :] = conv_s[p : p + 1, :] + extra
    for r in range(request_count):
        begin, end = marks[r]
        length = lens_ref[0, r]

        @pl.when(jnp.logical_and(begin > -lags, begin < row_count))
        def _(r=r, begin=begin, end=end, length=length):
            keep = cont_ref[0, r].astype(F32)
            source = source_ref[0, r]
            away = lax.rem(me // 2 - source // 2 + chips, chips)
            for ref, parity in ((edge_mine_ref, core), (edge_other_ref, 1 - core)):
                @pl.when(lax.rem(source, 2) == parity)
                def _(ref=ref):
                    edge_s[0:lags, :] = keep * ref[away].astype(F32)[0:lags, :]

            for p in range(lags):
                at = begin + p

                @pl.when(jnp.logical_and(jnp.logical_and(at >= 0, at < row_count), p < length))
                def _():
                    extra = jnp.zeros((1, inner), F32)
                    for lag in range(p + 1, lags + 1):
                        extra = extra + taps_ref[lags - lag : lags - lag + 1, :] * edge_s[
                            lags + p - lag : lags + p - lag + 1, :
                        ]
                    conv_s[pl.ds(at, 1), :] = conv_s[pl.ds(at, 1), :] + extra

        @pl.when(jnp.logical_and(end > 0, end <= row_count))
        def _(r=r, end=end, length=length):
            owner = owner_ref[0, r]
            for lag in range(lags):
                at = end - 1 - lag

                @pl.when(jnp.logical_and(length > lag, at >= 0))
                def _():
                    slot_edge_ref[owner, lags - 1 - lag : lags - lag, :] = rows_ref[
                        pl.ds(8 + at, 1), :
                    ]

                @pl.when(jnp.logical_and(length > lag, at < 0))
                def _():
                    slot_edge_ref[owner, lags - 1 - lag : lags - lag, :] = tail_s[
                        pl.ds(lags + at, 1), :
                    ]

                @pl.when(length <= lag)
                def _():
                    slot_edge_ref[owner, lags - 1 - lag : lags - lag, :] = edge_s[
                        pl.ds(lags + length - 1 - lag, 1), :
                    ]

    for k, cols in enumerate(blocks):
        v = conv_s[:, cols]
        mixed = (v / (1.0 + jnp.exp(-v))).astype(BF16)
        mixed_s[:, cols] = mixed
        base_ref[:, cols] = wide_row(skip_s, k * side, side) * mixed.astype(F32)
    projected = lax.dot_general(mixed_s[...], x_proj_ref[...], NT, preferred_element_type=F32)
    rank = dt_proj_ref.shape[0]
    dt_low = projected[:, :rank].astype(BF16)
    coef_ref[...] = projected[:, rank : rank + 2 * STATE]
    for s in range(STATE):
        at = rank + s
        b_s[s] = jnp.broadcast_to(projected[:, at : at + 1], (row_count, LANE))
        at = rank + STATE + s
        c_s[s] = jnp.broadcast_to(projected[:, at : at + 1], (row_count, LANE))
    last_begin = jnp.int32(0)
    jump = jnp.zeros((row_count, 1), F32)
    for begin, _ in marks:
        last_begin = jnp.where(
            jnp.logical_and(begin >= 0, begin < row_count), jnp.maximum(last_begin, begin), last_begin
        )
        jump = jump + (row == begin).astype(F32) * FAR
    in_last = (row >= last_begin).astype(F32)
    m_row, m_col, same = segment_masks(row_count, marks)
    later = tripled(jnp.logical_and(m_col > m_row, same))
    for k, cols in enumerate(blocks):
        step = softplus(
            jnp.dot(dt_low, dt_proj_ref[:, cols], preferred_element_type=F32)
            + wide_row(dt_bias_s, k * side, side)
        )
        step_ref[:, cols] = step
        jump_ref[:, cols] = step + jump
        push_ref[:, cols] = step * mixed_s[:, cols].astype(F32)
    for k, cols in enumerate(blocks):
        suffix = jnp.dot(later, three_parts(step_ref[:, cols]), preferred_element_type=F32)
        decay_ref[:, cols] = jnp.exp(-wide_row(rate_s, k * side, side) * suffix)

    def tile_step(i, carry):
        at = pl.multiple_of(i * LANE, LANE)
        cols = pl.ds(at, LANE)
        ext_ref[:, cols] = weighted_sum(
            push_ref[:, cols] * in_last, decay_ref[:, cols], b_s
        ).astype(BF16)
        sums_s[pl.ds(i, 1), :] = jnp.sum(step_ref[:, cols] * in_last, axis=0, keepdims=True)
        return carry

    sums_s[...] = jnp.zeros(sums_s.shape, F32)
    lax.fori_loop(0, inner // LANE, tile_step, 0, unroll=5)
    write_sums(ext_ref, sums_s[...], inner)


def weighted_sum(push, decay, b_ref):
    weight = push * decay
    totals = []
    for s in range(STATE):
        product = weight * b_ref[s]
        total = product[0:8, :]
        for k in range(8, push.shape[0], 8):
            total = total + product[k : k + 8, :]
        totals.append(total)
        if s + 1 < STATE:
            weight = weight * decay
    return jnp.concatenate(
        [sums_of_eight(totals[k : k + 8]) for k in range(0, STATE, 8)], axis=0
    )


def link_spans(earlier_of, later_of, whole, rate_ref, out_ref):
    tiles = rate_ref.shape[0]
    inner = tiles * LANE
    sums = []
    for i in range(tiles):
        cols = slice(i * LANE, (i + 1) * LANE)
        e0, s0 = earlier_of(cols, i, inner)
        e1, s1 = later_of(cols, i, inner)
        rate = rate_block(rate_ref[i : i + 1, :])
        out_ref[:, cols] = (e1 + whole * jnp.exp(-rate * s1) * e0).astype(BF16)
        sums.append(s1 + whole * s0)
    groups, _ = sum_layout(tiles)
    sums.append(jnp.zeros((groups * STATE - len(sums), LANE), F32))
    write_sums(out_ref, jnp.concatenate(sums, axis=0), inner)


def unbroken(marks, first, stop):
    whole = jnp.float32(1.0)
    for begin, _ in marks:
        whole = jnp.where(jnp.logical_and(begin >= first, begin < stop), 0.0, whole)
    return whole


def reader(ref):
    return lambda cols, i, inner: (ref[:, cols].astype(F32), read_sum(ref, i, inner))


def pair_kernel(tokens, lens_hbm, rate_ref, mine_ref, other_ref, out_ref, lens_ref, sems):
    for copy in start_all([(lens_hbm, lens_ref)], sems):
        copy.wait()
    core = lax.rem(lax.axis_index("seq"), 2)
    marks = request_marks(lens_ref, lax.axis_index("seq") * tokens)
    mine, other = reader(mine_ref.at[0]), reader(other_ref.at[0])

    def choose(number):
        def read(*where):
            return [jnp.where(core == number, a, b) for a, b in zip(mine(*where), other(*where))]

        return read

    second = (1 - core) * tokens
    link_spans(choose(0), choose(1), unbroken(marks, second, second + tokens), rate_ref, out_ref)


def span_kernel(tokens, chips, lens_hbm, rate_ref, mine_ref, before_ref, out_ref, lens_ref, sems):
    for copy in start_all([(lens_hbm, lens_ref)], sems):
        copy.wait()
    core = lax.rem(lax.axis_index("seq"), 2)
    marks = request_marks(lens_ref, lax.axis_index("seq") * tokens)
    stop = (2 - core) * tokens
    whole = unbroken(marks, stop - 2 * chips * tokens, stop)
    link_spans(reader(before_ref), reader(mine_ref), whole, rate_ref, out_ref)


def spread_kernel(lens_hbm, rate_s, step_ref, coef_ref, b_ref, c_ref, q_ref, lens_ref, sems):
    row_count, inner = step_ref.shape
    copies = start_all([(lens_hbm, lens_ref)], sems)
    spare = jnp.zeros((row_count, LANE - 2 * STATE), F32)
    flipped = jnp.transpose(jnp.concatenate([coef_ref[...], spare], axis=1))
    for t in range(row_count):
        b_ref[t] = jnp.broadcast_to(flipped[0:STATE, t : t + 1], (STATE, LANE))
        c_ref[t] = jnp.broadcast_to(flipped[STATE : 2 * STATE, t : t + 1], (STATE, LANE))
    copies[0].wait()
    marks = request_marks(lens_ref, lax.axis_index("seq") * row_count)
    m_row, m_col, same = segment_masks(row_count, marks)
    earlier = tripled(jnp.logical_and(m_col <= m_row, same))
    side = SIDE // LANE
    for k, cols in enumerate(lane_blocks(inner, SIDE)):
        prefix = jnp.dot(earlier, three_parts(step_ref[:, cols]), preferred_element_type=F32)
        q_ref[:, cols] = jnp.exp(-wide_row(rate_s, k * side, side) * prefix)


def scan_kernel(first_side, sides, fetched, *refs):
    fetch_hbm = refs[:fetched]
    rate_s, jump_ref, push_ref, base_ref, b_s, c_s, y_ref = refs[fetched : fetched + 7]
    copies = start_all(list(zip(fetch_hbm, refs[fetched + 7 :])), refs[-1])
    row_count = jump_ref.shape[0]
    tiles = SIDE // LANE
    width = SIDE

    def chunk_step(i, carry):
        at = pl.multiple_of((first_side + i) * width, LANE)
        rates = [-LOG2E * rate_block(row_of(rate_s, (first_side + i) * tiles + k)) for k in range(tiles)]

        def row_step(j, held):
            first = pl.multiple_of(j * 8, 8)
            rows = pl.ds(first, 8)
            held = list(held)
            for k in range(tiles):
                lanes = pl.ds(pl.multiple_of(at + k * LANE, LANE), LANE)
                jumps, pushes = jump_ref.at[rows, lanes], push_ref.at[rows, lanes]
                h = held[k]
                outs = []
                for t in range(8):
                    decay = jnp.exp2(rates[k] * jumps[t : t + 1, :])
                    h = decay * h + b_s[first + t] * pushes[t : t + 1, :]
                    product = c_s[first + t] * h
                    outs.append(product[0:8] + product[8:16])
                held[k] = h
                out_lanes = pl.ds(pl.multiple_of(i * width + k * LANE, LANE), LANE)
                y_ref[rows, out_lanes] = base_ref[rows, lanes] + sums_of_eight(outs)
            return tuple(held)

        lax.fori_loop(
            0, row_count // 8, row_step, tuple(jnp.zeros((STATE, LANE), F32) for _ in range(tiles)),
            unroll=2,
        )
        return carry

    lax.fori_loop(0, sides, chunk_step, 0)
    for copy in copies:
        copy.wait()


def close_kernel(stage_count, *refs):
    scalar_hbm = refs[:3]
    rate_hbm, hidden_hbm = refs[3:5]
    stage_refs = refs[5 : 5 + stage_count]
    (mine_ref, other_ref, c_s, y_first_ref, y_rest_ref, q_ref, gain_ref, weight_ref) = refs[
        5 + stage_count : 13 + stage_count
    ]
    refs = refs[1:]
    middle_ref, normed_ref, begins_ref = refs[12 + stage_count : 15 + stage_count]
    scalars = refs[15 + stage_count : 18 + stage_count]
    rate_s, hidden_s, ssm_s, sems = refs[18 + stage_count :]
    pair_ref = other_ref.at[0]
    lens_ref, cont_ref, source_ref = scalars
    row_count, inner = q_ref.shape
    width = middle_ref.shape[0]
    chips = mine_ref.shape[0] - 1
    copies = start_all(
        list(zip(scalar_hbm, scalars)) + [(rate_hbm, rate_s), (hidden_hbm, hidden_s)], sems
    )
    me = lax.axis_index("seq")
    core = lax.rem(me, 2)
    parting = y_first_ref.shape[1]
    ssm_s[:, 0:parting] = y_first_ref[...]
    ssm_s[:, parting:inner] = y_rest_ref[...]
    for copy in copies:
        copy.wait()
    marks = request_marks(lens_ref, me * row_count)
    tiles = 5
    side = tiles * LANE
    block = 32
    for r in range(lens_ref.shape[1]):
        begin, end = marks[r]
        low, high = jnp.maximum(begin, 0), jnp.minimum(end, row_count)

        @pl.when(high > low)
        def _(r=r, begin=begin, low=low, high=high):
            keep = cont_ref[0, r].astype(F32)
            source = source_ref[0, r]
            away = lax.rem(me // 2 - source // 2 + chips, chips)
            for ref, parity in ((mine_ref, core), (other_ref, 1 - core)):
                @pl.when(lax.rem(source, 2) == parity)
                def _(ref=ref):
                    begins_ref[r] = keep * ref[1 + away, :, 0:inner].astype(F32)

            for k in range(stage_count + 1):
                if k < stage_count:
                    away = 1 << (stage_count - 1 - k)
                    chip_first = me - core - 2 * away
                    ref = stage_refs[stage_count - 1 - k]
                    stage_end = -(core + 2 * (away - 1)) * row_count
                    valid = jnp.logical_and(chip_first >= 0, begin < stage_end)
                else:
                    ref = pair_ref
                    valid = jnp.logical_and(core == 1, begin < 0)

                @pl.when(valid)
                def _(ref=ref):
                    for i in range(inner // LANE):
                        cols = slice(i * LANE, (i + 1) * LANE)
                        decay = jnp.exp(-rate_block(rate_s[i : i + 1, :]) * read_sum(ref, i, inner))
                        begins_ref[r, :, cols] = (
                            ref[:, cols].astype(F32) + decay * begins_ref[r, :, cols]
                        )

            def block_step(j, carry):
                first = pl.multiple_of(j * block, block)
                rows = pl.ds(first, block)
                at_row = lax.broadcasted_iota(jnp.int32, (block, 1), 0) + first
                inside = jnp.logical_and(at_row >= low, at_row < high)

                def lane_step(i, inner_carry):
                    at = pl.multiple_of(i * side, LANE)
                    cols = pl.ds(at, side)
                    q = q_ref[rows, cols]
                    total = jnp.zeros((block, side), F32)
                    for s in range(STATE - 1, -1, -1):
                        c = c_s[s, rows, :]
                        c = jnp.concatenate([c] * tiles, axis=1)
                        total = (total + c * begins_ref[r, s : s + 1, cols]) * q
                    ssm_s[rows, cols] = ssm_s[rows, cols] + jnp.where(inside, total, 0.0)
                    return inner_carry

                lax.fori_loop(0, inner // side, lane_step, 0, unroll=True)
                return carry

            lax.fori_loop(low // block, (high + block - 1) // block, block_step, 0)

    total = hidden_s[...].astype(F32) + lax.dot_general(
        weight_ref[...], ssm_s[...].astype(BF16), NT, preferred_element_type=F32
    )
    middle_ref[...] = total
    total = total * lax.rsqrt(jnp.mean(total * total, axis=0, keepdims=True) + NORM_EPS)
    for cols in lane_blocks(width, LANE):
        normed_ref[:, cols] = (jnp.transpose(total[cols, :]) * gain_ref[:, cols]).astype(BF16)


def final_kernel(
    lens_hbm, owner_hbm, rate_hbm, step_ref, push_ref, decay_ref, b_ref, begins_ref,
    slot_edge_ref, keep_ref, send_ref, lens_ref, owner_ref, rate_s, held_s, edge_s, sems,
):
    pairs = [(lens_hbm, lens_ref), (owner_hbm, owner_ref), (rate_hbm, rate_s)]
    for copy in start_all(pairs, sems):
        copy.wait()
    row_count, inner = step_ref.shape
    block = 32
    me = lax.axis_index("seq")
    core = lax.rem(me, 2)
    chips = keep_ref.shape[0]
    marks = request_marks(lens_ref, me * row_count)
    lags = slot_edge_ref.shape[1]
    row = lax.broadcasted_iota(jnp.int32, (row_count, 1), 0)
    keep_ref[...] = jnp.zeros(keep_ref.shape, BF16)
    send_ref[...] = jnp.zeros(send_ref.shape, BF16)
    tiles = inner // LANE
    edge_groups = (keep_ref.shape[2] - inner) // LANE
    for r in range(lens_ref.shape[1]):
        begin, end = marks[r]

        @pl.when(jnp.logical_and(end > 0, end <= row_count))
        def _(r=r, begin=begin, end=end):
            owner = owner_ref[0, r]
            there = lax.rem(owner // 2 - me // 2 + chips, chips)
            mine = lax.rem(owner, 2) == core
            inside = jnp.logical_and(row >= begin, row < end).astype(F32)
            def put(cols, block):
                @pl.when(mine)
                def _():
                    keep_ref[there, :, cols] = block

                @pl.when(jnp.logical_not(mine))
                def _():
                    send_ref[there, :, cols] = block

            held_s[...] = jnp.zeros(held_s.shape, F32)

            def block_step(j, carry):
                first = pl.multiple_of(j * block, block)
                rows = pl.ds(first, block)
                at_row = lax.broadcasted_iota(jnp.int32, (block, 1), 0) + first
                here = jnp.logical_and(at_row >= begin, at_row < end).astype(F32)

                def add_tile(i, inner_carry):
                    cols = pl.ds(pl.multiple_of(i * LANE, LANE), LANE)
                    held_s[:, cols] = held_s[:, cols] + weighted_sum(
                        push_ref[rows, cols] * here, decay_ref[rows, cols], b_ref.at[:, rows, :]
                    )
                    return inner_carry

                lax.fori_loop(0, tiles, add_tile, 0, unroll=5)
                return carry

            lax.fori_loop(
                jnp.maximum(begin, 0) // block, (end + block - 1) // block, block_step, 0
            )

            def tile_step(i, carry):
                cols = pl.ds(pl.multiple_of(i * LANE, LANE), LANE)
                span = jnp.sum(step_ref[:, cols] * inside, axis=0, keepdims=True)
                carried = jnp.exp(-rate_block(row_of(rate_s, i)) * span) * begins_ref[r, :, cols]
                put(cols, (held_s[:, cols] + carried).astype(BF16))
                return carry

            lax.fori_loop(0, tiles, tile_step, 0)
            edge_s[...] = jnp.zeros(edge_s.shape, F32)
            for lag in range(lags):
                for i in range(tiles):
                    at = lag * tiles + i
                    edge_s[at : at + 1, :] = slot_edge_ref[
                        owner, lag : lag + 1, i * LANE : (i + 1) * LANE
                    ]
            for g in range(edge_groups):
                put(
                    slice(inner + g * LANE, inner + (g + 1) * LANE),
                    edge_s[g * STATE : (g + 1) * STATE, :].astype(BF16),
                )


def unpack_kernel(lags, *refs):
    got_refs, (state_ref, edge_ref, edge_s) = refs[:-3], refs[-3:]
    inner = state_ref.shape[1]
    tiles = inner // LANE

    def whole(cols):
        total = got_refs[0][:, cols].astype(F32)
        for ref in got_refs[1:]:
            total = total + ref[:, cols].astype(F32)
        return total

    state_ref[...] = whole(slice(0, inner))
    groups = (got_refs[0].shape[1] - inner) // LANE
    for g in range(groups):
        edge_s[g * STATE : (g + 1) * STATE, :] = whole(
            slice(inner + g * LANE, inner + (g + 1) * LANE)
        )
    for i in range(tiles):
        edge_ref[:, i * LANE : (i + 1) * LANE] = jnp.concatenate(
            [edge_s[lag * tiles + i : lag * tiles + i + 1, :] for lag in range(lags)], axis=0
        ).astype(BF16)


def feed_forward(tokens, gate_ref, up_ref, down_ref):
    gate = jnp.dot(tokens, gate_ref[...], preferred_element_type=F32)
    up = jnp.dot(tokens, up_ref[...], preferred_element_type=F32)
    hidden = (gate / (1.0 + jnp.exp(-gate)) * up).astype(BF16)
    return lax.dot_general(hidden, down_ref[...], NT, preferred_element_type=F32)


def own_kernel(token_ref, gate_ref, up_ref, down_ref, out_ref):
    out_ref[...] = feed_forward(token_ref[...], gate_ref, up_ref, down_ref)


def peer_kernel(*refs):
    count = (len(refs) - 3) // 2
    tokens = jnp.concatenate([ref[...] for ref in refs[:count]], axis=0)
    out = feed_forward(tokens, *refs[count : count + 3]).astype(BF16)
    part = out.shape[0] // count
    for k, ref in enumerate(refs[count + 3 :]):
        ref[...] = out[k * part : (k + 1) * part]


def far_kernel(low_ref, high_ref, gate_ref, up_ref, down_ref, out_ref):
    tokens = jnp.concatenate([low_ref[...], high_ref[...]], axis=0)
    out_ref[...] = feed_forward(tokens, gate_ref, up_ref, down_ref).astype(BF16)


def join_kernel(middle_ref, own_ref, *refs):
    whole = own_ref[...]
    for ref in refs[:-1]:
        whole = whole + ref[...].astype(F32)
    for cols in lane_blocks(whole.shape[1], LANE):
        refs[-1][cols, :] = (middle_ref[cols, :] + jnp.transpose(whole[:, cols])).astype(BF16)


def call(kernel, outs, scratch, operands, hbm=0, limit=16, micros=1.0, last=False):
    spaces = [pltpu.HBM if k < hbm else pltpu.VMEM for k in range(len(operands))]
    operands = [pltpu.with_memory_space_constraint(a, space) for a, space in zip(operands, spaces)]
    out_kind = jax.ShapeDtypeStruct if last else pltpu.VMEM
    return pl.pallas_call(
        kernel,
        out_shape=tuple(out_kind(shape, dtype) for shape, dtype in outs),
        in_specs=[pl.BlockSpec(memory_space=space) for space in spaces],
        out_specs=tuple(pl.BlockSpec(memory_space=pltpu.VMEM) for _ in outs),
        scratch_shapes=scratch,
        compiler_params=pltpu.CompilerParams(vmem_limit_bytes=limit * 1024 * 1024),
        cost_estimate=pl.CostEstimate(
            flops=int(micros * 1.15e9), bytes_accessed=int(micros * 3.6e6), transcendentals=0
        ),
    )(*operands)


def shifted(block, axis, distance):
    size = lax.axis_size(axis)
    return lax.ppermute(block, axis, [(i, (i + distance) % size) for i in range(size)])


def passed_up(block, axis, distance):
    size = lax.axis_size(axis)
    return lax.ppermute(block, axis, [(i, i + distance) for i in range(size - distance)])


def swapped(block, axis, mask):
    return lax.ppermute(block, axis, [(i, i ^ mask) for i in range(lax.axis_size(axis))])


def shards(
    hidden_in,
    mamba_in,
    conv_weight,
    conv_bias,
    x_proj,
    dt_proj,
    dt_bias,
    decay_rate,
    skip_gain,
    out_proj,
    norm_gain,
    mlp_gate,
    mlp_up,
    mlp_down,
    cache_state,
    cache_edge,
    req_lengths,
    cont_flag,
    cache_source,
    owner_slot,
):
    x = mamba_in[0]
    row_count, inner = x.shape
    width = hidden_in.shape[2]
    lags = cache_edge.shape[2]
    peers = lax.axis_size("seq")
    tiles = inner // LANE
    scalars = (req_lengths, cont_flag, cache_source, owner_slot)
    request_count = req_lengths.shape[1]
    chips = peers // 2
    dma = pltpu.SemaphoreType.DMA
    (offer,) = call(
        offer_kernel,
        [((OFFER, inner), BF16)],
        [
            pltpu.VMEM((STATE, inner), F32),
            pltpu.VMEM((lags, inner), BF16),
            pltpu.VMEM((STATE, inner), BF16),
            dma((3,)),
        ],
        (cache_state[0, 0], cache_edge[0, 0], x),
        hbm=3,
        limit=4,
    )
    offers = [offer] + [shifted(offer, "seq", 2 * k) for k in range(1, chips)]
    bias, dt_bias, rate, skip = [
        v.reshape(tiles, LANE) for v in (conv_bias, dt_bias, decay_rate, skip_gain)
    ]
    groups, extra = sum_layout(tiles)
    ext_shape = (STATE, inner + extra)
    scalar_s = pltpu.SMEM((1, request_count), jnp.int32)
    vec_s = pltpu.VMEM((tiles, LANE), F32)
    rank = x_proj.shape[1]
    full = ((row_count, inner), F32)
    bundle_shape = ((chips + 1, *ext_shape), BF16)
    wide = ((STATE, row_count, LANE), F32)
    blocks = len(lane_blocks(inner, SIDE))
    conv, rows, taps, dt_bias_v, rate_v, skip_v, x_proj_v, dt_proj_v, weight = call(
        conv_kernel,
        [
            full,
            ((8 + row_count, inner), F32),
            (conv_weight.shape, F32),
            ((tiles, LANE), F32),
            ((tiles, LANE), F32),
            ((tiles, LANE), F32),
            ((rank, inner), BF16),
            (dt_proj.shape, BF16),
            ((width, inner), BF16),
        ],
        [scalar_s, pltpu.VMEM((row_count, inner), BF16), vec_s, dma((9 + blocks,))],
        (
            req_lengths, x, conv_weight, bias, dt_bias, rate, skip, x_proj.T, dt_proj, out_proj.T,
        ),
        hbm=10,
        limit=8,
    )
    offers, conv = lax.optimization_barrier((offers, conv))
    (edge_mine,) = call(
        edges_kernel, [((chips, OFFER - STATE, inner), BF16)], [], tuple(offers), limit=4
    )
    edge_other = swapped(edge_mine, "seq", 1)
    step, jump, push, base, decay, b_wide, c_wide, coefs, slot_edge, bundle = call(
        functools.partial(terms_kernel, lags, chips),
        [full, full, full, full, full, wide, wide, ((row_count, 2 * STATE), F32),
         ((peers, lags, inner), F32), bundle_shape],
        [
            scalar_s, scalar_s, scalar_s, scalar_s,
            pltpu.VMEM((row_count, inner), BF16),
            pltpu.VMEM((row_count, inner), F32),
            pltpu.VMEM((8, inner), F32),
            pltpu.VMEM((8, inner), F32),
            pltpu.VMEM((groups * STATE, LANE), F32),
            dma((4,)),
        ],
        (
            *scalars, conv, rows, taps, dt_bias_v, rate_v, skip_v, x_proj_v, dt_proj_v,
            edge_mine, edge_other, *offers,
        ),
        hbm=4,
        limit=10,
    )
    other = swapped(bundle, "seq", 1)
    b_rows, c_rows, q = call(
        spread_kernel,
        [((row_count, STATE, LANE), F32), ((row_count, STATE, LANE), F32), full],
        [scalar_s, dma((1,))],
        (req_lengths, rate_v, step, coefs),
        hbm=1,
        limit=6,
    )
    other, b_rows, c_rows, q = lax.optimization_barrier((other, b_rows, c_rows, q))
    span_call = functools.partial(
        call, outs=[(ext_shape, BF16)], scratch=[scalar_s, dma((1,))], hbm=1, limit=4
    )
    (span,) = span_call(
        functools.partial(pair_kernel, row_count), operands=(req_lengths, rate_v, bundle, other)
    )

    def scan_call(first_side, sides, fetch):
        return call(
            functools.partial(scan_kernel, first_side, sides, len(fetch)),
            [((row_count, sides * SIDE), F32)] + [(w.shape, BF16) for w in fetch],
            [dma((len(fetch),))],
            (*fetch, rate_v, jump, push, base, b_rows, c_rows),
            hbm=len(fetch),
            limit=4,
        )

    all_sides = inner // SIDE
    early = (2 * all_sides) // 5
    y_first, gate = scan_call(0, early, (mlp_gate,))
    stages = [passed_up(span, "seq", 2)]
    first_stage, y_first, gate = lax.optimization_barrier((stages[0], y_first, gate))
    stages = [first_stage]
    reach = 2
    while reach < chips:
        (span,) = span_call(
            functools.partial(span_kernel, row_count, reach // 2),
            operands=(req_lengths, rate_v, span, stages[-1]),
        )
        stages.append(passed_up(span, "seq", 2 * reach))
        reach = 2 * reach
    y_rest, up, down = scan_call(early, all_sides - early, (mlp_up, mlp_down.T))
    middle, normed, begins = call(
        functools.partial(close_kernel, len(stages)),
        [
            ((width, row_count), F32),
            ((row_count, width), BF16),
            ((request_count, STATE, inner), F32),
        ],
        [
            scalar_s, scalar_s, scalar_s,
            vec_s,
            pltpu.VMEM((width, row_count), BF16),
            pltpu.VMEM((row_count, inner), F32),
            dma((5,)),
        ],
        (
            *scalars[:3], rate, hidden_in[0].T, *stages, bundle, other, c_wide, y_first, y_rest, q,
            norm_gain.reshape(1, width), weight,
        ),
        hbm=5,
        limit=12,
        micros=6,
    )
    weights = (gate, up, down)
    tokens_out = ((row_count, width), BF16)
    from_x, from_y = swapped(normed, "req", 1), swapped(normed, "req", 2)
    (own,) = call(
        own_kernel, [((row_count, width), F32)], [], (normed, *weights), limit=4, micros=3
    )
    edge_groups = -(-lags * tiles // STATE)
    packed = ((chips, STATE, inner + edge_groups * LANE), BF16)
    keep, send = call(
        final_kernel,
        [packed, packed],
        [
            scalar_s, scalar_s, vec_s,
            pltpu.VMEM((STATE, inner), F32),
            pltpu.VMEM((edge_groups * STATE, LANE), F32),
            dma((3,)),
        ],
        (req_lengths, owner_slot, rate, step, push, decay, b_wide, begins, slot_edge),
        hbm=3,
        limit=4,
        micros=4,
    )
    from_x, from_y, send = lax.optimization_barrier((from_x, from_y, send))
    got = swapped(send, "seq", 1)
    half = row_count // 2
    far_high = swapped(from_x[half:], "req", 2)
    far_low = swapped(from_y[:half], "req", 1)
    at_x, at_y = call(
        peer_kernel, [tokens_out] * 2, [], (from_x, from_y, *weights), limit=6, micros=4.5
    )
    got = lax.optimization_barrier((got, at_x))[0]
    parts = [keep[k] + got[k] for k in range(chips)]
    far_low, far_high, parts = lax.optimization_barrier((far_low, far_high, parts))
    back_x, back_y = swapped(at_x, "req", 1), swapped(at_y, "req", 2)
    (at_far,) = call(far_kernel, [tokens_out], [], (far_low, far_high, *weights), limit=4, micros=3)
    back_far = swapped(at_far, "req", 3)
    parts = [parts[0]] + [shifted(parts[k], "seq", 2 * k) for k in range(1, chips)]
    new_state, new_edge = call(
        functools.partial(unpack_kernel, lags),
        [((STATE, inner), F32), ((lags, inner), BF16)],
        [pltpu.VMEM((edge_groups * STATE, LANE), F32)],
        tuple(parts),
        limit=4,
        last=True,
    )
    (block_rows,) = call(
        join_kernel, [((width, row_count), BF16)], [], (middle, own, back_x, back_y, back_far), limit=4,
        last=True,
    )
    return (block_rows.T[None], new_state[None, None], new_edge[None, None])


def solution(mesh):
    return jax.shard_map(
        shards,
        mesh=mesh,
        in_specs=(
            P("req", "seq", None),
            P("req", "seq", None),
            P(),
            P(),
            P(),
            P(),
            P(),
            P(),
            P(),
            P(),
            P(),
            P(None, "req"),
            P(None, "req"),
            P("req", None),
            P("req", "seq", None, None),
            P("req", "seq", None, None),
            P("req", None),
            P("req", None),
            P("req", None),
            P("req", None),
        ),
        out_specs=(P("req", "seq", None), P("req", "seq", None, None), P("req", "seq", None, None)),
        check_vma=False,
    )
```

```python
import functools

import jax
import jax.numpy as jnp
from jax import lax
from jax.experimental import pallas as pl
from jax.experimental.pallas import tpu as pltpu
from jax.sharding import PartitionSpec as P

STATE = 16
NORM_EPS = 1e-06
LANE = 128
FAR = 1e30
OFFER = 24
LOG2E = 1.4426950408889634
F32 = jnp.float32
BF16 = jnp.bfloat16


def request_marks(lens_ref, first_pos):
    marks = []
    begin = -first_pos
    for r in range(lens_ref.shape[1]):
        end = begin + lens_ref[0, r]
        marks.append((begin, end))
        begin = end
    return marks


def segment_of(index, marks):
    total = jnp.zeros(index.shape, jnp.int32)
    for begin, _ in marks:
        total = total + (index >= begin).astype(jnp.int32)
    return total


def segment_masks(row_count, marks):
    row = lax.broadcasted_iota(jnp.int32, (row_count, row_count), 0)
    col = lax.broadcasted_iota(jnp.int32, (row_count, row_count), 1)
    same = segment_of(row, marks) == segment_of(col, marks)
    return row, col, same


def three_parts(values):
    high = values.astype(BF16)
    rest = values - high.astype(F32)
    middle = rest.astype(BF16)
    low = (rest - middle.astype(F32)).astype(BF16)
    return jnp.concatenate([high, middle, low], axis=0)


def tripled(mask):
    one = mask.astype(F32).astype(BF16)
    return jnp.concatenate([one, one, one], axis=1)


def rate_block(rate_row):
    power = lax.broadcasted_iota(jnp.int32, (STATE, rate_row.shape[1]), 0) + 1
    return power.astype(F32) * rate_row


def row_of(vec_ref, tile):
    return vec_ref[pl.ds(tile, 1), :]


def wide_row(vec_ref, first, count):
    return jnp.concatenate([vec_ref[first + k : first + k + 1, :] for k in range(count)], axis=1)


def sums_of_eight(parts):
    sub = lax.broadcasted_iota(jnp.int32, parts[0].shape, 0)
    stride = 1
    while len(parts) > 1:
        first = jnp.bitwise_and(sub, stride) == 0
        parts = [
            jnp.where(first, a, b) + pltpu.roll(jnp.where(first, b, a), stride, 0)
            for a, b in zip(parts[0::2], parts[1::2])
        ]
        stride = 2 * stride
    return parts[0]


def softplus(v):
    return jnp.maximum(v, 0.0) + jnp.log1p(jnp.exp(-jnp.abs(v)))


def sum_layout(tiles):
    groups = -(-tiles // STATE)
    return groups, 2 * groups * LANE


def read_sum(ext_ref, tile, inner):
    groups, _ = sum_layout(inner // LANE)
    group, row = divmod(tile, STATE)
    high = inner + group * LANE
    low = high + groups * LANE
    return ext_ref[row : row + 1, high : high + LANE].astype(F32) + ext_ref[
        row : row + 1, low : low + LANE
    ].astype(F32)


def write_sums(ext_ref, sums, inner):
    groups, _ = sum_layout(inner // LANE)
    for group in range(groups):
        part = sums[group * STATE : (group + 1) * STATE, :]
        high = part.astype(BF16)
        low = (part - high.astype(F32)).astype(BF16)
        at = inner + group * LANE
        ext_ref[:, at : at + LANE] = high
        ext_ref[:, at + groups * LANE : at + (groups + 1) * LANE] = low


NT = (((1,), (1,)), ((), ()))
SIDE = 5 * LANE


def start_all(pairs, sems):
    copies = [pltpu.make_async_copy(src, dst, sems.at[k]) for k, (src, dst) in enumerate(pairs)]
    for copy in copies:
        copy.start()
    return copies


def lane_blocks(size, width):
    return [slice(at, min(at + width, size)) for at in range(0, size, width)]


def offer_kernel(state_hbm, edge_hbm, x_hbm, out_ref, state_s, edge_s, tail_s, sems):
    rows = tail_s.shape[0]
    last = x_hbm.at[pl.ds(x_hbm.shape[0] - rows, rows)]
    for copy in start_all([(state_hbm, state_s), (edge_hbm, edge_s), (last, tail_s)], sems):
        copy.wait()
    lags = edge_s.shape[0]
    tail = tail_s[...].astype(F32)[rows - lags :]
    spare = jnp.zeros((OFFER - STATE - 2 * lags, tail.shape[1]), F32)
    whole = jnp.concatenate([state_s[...], edge_s[...].astype(F32), tail, spare], axis=0)
    out_ref[...] = whole.astype(BF16)


def edges_kernel(*refs):
    for k, ref in enumerate(refs[:-1]):
        refs[-1][k] = ref[...].astype(F32)[STATE:].astype(BF16)


def conv_kernel(
    lens_hbm, x_hbm, taps_hbm, bias_hbm, dt_bias_hbm, rate_hbm, skip_hbm, x_proj_hbm, dt_proj_hbm,
    out_proj_hbm, hidden_hbm, conv_ref, rows_ref, taps_ref, dt_bias_ref, rate_ref, skip_ref,
    x_proj_ref, dt_proj_ref, weight_ref, hidden_ref, lens_ref, x_s, bias_s, sems,
):
    row_count, inner = x_s.shape
    lags = taps_ref.shape[0] - 1
    blocks = lane_blocks(inner, SIDE)
    pairs = [(lens_hbm, lens_ref), (taps_hbm, taps_ref), (bias_hbm, bias_s)]
    pairs += [(x_hbm.at[:, cols], x_s.at[:, cols]) for cols in blocks]
    pairs += [
        (dt_bias_hbm, dt_bias_ref), (rate_hbm, rate_ref), (skip_hbm, skip_ref),
        (x_proj_hbm, x_proj_ref), (dt_proj_hbm, dt_proj_ref), (out_proj_hbm, weight_ref),
        (hidden_hbm, hidden_ref),
    ]
    copies = start_all(pairs, sems)
    for copy in copies[:3]:
        copy.wait()
    marks = request_marks(lens_ref, lax.axis_index("seq") * row_count)
    row = lax.broadcasted_iota(jnp.int32, (row_count, 1), 0)
    near = []
    for lag in range(1, lags + 1):
        hit = jnp.zeros((row_count, 1), jnp.int32)
        for begin, _ in marks:
            hit = hit + jnp.logical_and(row >= begin, row < begin + lag).astype(jnp.int32)
        near.append((hit == 0).astype(F32))
    rows_ref[0:8, :] = jnp.zeros((8, inner), F32)
    for k, cols in enumerate(blocks):
        copies[3 + k].wait()
        here = x_s[:, cols].astype(F32)
        rows_ref[8 : 8 + row_count, cols] = here
        total = wide_row(bias_s, k * (SIDE // LANE), SIDE // LANE) + taps_ref[
            lags : lags + 1, cols
        ] * here
        for lag in range(1, lags + 1):
            back = rows_ref[8 - lag : 8 - lag + row_count, cols]
            total = total + taps_ref[lags - lag : lags - lag + 1, cols] * (near[lag - 1] * back)
        conv_ref[:, cols] = total
    for copy in copies[3 + len(blocks) :]:
        copy.wait()


def terms_kernel(lags, seed_count, *refs):
    scalar_hbm = refs[:4]
    (conv_ref, rows_ref, taps_ref, dt_bias_s, rate_s, skip_s, x_proj_ref, dt_proj_ref,
     edge_mine_ref, edge_other_ref) = refs[4:14]
    seed_refs = refs[14 : 14 + seed_count]
    refs = refs[14 + seed_count :]
    (step_ref, jump_ref, push_ref, base_ref, decay_ref, b_s, c_s, coef_ref, slot_edge_ref,
     bundle_ref, whole_ref) = refs[:11]
    scalars = refs[11:15]
    mixed_s, conv_s, edge_s, tail_s, sums_s, sems = refs[15:]
    ext_ref = bundle_ref.at[0]
    lens_ref, cont_ref, source_ref, owner_ref = scalars
    row_count, inner = conv_s.shape
    request_count = lens_ref.shape[1]
    chips = edge_mine_ref.shape[0]
    blocks = lane_blocks(inner, SIDE)
    side = SIDE // LANE
    copies = start_all(list(zip(scalar_hbm, scalars)), sems)
    me = lax.axis_index("seq")
    core = lax.rem(me, 2)
    row = lax.broadcasted_iota(jnp.int32, (row_count, 1), 0)
    for cols in blocks:
        conv_s[:, cols] = conv_ref[:, cols]
    for k, ref in enumerate(seed_refs):
        bundle_ref[1 + k, :, 0:inner] = ref[...].astype(F32)[:STATE].astype(BF16)
    tail_s[0:lags, :] = edge_other_ref[1 - core].astype(F32)[lags : 2 * lags, :]
    slot_edge_ref[...] = jnp.zeros(slot_edge_ref.shape, F32)
    for copy in copies:
        copy.wait()
    marks = request_marks(lens_ref, me * row_count)
    for p in range(lags):
        extra = jnp.zeros((1, inner), F32)
        for lag in range(p + 1, lags + 1):
            near = jnp.float32(1.0)
            for begin, _ in marks:
                near = jnp.where(jnp.logical_and(begin <= p, begin > p - lag), 0.0, near)
            extra = extra + taps_ref[lags - lag : lags - lag + 1, :] * (
                near * tail_s[lags + p - lag : lags + p - lag + 1, :]
            )
        conv_s[p : p + 1, :] = conv_s[p : p + 1, :] + extra
    for r in range(request_count):
        begin, end = marks[r]
        length = lens_ref[0, r]

        @pl.when(jnp.logical_and(begin > -lags, begin < row_count))
        def _(r=r, begin=begin, end=end, length=length):
            keep = cont_ref[0, r].astype(F32)
            source = source_ref[0, r]
            away = lax.rem(me // 2 - source // 2 + chips, chips)
            for ref, parity in ((edge_mine_ref, core), (edge_other_ref, 1 - core)):
                @pl.when(lax.rem(source, 2) == parity)
                def _(ref=ref):
                    edge_s[0:lags, :] = keep * ref[away].astype(F32)[0:lags, :]

            for p in range(lags):
                at = begin + p

                @pl.when(jnp.logical_and(jnp.logical_and(at >= 0, at < row_count), p < length))
                def _():
                    extra = jnp.zeros((1, inner), F32)
                    for lag in range(p + 1, lags + 1):
                        extra = extra + taps_ref[lags - lag : lags - lag + 1, :] * edge_s[
                            lags + p - lag : lags + p - lag + 1, :
                        ]
                    conv_s[pl.ds(at, 1), :] = conv_s[pl.ds(at, 1), :] + extra

        @pl.when(jnp.logical_and(end > 0, end <= row_count))
        def _(r=r, end=end, length=length):
            owner = owner_ref[0, r]
            for lag in range(lags):
                at = end - 1 - lag

                @pl.when(jnp.logical_and(length > lag, at >= 0))
                def _():
                    slot_edge_ref[owner, lags - 1 - lag : lags - lag, :] = rows_ref[
                        pl.ds(8 + at, 1), :
                    ]

                @pl.when(jnp.logical_and(length > lag, at < 0))
                def _():
                    slot_edge_ref[owner, lags - 1 - lag : lags - lag, :] = tail_s[
                        pl.ds(lags + at, 1), :
                    ]

                @pl.when(length <= lag)
                def _():
                    slot_edge_ref[owner, lags - 1 - lag : lags - lag, :] = edge_s[
                        pl.ds(lags + length - 1 - lag, 1), :
                    ]

    for k, cols in enumerate(blocks):
        v = conv_s[:, cols]
        mixed = (v / (1.0 + jnp.exp(-v))).astype(BF16)
        mixed_s[:, cols] = mixed
        base_ref[:, cols] = wide_row(skip_s, k * side, side) * mixed.astype(F32)
    projected = lax.dot_general(mixed_s[...], x_proj_ref[...], NT, preferred_element_type=F32)
    rank = dt_proj_ref.shape[0]
    dt_low = projected[:, :rank].astype(BF16)
    coef_ref[...] = projected[:, rank : rank + 2 * STATE]
    for s in range(STATE):
        at = rank + s
        b_s[s] = jnp.broadcast_to(projected[:, at : at + 1], (row_count, LANE))
        at = rank + STATE + s
        c_s[s] = jnp.broadcast_to(projected[:, at : at + 1], (row_count, LANE))
    last_begin = jnp.int32(0)
    jump = jnp.zeros((row_count, 1), F32)
    for begin, _ in marks:
        last_begin = jnp.where(
            jnp.logical_and(begin >= 0, begin < row_count), jnp.maximum(last_begin, begin), last_begin
        )
        jump = jump + (row == begin).astype(F32) * FAR
    in_last = (row >= last_begin).astype(F32)
    second = (1 - core) * row_count
    flags = [unbroken(marks, second, second + row_count)]
    stop = second + row_count
    for k in range(1, whole_ref.shape[0]):
        flags.append(unbroken(marks, stop - (row_count << k), stop))
    for k, flag in enumerate(flags):
        whole_ref[k : k + 1, :] = jnp.zeros((1, LANE), F32) + flag
    m_row, m_col, same = segment_masks(row_count, marks)
    later = tripled(jnp.logical_and(m_col > m_row, same))
    for k, cols in enumerate(blocks):
        step = softplus(
            jnp.dot(dt_low, dt_proj_ref[:, cols], preferred_element_type=F32)
            + wide_row(dt_bias_s, k * side, side)
        )
        step_ref[:, cols] = step
        jump_ref[:, cols] = step + jump
        push_ref[:, cols] = step * mixed_s[:, cols].astype(F32)
    for k, cols in enumerate(blocks):
        suffix = jnp.dot(later, three_parts(step_ref[:, cols]), preferred_element_type=F32)
        decay_ref[:, cols] = jnp.exp(-wide_row(rate_s, k * side, side) * suffix)

    def tile_step(i, carry):
        at = pl.multiple_of(i * LANE, LANE)
        cols = pl.ds(at, LANE)
        ext_ref[:, cols] = weighted_sum(
            push_ref[:, cols] * in_last, decay_ref[:, cols], b_s
        ).astype(BF16)
        sums_s[pl.ds(i, 1), :] = jnp.sum(step_ref[:, cols] * in_last, axis=0, keepdims=True)
        return carry

    sums_s[...] = jnp.zeros(sums_s.shape, F32)
    lax.fori_loop(0, inner // LANE, tile_step, 0, unroll=5)
    write_sums(ext_ref, sums_s[...], inner)


def weighted_sum(push, decay, b_ref):
    weight = push * decay
    totals = []
    for s in range(STATE):
        product = weight * b_ref[s]
        total = product[0:8, :]
        for k in range(8, push.shape[0], 8):
            total = total + product[k : k + 8, :]
        totals.append(total)
        if s + 1 < STATE:
            weight = weight * decay
    return jnp.concatenate(
        [sums_of_eight(totals[k : k + 8]) for k in range(0, STATE, 8)], axis=0
    )


def link_spans(earlier_of, later_of, whole, rate_ref, out_ref):
    tiles = rate_ref.shape[0]
    inner = tiles * LANE
    sums = []
    for i in range(tiles):
        cols = slice(i * LANE, (i + 1) * LANE)
        e0, s0 = earlier_of(cols, i, inner)
        e1, s1 = later_of(cols, i, inner)
        rate = rate_block(rate_ref[i : i + 1, :])
        out_ref[:, cols] = (e1 + whole * jnp.exp(-rate * s1) * e0).astype(BF16)
        sums.append(s1 + whole * s0)
    groups, _ = sum_layout(tiles)
    sums.append(jnp.zeros((groups * STATE - len(sums), LANE), F32))
    write_sums(out_ref, jnp.concatenate(sums, axis=0), inner)


def unbroken(marks, first, stop):
    whole = jnp.float32(1.0)
    for begin, _ in marks:
        whole = jnp.where(jnp.logical_and(begin >= first, begin < stop), 0.0, whole)
    return whole


def reader(ref):
    return lambda cols, i, inner: (ref[:, cols].astype(F32), read_sum(ref, i, inner))


def pair_kernel(rate_ref, whole_ref, mine_ref, other_ref, out_ref):
    core = lax.rem(lax.axis_index("seq"), 2)
    mine, other = reader(mine_ref.at[0]), reader(other_ref.at[0])

    def choose(number):
        def read(*where):
            return [jnp.where(core == number, a, b) for a, b in zip(mine(*where), other(*where))]

        return read

    link_spans(choose(0), choose(1), whole_ref[0:1, :], rate_ref, out_ref)


def span_kernel(power, rate_ref, whole_ref, mine_ref, before_ref, out_ref):
    whole = whole_ref[power : power + 1, :]
    link_spans(reader(before_ref), reader(mine_ref), whole, rate_ref, out_ref)


def spread_kernel(lens_hbm, rate_s, step_ref, coef_ref, b_ref, c_ref, q_ref, lens_ref, sems):
    row_count, inner = step_ref.shape
    copies = start_all([(lens_hbm, lens_ref)], sems)
    spare = jnp.zeros((row_count, LANE - 2 * STATE), F32)
    flipped = jnp.transpose(jnp.concatenate([coef_ref[...], spare], axis=1))
    for t in range(row_count):
        b_ref[t] = jnp.broadcast_to(flipped[0:STATE, t : t + 1], (STATE, LANE))
        c_ref[t] = jnp.broadcast_to(flipped[STATE : 2 * STATE, t : t + 1], (STATE, LANE))
    copies[0].wait()
    marks = request_marks(lens_ref, lax.axis_index("seq") * row_count)
    m_row, m_col, same = segment_masks(row_count, marks)
    earlier = tripled(jnp.logical_and(m_col <= m_row, same))
    side = SIDE // LANE
    for k, cols in enumerate(lane_blocks(inner, SIDE)):
        prefix = jnp.dot(earlier, three_parts(step_ref[:, cols]), preferred_element_type=F32)
        q_ref[:, cols] = jnp.exp(-wide_row(rate_s, k * side, side) * prefix)


def scan_kernel(first_side, sides, fetched, *refs):
    fetch_hbm = refs[:fetched]
    rate_s, jump_ref, push_ref, base_ref, b_s, c_s, y_ref = refs[fetched : fetched + 7]
    copies = start_all(list(zip(fetch_hbm, refs[fetched + 7 :])), refs[-1])
    row_count = jump_ref.shape[0]
    tiles = SIDE // LANE
    width = SIDE

    def chunk_step(i, carry):
        at = pl.multiple_of((first_side + i) * width, LANE)
        rates = [-LOG2E * rate_block(row_of(rate_s, (first_side + i) * tiles + k)) for k in range(tiles)]

        def row_step(j, held):
            first = pl.multiple_of(j * 8, 8)
            rows = pl.ds(first, 8)
            held = list(held)
            for k in range(tiles):
                lanes = pl.ds(pl.multiple_of(at + k * LANE, LANE), LANE)
                jumps, pushes = jump_ref.at[rows, lanes], push_ref.at[rows, lanes]
                h = held[k]
                outs = []
                for t in range(8):
                    decay = jnp.exp2(rates[k] * jumps[t : t + 1, :])
                    h = decay * h + b_s[first + t] * pushes[t : t + 1, :]
                    product = c_s[first + t] * h
                    outs.append(product[0:8] + product[8:16])
                held[k] = h
                out_lanes = pl.ds(pl.multiple_of(i * width + k * LANE, LANE), LANE)
                y_ref[rows, out_lanes] = base_ref[rows, lanes] + sums_of_eight(outs)
            return tuple(held)

        lax.fori_loop(
            0, row_count // 8, row_step, tuple(jnp.zeros((STATE, LANE), F32) for _ in range(tiles)),
            unroll=2,
        )
        return carry

    lax.fori_loop(0, sides, chunk_step, 0)
    for copy in copies:
        copy.wait()


def close_kernel(stage_count, *refs):
    scalar_hbm = refs[:3]
    rate_s, hidden_s = refs[3:5]
    stage_refs = refs[5 : 5 + stage_count]
    (mine_ref, other_ref, c_s, y_first_ref, y_rest_ref, q_ref, gain_ref, weight_ref) = refs[
        5 + stage_count : 13 + stage_count
    ]
    middle_ref, normed_ref, begins_ref = refs[13 + stage_count : 16 + stage_count]
    scalars = refs[16 + stage_count : 19 + stage_count]
    ssm_s, sems = refs[19 + stage_count :]
    pair_ref = other_ref.at[0]
    lens_ref, cont_ref, source_ref = scalars
    row_count, inner = q_ref.shape
    width = middle_ref.shape[0]
    chips = mine_ref.shape[0] - 1
    copies = start_all(list(zip(scalar_hbm, scalars)), sems)
    me = lax.axis_index("seq")
    core = lax.rem(me, 2)
    parting = y_first_ref.shape[1]
    ssm_s[:, 0:parting] = y_first_ref[...]
    ssm_s[:, parting:inner] = y_rest_ref[...]
    for copy in copies:
        copy.wait()
    marks = request_marks(lens_ref, me * row_count)
    tiles = 5
    side = tiles * LANE
    block = 32
    for r in range(lens_ref.shape[1]):
        begin, end = marks[r]
        low, high = jnp.maximum(begin, 0), jnp.minimum(end, row_count)

        @pl.when(high > low)
        def _(r=r, begin=begin, low=low, high=high):
            keep = cont_ref[0, r].astype(F32)
            source = source_ref[0, r]
            away = lax.rem(me // 2 - source // 2 + chips, chips)
            for ref, parity in ((mine_ref, core), (other_ref, 1 - core)):
                @pl.when(lax.rem(source, 2) == parity)
                def _(ref=ref):
                    begins_ref[r] = keep * ref[1 + away, :, 0:inner].astype(F32)

            for k in range(stage_count + 1):
                if k < stage_count:
                    away = 1 << (stage_count - 1 - k)
                    chip_first = me - core - 2 * away
                    ref = stage_refs[stage_count - 1 - k]
                    stage_end = -(core + 2 * (away - 1)) * row_count
                    valid = jnp.logical_and(chip_first >= 0, begin < stage_end)
                else:
                    ref = pair_ref
                    valid = jnp.logical_and(core == 1, begin < 0)

                @pl.when(valid)
                def _(ref=ref):
                    for i in range(inner // LANE):
                        cols = slice(i * LANE, (i + 1) * LANE)
                        decay = jnp.exp(-rate_block(rate_s[i : i + 1, :]) * read_sum(ref, i, inner))
                        begins_ref[r, :, cols] = (
                            ref[:, cols].astype(F32) + decay * begins_ref[r, :, cols]
                        )

            def block_step(j, carry):
                first = pl.multiple_of(j * block, block)
                rows = pl.ds(first, block)
                at_row = lax.broadcasted_iota(jnp.int32, (block, 1), 0) + first
                inside = jnp.logical_and(at_row >= low, at_row < high)

                def lane_step(i, inner_carry):
                    at = pl.multiple_of(i * side, LANE)
                    cols = pl.ds(at, side)
                    q = q_ref[rows, cols]
                    total = jnp.zeros((block, side), F32)
                    for s in range(STATE - 1, -1, -1):
                        c = c_s[s, rows, :]
                        c = jnp.concatenate([c] * tiles, axis=1)
                        total = (total + c * begins_ref[r, s : s + 1, cols]) * q
                    ssm_s[rows, cols] = ssm_s[rows, cols] + jnp.where(inside, total, 0.0)
                    return inner_carry

                lax.fori_loop(0, inner // side, lane_step, 0, unroll=True)
                return carry

            lax.fori_loop(low // block, (high + block - 1) // block, block_step, 0)

    total = hidden_s[...].astype(F32) + lax.dot_general(
        weight_ref[...], ssm_s[...].astype(BF16), NT, preferred_element_type=F32
    )
    middle_ref[...] = total
    total = total * lax.rsqrt(jnp.mean(total * total, axis=0, keepdims=True) + NORM_EPS)
    for cols in lane_blocks(width, LANE):
        normed_ref[:, cols] = (jnp.transpose(total[cols, :]) * gain_ref[:, cols]).astype(BF16)


def final_kernel(
    lens_hbm, owner_hbm, rate_s, step_ref, push_ref, decay_ref, b_ref, begins_ref,
    slot_edge_ref, keep_ref, send_ref, lens_ref, owner_ref, held_s, edge_s, sems,
):
    pairs = [(lens_hbm, lens_ref), (owner_hbm, owner_ref)]
    for copy in start_all(pairs, sems):
        copy.wait()
    row_count, inner = step_ref.shape
    block = 32
    me = lax.axis_index("seq")
    core = lax.rem(me, 2)
    chips = keep_ref.shape[0]
    marks = request_marks(lens_ref, me * row_count)
    lags = slot_edge_ref.shape[1]
    row = lax.broadcasted_iota(jnp.int32, (row_count, 1), 0)
    keep_ref[...] = jnp.zeros(keep_ref.shape, BF16)
    send_ref[...] = jnp.zeros(send_ref.shape, BF16)
    tiles = inner // LANE
    edge_groups = (keep_ref.shape[2] - inner) // LANE
    for r in range(lens_ref.shape[1]):
        begin, end = marks[r]

        @pl.when(jnp.logical_and(end > 0, end <= row_count))
        def _(r=r, begin=begin, end=end):
            owner = owner_ref[0, r]
            there = lax.rem(owner // 2 - me // 2 + chips, chips)
            mine = lax.rem(owner, 2) == core
            inside = jnp.logical_and(row >= begin, row < end).astype(F32)
            def put(cols, block):
                @pl.when(mine)
                def _():
                    keep_ref[there, :, cols] = block

                @pl.when(jnp.logical_not(mine))
                def _():
                    send_ref[there, :, cols] = block

            held_s[...] = jnp.zeros(held_s.shape, F32)

            def block_step(j, carry):
                first = pl.multiple_of(j * block, block)
                rows = pl.ds(first, block)
                at_row = lax.broadcasted_iota(jnp.int32, (block, 1), 0) + first
                here = jnp.logical_and(at_row >= begin, at_row < end).astype(F32)

                def add_tile(i, inner_carry):
                    cols = pl.ds(pl.multiple_of(i * LANE, LANE), LANE)
                    held_s[:, cols] = held_s[:, cols] + weighted_sum(
                        push_ref[rows, cols] * here, decay_ref[rows, cols], b_ref.at[:, rows, :]
                    )
                    return inner_carry

                lax.fori_loop(0, tiles, add_tile, 0, unroll=5)
                return carry

            lax.fori_loop(
                jnp.maximum(begin, 0) // block, (end + block - 1) // block, block_step, 0
            )

            def tile_step(i, carry):
                cols = pl.ds(pl.multiple_of(i * LANE, LANE), LANE)
                span = jnp.sum(step_ref[:, cols] * inside, axis=0, keepdims=True)
                carried = jnp.exp(-rate_block(row_of(rate_s, i)) * span) * begins_ref[r, :, cols]
                put(cols, (held_s[:, cols] + carried).astype(BF16))
                return carry

            lax.fori_loop(0, tiles, tile_step, 0)
            edge_s[...] = jnp.zeros(edge_s.shape, F32)
            for lag in range(lags):
                for i in range(tiles):
                    at = lag * tiles + i
                    edge_s[at : at + 1, :] = slot_edge_ref[
                        owner, lag : lag + 1, i * LANE : (i + 1) * LANE
                    ]
            for g in range(edge_groups):
                put(
                    slice(inner + g * LANE, inner + (g + 1) * LANE),
                    edge_s[g * STATE : (g + 1) * STATE, :].astype(BF16),
                )


def unpack_kernel(lags, *refs):
    got_refs, (state_ref, edge_ref, edge_s) = refs[:-3], refs[-3:]
    inner = state_ref.shape[1]
    tiles = inner // LANE

    def whole(cols):
        total = got_refs[0][:, cols].astype(F32)
        for ref in got_refs[1:]:
            total = total + ref[:, cols].astype(F32)
        return total

    state_ref[...] = whole(slice(0, inner))
    groups = (got_refs[0].shape[1] - inner) // LANE
    for g in range(groups):
        edge_s[g * STATE : (g + 1) * STATE, :] = whole(
            slice(inner + g * LANE, inner + (g + 1) * LANE)
        )
    for i in range(tiles):
        edge_ref[:, i * LANE : (i + 1) * LANE] = jnp.concatenate(
            [edge_s[lag * tiles + i : lag * tiles + i + 1, :] for lag in range(lags)], axis=0
        ).astype(BF16)


def feed_forward(tokens, gate_ref, up_ref, down_ref):
    gate = jnp.dot(tokens, gate_ref[...], preferred_element_type=F32)
    up = jnp.dot(tokens, up_ref[...], preferred_element_type=F32)
    hidden = (gate / (1.0 + jnp.exp(-gate)) * up).astype(BF16)
    return lax.dot_general(hidden, down_ref[...], NT, preferred_element_type=F32)


def own_kernel(token_ref, gate_ref, up_ref, down_ref, out_ref):
    out_ref[...] = feed_forward(token_ref[...], gate_ref, up_ref, down_ref)


def peer_kernel(*refs):
    count = (len(refs) - 3) // 2
    tokens = jnp.concatenate([ref[...] for ref in refs[:count]], axis=0)
    out = feed_forward(tokens, *refs[count : count + 3]).astype(BF16)
    part = out.shape[0] // count
    for k, ref in enumerate(refs[count + 3 :]):
        ref[...] = out[k * part : (k + 1) * part]


def far_kernel(low_ref, high_ref, gate_ref, up_ref, down_ref, out_ref):
    tokens = jnp.concatenate([low_ref[...], high_ref[...]], axis=0)
    out_ref[...] = feed_forward(tokens, gate_ref, up_ref, down_ref).astype(BF16)


def join_kernel(middle_ref, own_ref, *refs):
    whole = own_ref[...]
    for ref in refs[:-1]:
        whole = whole + ref[...].astype(F32)
    for cols in lane_blocks(whole.shape[1], LANE):
        refs[-1][cols, :] = (middle_ref[cols, :] + jnp.transpose(whole[:, cols])).astype(BF16)


def call(kernel, outs, scratch, operands, hbm=0, limit=16, micros=1.0, last=False):
    spaces = [pltpu.HBM if k < hbm else pltpu.VMEM for k in range(len(operands))]
    operands = [pltpu.with_memory_space_constraint(a, space) for a, space in zip(operands, spaces)]
    out_kind = jax.ShapeDtypeStruct if last else pltpu.VMEM
    return pl.pallas_call(
        kernel,
        out_shape=tuple(out_kind(shape, dtype) for shape, dtype in outs),
        in_specs=[pl.BlockSpec(memory_space=space) for space in spaces],
        out_specs=tuple(pl.BlockSpec(memory_space=pltpu.VMEM) for _ in outs),
        scratch_shapes=scratch,
        compiler_params=pltpu.CompilerParams(vmem_limit_bytes=limit * 1024 * 1024),
        cost_estimate=pl.CostEstimate(
            flops=int(micros * 1.15e9), bytes_accessed=int(micros * 3.6e6), transcendentals=0
        ),
    )(*operands)


def shifted(block, axis, distance):
    size = lax.axis_size(axis)
    return lax.ppermute(block, axis, [(i, (i + distance) % size) for i in range(size)])


def passed_up(block, axis, distance):
    size = lax.axis_size(axis)
    return lax.ppermute(block, axis, [(i, i + distance) for i in range(size - distance)])


def swapped(block, axis, mask):
    return lax.ppermute(block, axis, [(i, i ^ mask) for i in range(lax.axis_size(axis))])


def shards(
    hidden_in,
    mamba_in,
    conv_weight,
    conv_bias,
    x_proj,
    dt_proj,
    dt_bias,
    decay_rate,
    skip_gain,
    out_proj,
    norm_gain,
    mlp_gate,
    mlp_up,
    mlp_down,
    cache_state,
    cache_edge,
    req_lengths,
    cont_flag,
    cache_source,
    owner_slot,
):
    x = mamba_in[0]
    row_count, inner = x.shape
    width = hidden_in.shape[2]
    lags = cache_edge.shape[2]
    peers = lax.axis_size("seq")
    tiles = inner // LANE
    scalars = (req_lengths, cont_flag, cache_source, owner_slot)
    request_count = req_lengths.shape[1]
    chips = peers // 2
    dma = pltpu.SemaphoreType.DMA
    (offer,) = call(
        offer_kernel,
        [((OFFER, inner), BF16)],
        [
            pltpu.VMEM((STATE, inner), F32),
            pltpu.VMEM((lags, inner), BF16),
            pltpu.VMEM((STATE, inner), BF16),
            dma((3,)),
        ],
        (cache_state[0, 0], cache_edge[0, 0], x),
        hbm=3,
        limit=4,
    )
    offers = [offer] + [shifted(offer, "seq", 2 * k) for k in range(1, chips)]
    bias, dt_bias, rate, skip = [
        v.reshape(tiles, LANE) for v in (conv_bias, dt_bias, decay_rate, skip_gain)
    ]
    groups, extra = sum_layout(tiles)
    ext_shape = (STATE, inner + extra)
    scalar_s = pltpu.SMEM((1, request_count), jnp.int32)
    vec_s = pltpu.VMEM((tiles, LANE), F32)
    rank = x_proj.shape[1]
    full = ((row_count, inner), F32)
    bundle_shape = ((chips + 1, *ext_shape), BF16)
    wide = ((STATE, row_count, LANE), F32)
    blocks = len(lane_blocks(inner, SIDE))
    conv, rows, taps, dt_bias_v, rate_v, skip_v, x_proj_v, dt_proj_v, weight, hidden = call(
        conv_kernel,
        [
            full,
            ((8 + row_count, inner), F32),
            (conv_weight.shape, F32),
            ((tiles, LANE), F32),
            ((tiles, LANE), F32),
            ((tiles, LANE), F32),
            ((rank, inner), BF16),
            (dt_proj.shape, BF16),
            ((width, inner), BF16),
            ((width, row_count), BF16),
        ],
        [scalar_s, pltpu.VMEM((row_count, inner), BF16), vec_s, dma((10 + blocks,))],
        (
            req_lengths, x, conv_weight, bias, dt_bias, rate, skip, x_proj.T, dt_proj, out_proj.T,
            hidden_in[0].T,
        ),
        hbm=11,
        limit=8,
    )
    offers, conv = lax.optimization_barrier((offers, conv))
    (edge_mine,) = call(
        edges_kernel, [((chips, OFFER - STATE, inner), BF16)], [], tuple(offers), limit=4
    )
    edge_other = swapped(edge_mine, "seq", 1)
    step, jump, push, base, decay, b_wide, c_wide, coefs, slot_edge, bundle, whole = call(
        functools.partial(terms_kernel, lags, chips),
        [full, full, full, full, full, wide, wide, ((row_count, 2 * STATE), F32),
         ((peers, lags, inner), F32), bundle_shape, ((chips.bit_length(), LANE), F32)],
        [
            scalar_s, scalar_s, scalar_s, scalar_s,
            pltpu.VMEM((row_count, inner), BF16),
            pltpu.VMEM((row_count, inner), F32),
            pltpu.VMEM((8, inner), F32),
            pltpu.VMEM((8, inner), F32),
            pltpu.VMEM((groups * STATE, LANE), F32),
            dma((4,)),
        ],
        (
            *scalars, conv, rows, taps, dt_bias_v, rate_v, skip_v, x_proj_v, dt_proj_v,
            edge_mine, edge_other, *offers,
        ),
        hbm=4,
        limit=10,
    )
    other = swapped(bundle, "seq", 1)
    b_rows, c_rows, q = call(
        spread_kernel,
        [((row_count, STATE, LANE), F32), ((row_count, STATE, LANE), F32), full],
        [scalar_s, dma((1,))],
        (req_lengths, rate_v, step, coefs),
        hbm=1,
        limit=6,
    )
    other, b_rows, c_rows, q = lax.optimization_barrier((other, b_rows, c_rows, q))
    span_call = functools.partial(
        call, outs=[(ext_shape, BF16)], scratch=[], limit=4
    )
    (span,) = span_call(pair_kernel, operands=(rate_v, whole, bundle, other))

    def scan_call(first_side, sides, fetch):
        return call(
            functools.partial(scan_kernel, first_side, sides, len(fetch)),
            [((row_count, sides * SIDE), F32)] + [(w.shape, BF16) for w in fetch],
            [dma((len(fetch),))],
            (*fetch, rate_v, jump, push, base, b_rows, c_rows),
            hbm=len(fetch),
            limit=4,
        )

    all_sides = inner // SIDE
    early = (2 * all_sides) // 5
    y_first, gate = scan_call(0, early, (mlp_gate,))
    stages = [passed_up(span, "seq", 2)]
    first_stage, y_first, gate = lax.optimization_barrier((stages[0], y_first, gate))
    stages = [first_stage]
    reach = 2
    while reach < chips:
        (span,) = span_call(
            functools.partial(span_kernel, reach.bit_length() - 1),
            operands=(rate_v, whole, span, stages[-1]),
        )
        stages.append(passed_up(span, "seq", 2 * reach))
        reach = 2 * reach
    y_rest, up, down = scan_call(early, all_sides - early, (mlp_up, mlp_down.T))
    middle, normed, begins = call(
        functools.partial(close_kernel, len(stages)),
        [
            ((width, row_count), F32),
            ((row_count, width), BF16),
            ((request_count, STATE, inner), F32),
        ],
        [
            scalar_s, scalar_s, scalar_s,
            pltpu.VMEM((row_count, inner), F32),
            dma((3,)),
        ],
        (
            *scalars[:3], rate_v, hidden, *stages, bundle, other, c_wide, y_first, y_rest, q,
            norm_gain.reshape(1, width), weight,
        ),
        hbm=3,
        limit=14,
        micros=6,
    )
    weights = (gate, up, down)
    tokens_out = ((row_count, width), BF16)
    from_x, from_y = swapped(normed, "req", 1), swapped(normed, "req", 2)
    (own,) = call(
        own_kernel, [((row_count, width), F32)], [], (normed, *weights), limit=4, micros=3
    )
    edge_groups = -(-lags * tiles // STATE)
    packed = ((chips, STATE, inner + edge_groups * LANE), BF16)
    keep, send = call(
        final_kernel,
        [packed, packed],
        [
            scalar_s, scalar_s,
            pltpu.VMEM((STATE, inner), F32),
            pltpu.VMEM((edge_groups * STATE, LANE), F32),
            dma((2,)),
        ],
        (req_lengths, owner_slot, rate_v, step, push, decay, b_wide, begins, slot_edge),
        hbm=2,
        limit=4,
        micros=4,
    )
    from_x, from_y, send = lax.optimization_barrier((from_x, from_y, send))
    got = swapped(send, "seq", 1)
    half = row_count // 2
    far_high = swapped(from_x[half:], "req", 2)
    far_low = swapped(from_y[:half], "req", 1)
    at_x, at_y = call(
        peer_kernel, [tokens_out] * 2, [], (from_x, from_y, *weights), limit=6, micros=4.5
    )
    got = lax.optimization_barrier((got, at_x))[0]
    parts = [keep[k] + got[k] for k in range(chips)]
    far_low, far_high, parts = lax.optimization_barrier((far_low, far_high, parts))
    back_x, back_y = swapped(at_x, "req", 1), swapped(at_y, "req", 2)
    (at_far,) = call(far_kernel, [tokens_out], [], (far_low, far_high, *weights), limit=4, micros=3)
    back_far = swapped(at_far, "req", 3)
    parts = [parts[0]] + [shifted(parts[k], "seq", 2 * k) for k in range(1, chips)]
    new_state, new_edge = call(
        functools.partial(unpack_kernel, lags),
        [((STATE, inner), F32), ((lags, inner), BF16)],
        [pltpu.VMEM((edge_groups * STATE, LANE), F32)],
        tuple(parts),
        limit=4,
        last=True,
    )
    (block_rows,) = call(
        join_kernel, [((width, row_count), BF16)], [], (middle, own, back_x, back_y, back_far), limit=4,
        last=True,
    )
    return (block_rows.T[None], new_state[None, None], new_edge[None, None])


def solution(mesh):
    return jax.shard_map(
        shards,
        mesh=mesh,
        in_specs=(
            P("req", "seq", None),
            P("req", "seq", None),
            P(),
            P(),
            P(),
            P(),
            P(),
            P(),
            P(),
            P(),
            P(),
            P(None, "req"),
            P(None, "req"),
            P("req", None),
            P("req", "seq", None, None),
            P("req", "seq", None, None),
            P("req", None),
            P("req", None),
            P("req", None),
            P("req", None),
        ),
        out_specs=(P("req", "seq", None), P("req", "seq", None, None), P("req", "seq", None, None)),
        check_vma=False,
    )
```

```python
import functools

import jax
import jax.numpy as jnp
from jax import lax
from jax.experimental import pallas as pl
from jax.experimental.pallas import tpu as pltpu
from jax.sharding import PartitionSpec as P

STATE = 16
NORM_EPS = 1e-06
LANE = 128
FAR = 1e30
OFFER = 24
LOG2E = 1.4426950408889634
F32 = jnp.float32
BF16 = jnp.bfloat16


def request_marks(lens_ref, first_pos):
    marks = []
    begin = -first_pos
    for r in range(lens_ref.shape[1]):
        end = begin + lens_ref[0, r]
        marks.append((begin, end))
        begin = end
    return marks


def segment_of(index, marks):
    total = jnp.zeros(index.shape, jnp.int32)
    for begin, _ in marks:
        total = total + (index >= begin).astype(jnp.int32)
    return total


def segment_masks(row_count, marks):
    row = lax.broadcasted_iota(jnp.int32, (row_count, row_count), 0)
    col = lax.broadcasted_iota(jnp.int32, (row_count, row_count), 1)
    same = segment_of(row, marks) == segment_of(col, marks)
    return row, col, same


def three_parts(values):
    high = values.astype(BF16)
    rest = values - high.astype(F32)
    middle = rest.astype(BF16)
    low = (rest - middle.astype(F32)).astype(BF16)
    return jnp.concatenate([high, middle, low], axis=0)


def tripled(mask):
    one = mask.astype(F32).astype(BF16)
    return jnp.concatenate([one, one, one], axis=1)


def rate_block(rate_row):
    power = lax.broadcasted_iota(jnp.int32, (STATE, rate_row.shape[1]), 0) + 1
    return power.astype(F32) * rate_row


def row_of(vec_ref, tile):
    return vec_ref[pl.ds(tile, 1), :]


def wide_row(vec_ref, first, count):
    return jnp.concatenate([vec_ref[first + k : first + k + 1, :] for k in range(count)], axis=1)


def sums_of_eight(parts):
    sub = lax.broadcasted_iota(jnp.int32, parts[0].shape, 0)
    stride = 1
    while len(parts) > 1:
        first = jnp.bitwise_and(sub, stride) == 0
        parts = [
            jnp.where(first, a, b) + pltpu.roll(jnp.where(first, b, a), stride, 0)
            for a, b in zip(parts[0::2], parts[1::2])
        ]
        stride = 2 * stride
    return parts[0]


def softplus(v):
    return jnp.maximum(v, 0.0) + jnp.log1p(jnp.exp(-jnp.abs(v)))


def sum_layout(tiles):
    groups = -(-tiles // STATE)
    return groups, 2 * groups * LANE


def read_sum(ext_ref, tile, inner):
    groups, _ = sum_layout(inner // LANE)
    group, row = divmod(tile, STATE)
    high = inner + group * LANE
    low = high + groups * LANE
    return ext_ref[row : row + 1, high : high + LANE].astype(F32) + ext_ref[
        row : row + 1, low : low + LANE
    ].astype(F32)


def write_sums(ext_ref, sums, inner):
    groups, _ = sum_layout(inner // LANE)
    for group in range(groups):
        part = sums[group * STATE : (group + 1) * STATE, :]
        high = part.astype(BF16)
        low = (part - high.astype(F32)).astype(BF16)
        at = inner + group * LANE
        ext_ref[:, at : at + LANE] = high
        ext_ref[:, at + groups * LANE : at + (groups + 1) * LANE] = low


NT = (((1,), (1,)), ((), ()))
SIDE = 5 * LANE


def start_all(pairs, sems):
    copies = [pltpu.make_async_copy(src, dst, sems.at[k]) for k, (src, dst) in enumerate(pairs)]
    for copy in copies:
        copy.start()
    return copies


def lane_blocks(size, width):
    return [slice(at, min(at + width, size)) for at in range(0, size, width)]


def offer_kernel(state_hbm, edge_hbm, x_hbm, out_ref, state_s, edge_s, tail_s, sems):
    rows = tail_s.shape[0]
    last = x_hbm.at[pl.ds(x_hbm.shape[0] - rows, rows)]
    for copy in start_all([(state_hbm, state_s), (edge_hbm, edge_s), (last, tail_s)], sems):
        copy.wait()
    lags = edge_s.shape[0]
    tail = tail_s[...].astype(F32)[rows - lags :]
    spare = jnp.zeros((OFFER - STATE - 2 * lags, tail.shape[1]), F32)
    whole = jnp.concatenate([state_s[...], edge_s[...].astype(F32), tail, spare], axis=0)
    out_ref[...] = whole.astype(BF16)


def edges_kernel(*refs):
    for k, ref in enumerate(refs[:-1]):
        refs[-1][k] = ref[...].astype(F32)[STATE:].astype(BF16)


def conv_kernel(
    lens_hbm, x_hbm, taps_hbm, bias_hbm, dt_bias_hbm, rate_hbm, skip_hbm, x_proj_hbm, dt_proj_hbm,
    out_proj_hbm, hidden_hbm, conv_ref, rows_ref, taps_ref, dt_bias_ref, rate_ref, skip_ref,
    x_proj_ref, dt_proj_ref, weight_ref, hidden_ref, lens_ref, x_s, bias_s, sems,
):
    row_count, inner = x_s.shape
    lags = taps_ref.shape[0] - 1
    blocks = lane_blocks(inner, SIDE)
    pairs = [(lens_hbm, lens_ref), (taps_hbm, taps_ref), (bias_hbm, bias_s)]
    pairs += [(x_hbm.at[:, cols], x_s.at[:, cols]) for cols in blocks]
    pairs += [
        (dt_bias_hbm, dt_bias_ref), (rate_hbm, rate_ref), (skip_hbm, skip_ref),
        (x_proj_hbm, x_proj_ref), (dt_proj_hbm, dt_proj_ref), (out_proj_hbm, weight_ref),
        (hidden_hbm, hidden_ref),
    ]
    copies = start_all(pairs, sems)
    for copy in copies[:3]:
        copy.wait()
    marks = request_marks(lens_ref, lax.axis_index("seq") * row_count)
    row = lax.broadcasted_iota(jnp.int32, (row_count, 1), 0)
    near = []
    for lag in range(1, lags + 1):
        hit = jnp.zeros((row_count, 1), jnp.int32)
        for begin, _ in marks:
            hit = hit + jnp.logical_and(row >= begin, row < begin + lag).astype(jnp.int32)
        near.append((hit == 0).astype(F32))
    rows_ref[0:8, :] = jnp.zeros((8, inner), F32)
    for k, cols in enumerate(blocks):
        copies[3 + k].wait()
        here = x_s[:, cols].astype(F32)
        rows_ref[8 : 8 + row_count, cols] = here
        total = wide_row(bias_s, k * (SIDE // LANE), SIDE // LANE) + taps_ref[
            lags : lags + 1, cols
        ] * here
        for lag in range(1, lags + 1):
            back = rows_ref[8 - lag : 8 - lag + row_count, cols]
            total = total + taps_ref[lags - lag : lags - lag + 1, cols] * (near[lag - 1] * back)
        conv_ref[:, cols] = total
    for copy in copies[3 + len(blocks) :]:
        copy.wait()


def terms_kernel(lags, seed_count, *refs):
    scalar_hbm = refs[:4]
    (conv_ref, rows_ref, taps_ref, dt_bias_s, rate_s, skip_s, x_proj_ref, dt_proj_ref,
     edge_mine_ref, edge_other_ref) = refs[4:14]
    seed_refs = refs[14 : 14 + seed_count]
    refs = refs[14 + seed_count :]
    (step_ref, jump_ref, push_ref, base_ref, decay_ref, b_s, c_s, coef_ref, slot_edge_ref,
     bundle_ref, whole_ref) = refs[:11]
    scalars = refs[11:15]
    mixed_s, conv_s, edge_s, tail_s, sums_s, sems = refs[15:]
    ext_ref = bundle_ref.at[0]
    lens_ref, cont_ref, source_ref, owner_ref = scalars
    row_count, inner = conv_s.shape
    request_count = lens_ref.shape[1]
    chips = edge_mine_ref.shape[0]
    blocks = lane_blocks(inner, SIDE)
    side = SIDE // LANE
    copies = start_all(list(zip(scalar_hbm, scalars)), sems)
    me = lax.axis_index("seq")
    core = lax.rem(me, 2)
    row = lax.broadcasted_iota(jnp.int32, (row_count, 1), 0)
    for cols in blocks:
        conv_s[:, cols] = conv_ref[:, cols]
    for k, ref in enumerate(seed_refs):
        bundle_ref[1 + k, :, 0:inner] = ref[...].astype(F32)[:STATE].astype(BF16)
    tail_s[0:lags, :] = edge_other_ref[1 - core].astype(F32)[lags : 2 * lags, :]
    slot_edge_ref[...] = jnp.zeros(slot_edge_ref.shape, F32)
    for copy in copies:
        copy.wait()
    marks = request_marks(lens_ref, me * row_count)
    for p in range(lags):
        extra = jnp.zeros((1, inner), F32)
        for lag in range(p + 1, lags + 1):
            near = jnp.float32(1.0)
            for begin, _ in marks:
                near = jnp.where(jnp.logical_and(begin <= p, begin > p - lag), 0.0, near)
            extra = extra + taps_ref[lags - lag : lags - lag + 1, :] * (
                near * tail_s[lags + p - lag : lags + p - lag + 1, :]
            )
        conv_s[p : p + 1, :] = conv_s[p : p + 1, :] + extra
    for r in range(request_count):
        begin, end = marks[r]
        length = lens_ref[0, r]

        @pl.when(jnp.logical_and(begin > -lags, begin < row_count))
        def _(r=r, begin=begin, end=end, length=length):
            keep = cont_ref[0, r].astype(F32)
            source = source_ref[0, r]
            away = lax.rem(me // 2 - source // 2 + chips, chips)
            for ref, parity in ((edge_mine_ref, core), (edge_other_ref, 1 - core)):
                @pl.when(lax.rem(source, 2) == parity)
                def _(ref=ref):
                    edge_s[0:lags, :] = keep * ref[away].astype(F32)[0:lags, :]

            for p in range(lags):
                at = begin + p

                @pl.when(jnp.logical_and(jnp.logical_and(at >= 0, at < row_count), p < length))
                def _():
                    extra = jnp.zeros((1, inner), F32)
                    for lag in range(p + 1, lags + 1):
                        extra = extra + taps_ref[lags - lag : lags - lag + 1, :] * edge_s[
                            lags + p - lag : lags + p - lag + 1, :
                        ]
                    conv_s[pl.ds(at, 1), :] = conv_s[pl.ds(at, 1), :] + extra

        @pl.when(jnp.logical_and(end > 0, end <= row_count))
        def _(r=r, end=end, length=length):
            owner = owner_ref[0, r]
            for lag in range(lags):
                at = end - 1 - lag

                @pl.when(jnp.logical_and(length > lag, at >= 0))
                def _():
                    slot_edge_ref[owner, lags - 1 - lag : lags - lag, :] = rows_ref[
                        pl.ds(8 + at, 1), :
                    ]

                @pl.when(jnp.logical_and(length > lag, at < 0))
                def _():
                    slot_edge_ref[owner, lags - 1 - lag : lags - lag, :] = tail_s[
                        pl.ds(lags + at, 1), :
                    ]

                @pl.when(length <= lag)
                def _():
                    slot_edge_ref[owner, lags - 1 - lag : lags - lag, :] = edge_s[
                        pl.ds(lags + length - 1 - lag, 1), :
                    ]

    for k, cols in enumerate(blocks):
        v = conv_s[:, cols]
        mixed = (v / (1.0 + jnp.exp(-v))).astype(BF16)
        mixed_s[:, cols] = mixed
        base_ref[:, cols] = wide_row(skip_s, k * side, side) * mixed.astype(F32)
    projected = lax.dot_general(mixed_s[...], x_proj_ref[...], NT, preferred_element_type=F32)
    rank = dt_proj_ref.shape[0]
    dt_low = projected[:, :rank].astype(BF16)
    coef_ref[...] = projected[:, rank : rank + 2 * STATE]
    for s in range(STATE):
        at = rank + s
        b_s[s] = jnp.broadcast_to(projected[:, at : at + 1], (row_count, LANE))
        at = rank + STATE + s
        c_s[s] = jnp.broadcast_to(projected[:, at : at + 1], (row_count, LANE))
    last_begin = jnp.int32(0)
    jump = jnp.zeros((row_count, 1), F32)
    for begin, _ in marks:
        last_begin = jnp.where(
            jnp.logical_and(begin >= 0, begin < row_count), jnp.maximum(last_begin, begin), last_begin
        )
        jump = jump + (row == begin).astype(F32) * FAR
    in_last = (row >= last_begin).astype(F32)
    second = (1 - core) * row_count
    flags = [unbroken(marks, second, second + row_count)]
    stop = second + row_count
    for k in range(1, whole_ref.shape[0]):
        flags.append(unbroken(marks, stop - (row_count << k), stop))
    for k, flag in enumerate(flags):
        whole_ref[k : k + 1, :] = jnp.zeros((1, LANE), F32) + flag
    m_row, m_col, same = segment_masks(row_count, marks)
    later = tripled(jnp.logical_and(m_col > m_row, same))
    for k, cols in enumerate(blocks):
        step = softplus(
            jnp.dot(dt_low, dt_proj_ref[:, cols], preferred_element_type=F32)
            + wide_row(dt_bias_s, k * side, side)
        )
        step_ref[:, cols] = step
        jump_ref[:, cols] = step + jump
        push_ref[:, cols] = step * mixed_s[:, cols].astype(F32)
    for k, cols in enumerate(blocks):
        suffix = jnp.dot(later, three_parts(step_ref[:, cols]), preferred_element_type=F32)
        decay_ref[:, cols] = jnp.exp(-wide_row(rate_s, k * side, side) * suffix)

    def tile_step(i, carry):
        at = pl.multiple_of(i * LANE, LANE)
        cols = pl.ds(at, LANE)
        ext_ref[:, cols] = weighted_sum(
            push_ref[:, cols] * in_last, decay_ref[:, cols], b_s
        ).astype(BF16)
        sums_s[pl.ds(i, 1), :] = jnp.sum(step_ref[:, cols] * in_last, axis=0, keepdims=True)
        return carry

    sums_s[...] = jnp.zeros(sums_s.shape, F32)
    lax.fori_loop(0, inner // LANE, tile_step, 0, unroll=True)
    write_sums(ext_ref, sums_s[...], inner)


def weighted_sum(push, decay, b_ref):
    weight = push * decay
    totals = []
    for s in range(STATE):
        product = weight * b_ref[s]
        total = product[0:8, :]
        for k in range(8, push.shape[0], 8):
            total = total + product[k : k + 8, :]
        totals.append(total)
        if s + 1 < STATE:
            weight = weight * decay
    return jnp.concatenate(
        [sums_of_eight(totals[k : k + 8]) for k in range(0, STATE, 8)], axis=0
    )


def link_spans(earlier_of, later_of, whole, rate_ref, out_ref):
    tiles = rate_ref.shape[0]
    inner = tiles * LANE
    sums = []
    for i in range(tiles):
        cols = slice(i * LANE, (i + 1) * LANE)
        e0, s0 = earlier_of(cols, i, inner)
        e1, s1 = later_of(cols, i, inner)
        rate = rate_block(rate_ref[i : i + 1, :])
        out_ref[:, cols] = (e1 + whole * jnp.exp(-rate * s1) * e0).astype(BF16)
        sums.append(s1 + whole * s0)
    groups, _ = sum_layout(tiles)
    sums.append(jnp.zeros((groups * STATE - len(sums), LANE), F32))
    write_sums(out_ref, jnp.concatenate(sums, axis=0), inner)


def unbroken(marks, first, stop):
    whole = jnp.float32(1.0)
    for begin, _ in marks:
        whole = jnp.where(jnp.logical_and(begin >= first, begin < stop), 0.0, whole)
    return whole


def reader(ref):
    return lambda cols, i, inner: (ref[:, cols].astype(F32), read_sum(ref, i, inner))


def pair_kernel(rate_ref, whole_ref, mine_ref, other_ref, out_ref):
    core = lax.rem(lax.axis_index("seq"), 2)
    mine, other = reader(mine_ref.at[0]), reader(other_ref.at[0])

    def choose(number):
        def read(*where):
            return [jnp.where(core == number, a, b) for a, b in zip(mine(*where), other(*where))]

        return read

    link_spans(choose(0), choose(1), whole_ref[0:1, :], rate_ref, out_ref)


def span_kernel(power, rate_ref, whole_ref, mine_ref, before_ref, out_ref):
    whole = whole_ref[power : power + 1, :]
    link_spans(reader(before_ref), reader(mine_ref), whole, rate_ref, out_ref)


def spread_kernel(lens_hbm, rate_s, step_ref, coef_ref, b_ref, c_ref, q_ref, lens_ref, sems):
    row_count, inner = step_ref.shape
    copies = start_all([(lens_hbm, lens_ref)], sems)
    spare = jnp.zeros((row_count, LANE - 2 * STATE), F32)
    flipped = jnp.transpose(jnp.concatenate([coef_ref[...], spare], axis=1))
    for t in range(row_count):
        b_ref[t] = jnp.broadcast_to(flipped[0:STATE, t : t + 1], (STATE, LANE))
        c_ref[t] = jnp.broadcast_to(flipped[STATE : 2 * STATE, t : t + 1], (STATE, LANE))
    copies[0].wait()
    marks = request_marks(lens_ref, lax.axis_index("seq") * row_count)
    m_row, m_col, same = segment_masks(row_count, marks)
    earlier = tripled(jnp.logical_and(m_col <= m_row, same))
    side = SIDE // LANE
    for k, cols in enumerate(lane_blocks(inner, SIDE)):
        prefix = jnp.dot(earlier, three_parts(step_ref[:, cols]), preferred_element_type=F32)
        q_ref[:, cols] = jnp.exp(-wide_row(rate_s, k * side, side) * prefix)


def scan_kernel(first_side, sides, fetched, *refs):
    fetch_hbm = refs[:fetched]
    rate_s, jump_ref, push_ref, base_ref, b_s, c_s, y_ref = refs[fetched : fetched + 7]
    copies = start_all(list(zip(fetch_hbm, refs[fetched + 7 :])), refs[-1])
    row_count = jump_ref.shape[0]
    tiles = SIDE // LANE
    width = SIDE

    def chunk_step(i, carry):
        at = pl.multiple_of((first_side + i) * width, LANE)
        rates = [-LOG2E * rate_block(row_of(rate_s, (first_side + i) * tiles + k)) for k in range(tiles)]

        def row_step(j, held):
            first = pl.multiple_of(j * 8, 8)
            rows = pl.ds(first, 8)
            held = list(held)
            for k in range(tiles):
                lanes = pl.ds(pl.multiple_of(at + k * LANE, LANE), LANE)
                jumps, pushes = jump_ref.at[rows, lanes], push_ref.at[rows, lanes]
                h = held[k]
                outs = []
                for t in range(8):
                    decay = jnp.exp2(rates[k] * jumps[t : t + 1, :])
                    h = decay * h + b_s[first + t] * pushes[t : t + 1, :]
                    product = c_s[first + t] * h
                    outs.append(product[0:8] + product[8:16])
                held[k] = h
                out_lanes = pl.ds(pl.multiple_of(i * width + k * LANE, LANE), LANE)
                y_ref[rows, out_lanes] = base_ref[rows, lanes] + sums_of_eight(outs)
            return tuple(held)

        lax.fori_loop(
            0, row_count // 8, row_step, tuple(jnp.zeros((STATE, LANE), F32) for _ in range(tiles)),
            unroll=4,
        )
        return carry

    lax.fori_loop(0, sides, chunk_step, 0)
    for copy in copies:
        copy.wait()


def close_kernel(stage_count, *refs):
    scalar_hbm = refs[:3]
    rate_s, hidden_s = refs[3:5]
    stage_refs = refs[5 : 5 + stage_count]
    (mine_ref, other_ref, c_s, y_first_ref, y_rest_ref, q_ref, gain_ref, weight_ref) = refs[
        5 + stage_count : 13 + stage_count
    ]
    middle_ref, normed_ref, begins_ref = refs[13 + stage_count : 16 + stage_count]
    scalars = refs[16 + stage_count : 19 + stage_count]
    ssm_s, sems = refs[19 + stage_count :]
    pair_ref = other_ref.at[0]
    lens_ref, cont_ref, source_ref = scalars
    row_count, inner = q_ref.shape
    width = middle_ref.shape[0]
    chips = mine_ref.shape[0] - 1
    copies = start_all(list(zip(scalar_hbm, scalars)), sems)
    me = lax.axis_index("seq")
    core = lax.rem(me, 2)
    parting = y_first_ref.shape[1]
    ssm_s[:, 0:parting] = y_first_ref[...]
    ssm_s[:, parting:inner] = y_rest_ref[...]
    for copy in copies:
        copy.wait()
    marks = request_marks(lens_ref, me * row_count)
    tiles = 5
    side = tiles * LANE
    block = 32
    for r in range(lens_ref.shape[1]):
        begin, end = marks[r]
        low, high = jnp.maximum(begin, 0), jnp.minimum(end, row_count)

        @pl.when(high > low)
        def _(r=r, begin=begin, low=low, high=high):
            keep = cont_ref[0, r].astype(F32)
            source = source_ref[0, r]
            away = lax.rem(me // 2 - source // 2 + chips, chips)
            for ref, parity in ((mine_ref, core), (other_ref, 1 - core)):
                @pl.when(lax.rem(source, 2) == parity)
                def _(ref=ref):
                    begins_ref[r] = keep * ref[1 + away, :, 0:inner].astype(F32)

            for k in range(stage_count + 1):
                if k < stage_count:
                    away = 1 << (stage_count - 1 - k)
                    chip_first = me - core - 2 * away
                    ref = stage_refs[stage_count - 1 - k]
                    stage_end = -(core + 2 * (away - 1)) * row_count
                    valid = jnp.logical_and(chip_first >= 0, begin < stage_end)
                else:
                    ref = pair_ref
                    valid = jnp.logical_and(core == 1, begin < 0)

                @pl.when(valid)
                def _(ref=ref):
                    for i in range(inner // LANE):
                        cols = slice(i * LANE, (i + 1) * LANE)
                        decay = jnp.exp(-rate_block(rate_s[i : i + 1, :]) * read_sum(ref, i, inner))
                        begins_ref[r, :, cols] = (
                            ref[:, cols].astype(F32) + decay * begins_ref[r, :, cols]
                        )

            def block_step(j, carry):
                first = pl.multiple_of(j * block, block)
                rows = pl.ds(first, block)
                at_row = lax.broadcasted_iota(jnp.int32, (block, 1), 0) + first
                inside = jnp.logical_and(at_row >= low, at_row < high)

                def lane_step(i, inner_carry):
                    at = pl.multiple_of(i * side, LANE)
                    cols = pl.ds(at, side)
                    q = q_ref[rows, cols]
                    total = jnp.zeros((block, side), F32)
                    for s in range(STATE - 1, -1, -1):
                        c = c_s[s, rows, :]
                        c = jnp.concatenate([c] * tiles, axis=1)
                        total = (total + c * begins_ref[r, s : s + 1, cols]) * q
                    ssm_s[rows, cols] = ssm_s[rows, cols] + jnp.where(inside, total, 0.0)
                    return inner_carry

                lax.fori_loop(0, inner // side, lane_step, 0, unroll=True)
                return carry

            lax.fori_loop(low // block, (high + block - 1) // block, block_step, 0)

    total = hidden_s[...].astype(F32) + lax.dot_general(
        weight_ref[...], ssm_s[...].astype(BF16), NT, preferred_element_type=F32
    )
    middle_ref[...] = total
    total = total * lax.rsqrt(jnp.mean(total * total, axis=0, keepdims=True) + NORM_EPS)
    for cols in lane_blocks(width, LANE):
        normed_ref[:, cols] = (jnp.transpose(total[cols, :]) * gain_ref[:, cols]).astype(BF16)


def final_kernel(
    lens_hbm, owner_hbm, rate_s, step_ref, push_ref, decay_ref, b_ref, begins_ref,
    slot_edge_ref, keep_ref, send_ref, lens_ref, owner_ref, held_s, edge_s, sems,
):
    pairs = [(lens_hbm, lens_ref), (owner_hbm, owner_ref)]
    for copy in start_all(pairs, sems):
        copy.wait()
    row_count, inner = step_ref.shape
    block = 32
    me = lax.axis_index("seq")
    core = lax.rem(me, 2)
    chips = keep_ref.shape[0]
    marks = request_marks(lens_ref, me * row_count)
    lags = slot_edge_ref.shape[1]
    row = lax.broadcasted_iota(jnp.int32, (row_count, 1), 0)
    keep_ref[...] = jnp.zeros(keep_ref.shape, BF16)
    send_ref[...] = jnp.zeros(send_ref.shape, BF16)
    tiles = inner // LANE
    edge_groups = (keep_ref.shape[2] - inner) // LANE
    for r in range(lens_ref.shape[1]):
        begin, end = marks[r]

        @pl.when(jnp.logical_and(end > 0, end <= row_count))
        def _(r=r, begin=begin, end=end):
            owner = owner_ref[0, r]
            there = lax.rem(owner // 2 - me // 2 + chips, chips)
            mine = lax.rem(owner, 2) == core
            inside = jnp.logical_and(row >= begin, row < end).astype(F32)
            def put(cols, block):
                @pl.when(mine)
                def _():
                    keep_ref[there, :, cols] = block

                @pl.when(jnp.logical_not(mine))
                def _():
                    send_ref[there, :, cols] = block

            held_s[...] = jnp.zeros(held_s.shape, F32)

            def block_step(j, carry):
                first = pl.multiple_of(j * block, block)
                rows = pl.ds(first, block)
                at_row = lax.broadcasted_iota(jnp.int32, (block, 1), 0) + first
                here = jnp.logical_and(at_row >= begin, at_row < end).astype(F32)

                def add_tile(i, inner_carry):
                    cols = pl.ds(pl.multiple_of(i * LANE, LANE), LANE)
                    held_s[:, cols] = held_s[:, cols] + weighted_sum(
                        push_ref[rows, cols] * here, decay_ref[rows, cols], b_ref.at[:, rows, :]
                    )
                    return inner_carry

                lax.fori_loop(0, tiles, add_tile, 0, unroll=5)
                return carry

            lax.fori_loop(
                jnp.maximum(begin, 0) // block, (end + block - 1) // block, block_step, 0
            )

            def tile_step(i, carry):
                cols = pl.ds(pl.multiple_of(i * LANE, LANE), LANE)
                span = jnp.sum(step_ref[:, cols] * inside, axis=0, keepdims=True)
                carried = jnp.exp(-rate_block(row_of(rate_s, i)) * span) * begins_ref[r, :, cols]
                put(cols, (held_s[:, cols] + carried).astype(BF16))
                return carry

            lax.fori_loop(0, tiles, tile_step, 0)
            edge_s[...] = jnp.zeros(edge_s.shape, F32)
            for lag in range(lags):
                for i in range(tiles):
                    at = lag * tiles + i
                    edge_s[at : at + 1, :] = slot_edge_ref[
                        owner, lag : lag + 1, i * LANE : (i + 1) * LANE
                    ]
            for g in range(edge_groups):
                put(
                    slice(inner + g * LANE, inner + (g + 1) * LANE),
                    edge_s[g * STATE : (g + 1) * STATE, :].astype(BF16),
                )


def unpack_kernel(lags, *refs):
    got_refs, (state_ref, edge_ref, edge_s) = refs[:-3], refs[-3:]
    inner = state_ref.shape[1]
    tiles = inner // LANE

    def whole(cols):
        total = got_refs[0][:, cols].astype(F32)
        for ref in got_refs[1:]:
            total = total + ref[:, cols].astype(F32)
        return total

    state_ref[...] = whole(slice(0, inner))
    groups = (got_refs[0].shape[1] - inner) // LANE
    for g in range(groups):
        edge_s[g * STATE : (g + 1) * STATE, :] = whole(
            slice(inner + g * LANE, inner + (g + 1) * LANE)
        )
    for i in range(tiles):
        edge_ref[:, i * LANE : (i + 1) * LANE] = jnp.concatenate(
            [edge_s[lag * tiles + i : lag * tiles + i + 1, :] for lag in range(lags)], axis=0
        ).astype(BF16)


def feed_forward(tokens, gate_ref, up_ref, down_ref):
    gate = jnp.dot(tokens, gate_ref[...], preferred_element_type=F32)
    up = jnp.dot(tokens, up_ref[...], preferred_element_type=F32)
    hidden = (gate / (1.0 + jnp.exp(-gate)) * up).astype(BF16)
    return lax.dot_general(hidden, down_ref[...], NT, preferred_element_type=F32)


def own_kernel(token_ref, gate_ref, up_ref, down_ref, out_ref):
    out_ref[...] = feed_forward(token_ref[...], gate_ref, up_ref, down_ref)


def peer_kernel(*refs):
    count = (len(refs) - 3) // 2
    tokens = jnp.concatenate([ref[...] for ref in refs[:count]], axis=0)
    out = feed_forward(tokens, *refs[count : count + 3]).astype(BF16)
    part = out.shape[0] // count
    for k, ref in enumerate(refs[count + 3 :]):
        ref[...] = out[k * part : (k + 1) * part]


def far_kernel(low_ref, high_ref, gate_ref, up_ref, down_ref, out_ref):
    tokens = jnp.concatenate([low_ref[...], high_ref[...]], axis=0)
    out_ref[...] = feed_forward(tokens, gate_ref, up_ref, down_ref).astype(BF16)


def join_kernel(middle_ref, own_ref, *refs):
    whole = own_ref[...]
    for ref in refs[:-1]:
        whole = whole + ref[...].astype(F32)
    for cols in lane_blocks(whole.shape[1], LANE):
        refs[-1][cols, :] = (middle_ref[cols, :] + jnp.transpose(whole[:, cols])).astype(BF16)


def call(kernel, outs, scratch, operands, hbm=0, limit=16, micros=1.0, last=False):
    spaces = [pltpu.HBM if k < hbm else pltpu.VMEM for k in range(len(operands))]
    operands = [pltpu.with_memory_space_constraint(a, space) for a, space in zip(operands, spaces)]
    out_kind = jax.ShapeDtypeStruct if last else pltpu.VMEM
    return pl.pallas_call(
        kernel,
        out_shape=tuple(out_kind(shape, dtype) for shape, dtype in outs),
        in_specs=[pl.BlockSpec(memory_space=space) for space in spaces],
        out_specs=tuple(pl.BlockSpec(memory_space=pltpu.VMEM) for _ in outs),
        scratch_shapes=scratch,
        compiler_params=pltpu.CompilerParams(vmem_limit_bytes=limit * 1024 * 1024),
        cost_estimate=pl.CostEstimate(
            flops=int(micros * 1.15e9), bytes_accessed=int(micros * 3.6e6), transcendentals=0
        ),
    )(*operands)


def shifted(block, axis, distance):
    size = lax.axis_size(axis)
    return lax.ppermute(block, axis, [(i, (i + distance) % size) for i in range(size)])


def passed_up(block, axis, distance):
    size = lax.axis_size(axis)
    return lax.ppermute(block, axis, [(i, i + distance) for i in range(size - distance)])


def swapped(block, axis, mask):
    return lax.ppermute(block, axis, [(i, i ^ mask) for i in range(lax.axis_size(axis))])


def shards(
    hidden_in,
    mamba_in,
    conv_weight,
    conv_bias,
    x_proj,
    dt_proj,
    dt_bias,
    decay_rate,
    skip_gain,
    out_proj,
    norm_gain,
    mlp_gate,
    mlp_up,
    mlp_down,
    cache_state,
    cache_edge,
    req_lengths,
    cont_flag,
    cache_source,
    owner_slot,
):
    x = mamba_in[0]
    row_count, inner = x.shape
    width = hidden_in.shape[2]
    lags = cache_edge.shape[2]
    peers = lax.axis_size("seq")
    tiles = inner // LANE
    scalars = (req_lengths, cont_flag, cache_source, owner_slot)
    request_count = req_lengths.shape[1]
    chips = peers // 2
    dma = pltpu.SemaphoreType.DMA
    (offer,) = call(
        offer_kernel,
        [((OFFER, inner), BF16)],
        [
            pltpu.VMEM((STATE, inner), F32),
            pltpu.VMEM((lags, inner), BF16),
            pltpu.VMEM((STATE, inner), BF16),
            dma((3,)),
        ],
        (cache_state[0, 0], cache_edge[0, 0], x),
        hbm=3,
        limit=4,
    )
    offers = [offer] + [shifted(offer, "seq", 2 * k) for k in range(1, chips)]
    bias, dt_bias, rate, skip = [
        v.reshape(tiles, LANE) for v in (conv_bias, dt_bias, decay_rate, skip_gain)
    ]
    groups, extra = sum_layout(tiles)
    ext_shape = (STATE, inner + extra)
    scalar_s = pltpu.SMEM((1, request_count), jnp.int32)
    vec_s = pltpu.VMEM((tiles, LANE), F32)
    rank = x_proj.shape[1]
    full = ((row_count, inner), F32)
    bundle_shape = ((chips + 1, *ext_shape), BF16)
    wide = ((STATE, row_count, LANE), F32)
    blocks = len(lane_blocks(inner, SIDE))
    conv, rows, taps, dt_bias_v, rate_v, skip_v, x_proj_v, dt_proj_v, weight, hidden = call(
        conv_kernel,
        [
            full,
            ((8 + row_count, inner), F32),
            (conv_weight.shape, F32),
            ((tiles, LANE), F32),
            ((tiles, LANE), F32),
            ((tiles, LANE), F32),
            ((rank, inner), BF16),
            (dt_proj.shape, BF16),
            ((width, inner), BF16),
            ((width, row_count), BF16),
        ],
        [scalar_s, pltpu.VMEM((row_count, inner), BF16), vec_s, dma((10 + blocks,))],
        (
            req_lengths, x, conv_weight, bias, dt_bias, rate, skip, x_proj.T, dt_proj, out_proj.T,
            hidden_in[0].T,
        ),
        hbm=11,
        limit=8,
    )
    offers, conv = lax.optimization_barrier((offers, conv))
    (edge_mine,) = call(
        edges_kernel, [((chips, OFFER - STATE, inner), BF16)], [], tuple(offers), limit=4
    )
    edge_other = swapped(edge_mine, "seq", 1)
    step, jump, push, base, decay, b_wide, c_wide, coefs, slot_edge, bundle, whole = call(
        functools.partial(terms_kernel, lags, chips),
        [full, full, full, full, full, wide, wide, ((row_count, 2 * STATE), F32),
         ((peers, lags, inner), F32), bundle_shape, ((chips.bit_length(), LANE), F32)],
        [
            scalar_s, scalar_s, scalar_s, scalar_s,
            pltpu.VMEM((row_count, inner), BF16),
            pltpu.VMEM((row_count, inner), F32),
            pltpu.VMEM((8, inner), F32),
            pltpu.VMEM((8, inner), F32),
            pltpu.VMEM((groups * STATE, LANE), F32),
            dma((4,)),
        ],
        (
            *scalars, conv, rows, taps, dt_bias_v, rate_v, skip_v, x_proj_v, dt_proj_v,
            edge_mine, edge_other, *offers,
        ),
        hbm=4,
        limit=10,
    )
    other = swapped(bundle, "seq", 1)
    b_rows, c_rows, q = call(
        spread_kernel,
        [((row_count, STATE, LANE), F32), ((row_count, STATE, LANE), F32), full],
        [scalar_s, dma((1,))],
        (req_lengths, rate_v, step, coefs),
        hbm=1,
        limit=6,
    )
    other, b_rows, c_rows, q = lax.optimization_barrier((other, b_rows, c_rows, q))
    span_call = functools.partial(
        call, outs=[(ext_shape, BF16)], scratch=[], limit=4
    )
    (span,) = span_call(pair_kernel, operands=(rate_v, whole, bundle, other))

    def scan_call(first_side, sides, fetch):
        return call(
            functools.partial(scan_kernel, first_side, sides, len(fetch)),
            [((row_count, sides * SIDE), F32)] + [(w.shape, BF16) for w in fetch],
            [dma((len(fetch),))],
            (*fetch, rate_v, jump, push, base, b_rows, c_rows),
            hbm=len(fetch),
            limit=4,
        )

    all_sides = inner // SIDE
    early = (2 * all_sides) // 5
    y_first, gate = scan_call(0, early, (mlp_gate,))
    stages = [passed_up(span, "seq", 2)]
    first_stage, y_first, gate = lax.optimization_barrier((stages[0], y_first, gate))
    stages = [first_stage]
    reach = 2
    while reach < chips:
        (span,) = span_call(
            functools.partial(span_kernel, reach.bit_length() - 1),
            operands=(rate_v, whole, span, stages[-1]),
        )
        stages.append(passed_up(span, "seq", 2 * reach))
        reach = 2 * reach
    y_rest, up, down = scan_call(early, all_sides - early, (mlp_up, mlp_down.T))
    middle, normed, begins = call(
        functools.partial(close_kernel, len(stages)),
        [
            ((width, row_count), F32),
            ((row_count, width), BF16),
            ((request_count, STATE, inner), F32),
        ],
        [
            scalar_s, scalar_s, scalar_s,
            pltpu.VMEM((row_count, inner), F32),
            dma((3,)),
        ],
        (
            *scalars[:3], rate_v, hidden, *stages, bundle, other, c_wide, y_first, y_rest, q,
            norm_gain.reshape(1, width), weight,
        ),
        hbm=3,
        limit=14,
        micros=6,
    )
    weights = (gate, up, down)
    tokens_out = ((row_count, width), BF16)
    from_x, from_y = swapped(normed, "req", 1), swapped(normed, "req", 2)
    (own,) = call(
        own_kernel, [((row_count, width), F32)], [], (normed, *weights), limit=4, micros=3
    )
    edge_groups = -(-lags * tiles // STATE)
    packed = ((chips, STATE, inner + edge_groups * LANE), BF16)
    keep, send = call(
        final_kernel,
        [packed, packed],
        [
            scalar_s, scalar_s,
            pltpu.VMEM((STATE, inner), F32),
            pltpu.VMEM((edge_groups * STATE, LANE), F32),
            dma((2,)),
        ],
        (req_lengths, owner_slot, rate_v, step, push, decay, b_wide, begins, slot_edge),
        hbm=2,
        limit=4,
        micros=4,
    )
    from_x, from_y, send = lax.optimization_barrier((from_x, from_y, send))
    got = swapped(send, "seq", 1)
    half = row_count // 2
    far_high = swapped(from_x[half:], "req", 2)
    far_low = swapped(from_y[:half], "req", 1)
    at_x, at_y = call(
        peer_kernel, [tokens_out] * 2, [], (from_x, from_y, *weights), limit=6, micros=4.5
    )
    got = lax.optimization_barrier((got, at_x))[0]
    parts = [keep[k] + got[k] for k in range(chips)]
    far_low, far_high, parts = lax.optimization_barrier((far_low, far_high, parts))
    back_x, back_y = swapped(at_x, "req", 1), swapped(at_y, "req", 2)
    (at_far,) = call(far_kernel, [tokens_out], [], (far_low, far_high, *weights), limit=4, micros=3)
    back_far = swapped(at_far, "req", 3)
    parts = [parts[0]] + [shifted(parts[k], "seq", 2 * k) for k in range(1, chips)]
    new_state, new_edge = call(
        functools.partial(unpack_kernel, lags),
        [((STATE, inner), F32), ((lags, inner), BF16)],
        [pltpu.VMEM((edge_groups * STATE, LANE), F32)],
        tuple(parts),
        limit=4,
        last=True,
    )
    (block_rows,) = call(
        join_kernel, [((width, row_count), BF16)], [], (middle, own, back_x, back_y, back_far), limit=4,
        last=True,
    )
    return (block_rows.T[None], new_state[None, None], new_edge[None, None])


def solution(mesh):
    return jax.shard_map(
        shards,
        mesh=mesh,
        in_specs=(
            P("req", "seq", None),
            P("req", "seq", None),
            P(),
            P(),
            P(),
            P(),
            P(),
            P(),
            P(),
            P(),
            P(),
            P(None, "req"),
            P(None, "req"),
            P("req", None),
            P("req", "seq", None, None),
            P("req", "seq", None, None),
            P("req", None),
            P("req", None),
            P("req", None),
            P("req", None),
        ),
        out_specs=(P("req", "seq", None), P("req", "seq", None, None), P("req", "seq", None, None)),
        check_vma=False,
    )
```
